32 devices in a mesh: wide: 8 (over y, x, core), narrow: 4 (over z).
Axes of the slice: x: 2, y: 2, z: 4, core: 2. Of those that a mesh axis runs over, the one named last changes fastest.
Arguments:
- inputs: bfloat16 [32768, 768], P(('wide', 'narrow')), may hold values from -6 to 6
- segment_ids: int32 [32, 1024], P(('wide', 'narrow')), may hold values from 0 to 3, never falling along the last dimension, each value on 1 to 512 neighbouring positions
- routes: int32 [32768, 2], P(('wide', 'narrow')), may hold values from 0 to 3, all different within a row; in each aligned block of 1024 rows (0 to 1023, 1024 to 2047, ...) at most 768 rows name the same one
- attention_gain: bfloat16 [768], P(('wide', 'narrow')), may hold values from 0.25 to 1.75
- qkv_weight: bfloat16 [768, 2304], P(('wide', 'narrow')), may hold values from -0.3125 to 0.3125
- output_weight: bfloat16 [768, 768], P(('wide', 'narrow')), may hold values from -1.75 to 1.75
- mixture_gain: bfloat16 [768], P(('wide', 'narrow')), may hold values from 0.25 to 1.75
- router_train: bfloat16 [768, 2], P(('wide', 'narrow')), may hold values from -0.15625 to 0.15625
- router_frozen: bfloat16 [768, 2], P(('wide', 'narrow')), may hold values from -0.15625 to 0.15625
- expert_in: bfloat16 [768, 2, 3072], P(('wide', 'narrow')), may hold values from -0.21875 to 0.21875
- expert_out: bfloat16 [3072, 2, 768], P(('wide', 'narrow')), may hold values from -0.21875 to 0.21875
- frozen_in: bfloat16 [768, 2, 3072], P(('wide', 'narrow')), may hold values from -0.21875 to 0.21875
- frozen_out: bfloat16 [3072, 2, 768], P(('wide', 'narrow')), may hold values from -0.21875 to 0.21875
- cotangent: bfloat16 [32768, 768], P(('wide', 'narrow')), may hold values from -6 to 6
Outputs:
- block_output: bfloat16 [32768, 768], P(('wide', 'narrow'))
- input_grad: float32 [32768, 768], P(('wide', 'narrow'))
- attention_gain_grad: float32 [768], P(('wide', 'narrow'))
- qkv_grad: float32 [768, 2304], P(('wide', 'narrow'))
- output_weight_grad: float32 [768, 768], P(('wide', 'narrow'))
- mixture_gain_grad: float32 [768], P(('wide', 'narrow'))
- router_grad: float32 [768, 2], P(('wide', 'narrow'))
- expert_in_grad: float32 [768, 2, 3072], P(('wide', 'narrow'))
- expert_out_grad: float32 [3072, 2, 768], P(('wide', 'narrow'))
The draws below stay inside these ranges and needn't reach their ends.
Inputs may be any that keep to these rules, and one draw needn't show every extreme that they name: `routes`: each token names two different experts; among the 1024 tokens of one sequence no expert is named more than 768 times, a bound that some block reaches. `segment_ids`: within a sequence the document numbers never fall; each of the 4 documents has 1 to 512 tokens.
All inputs are finite; a program needn't handle non-finite values.
Results may differ from the reference program's by a relative error of at most 0.013.
The reference program's roundings to bfloat16 on the way count: a program that leaves them out, or rounds other values in their place, can miss the bound.
Values may be sent and summed in bfloat16 or wider, within the bound.
No kernel may reach another device: no remote copies, remote signals or barrier semaphores. Data moves between devices by JAX's collectives and lax.ppermute only.
A program may use at most 320 MiB of HBM per device.

```python
import math
import jax
import jax.numpy as jnp
import numpy as np
from jax import lax

D = 768
HEADS = 12
HEAD_DIM = 64
FF = 3072
E_TRAIN = 2
E_FROZEN = 2
DOCS = 4
TOK_DEV = 1024
EXPERTS = 4
CAP = 768
ROWS = 32
TOKENS = 32768


def raised(values, key, source, target, blocks, factor):
    def block_of(axis_at):
        return (jnp.arange(values.shape[axis_at]) // (values.shape[axis_at] // blocks)).reshape((-1,) + (1,) * (values.ndim - 1 - axis_at))

    one_side = jax.random.permutation(key, blocks)[block_of(target)]
    other_side = (block_of(target) + blocks // 2) % blocks
    return jnp.where((block_of(source) == one_side) | (block_of(source) == other_side), factor * values, values)


def steps_of(stream_key, dims, cuts, smallest, top_value):
    gain = 1.0
    for dim, blocks in cuts:
        heights = jax.random.uniform(jax.random.fold_in(jax.random.fold_in(stream_key, 6), dim), (blocks,), jnp.float32, smallest / len(cuts), top_value / len(cuts))
        gain = gain * jnp.repeat(jnp.exp(heights), dims[dim] // blocks).reshape((-1,) + (1,) * (len(dims) - 1 - dim))
    return gain


def profile(amount, total, limit, lean):
    weights = [(1 << 20) // math.isqrt(standing ** lean) + 1 for standing in range(2, amount + 1)]
    rest, holding = total - limit - (amount - 1), [1] * (amount - 1)
    while rest > 0:
        candidates = [i for i in range(amount - 1) if holding[i] < limit]
        mass, left = sum([weights[i] for i in candidates]), rest
        for i in candidates:
            more = min(limit - holding[i], max(1, left * weights[i] // mass), rest)
            holding[i] = holding[i] + more
            rest = rest - more
    return np.array([limit] + holding)


def uneven_parts(rng, amount, total, bound, slope):
    if amount == 2:
        one = jax.random.randint(rng, (), max(1, total - bound), min(bound, total - 1) + 1)
        return jnp.stack([one, total - one])
    sizes = jnp.asarray(profile(amount, total, bound, slope), jnp.int32)
    couples = (amount - 1) // 2
    source_of, taker = sizes[1:1 + 2 * couples:2], sizes[2:2 + 2 * couples:2]
    slack = jnp.minimum(source_of - 1, bound - taker)
    moved = jax.random.randint(jax.random.fold_in(rng, 1), (couples,), 0, 1 << 20) % (slack + 1)
    sizes = sizes.at[1:1 + 2 * couples:2].set(source_of - moved).at[2:2 + 2 * couples:2].set(taker + moved)
    return sizes[jax.random.permutation(jax.random.fold_in(rng, 2), amount)]


def routed_block(own_key, own, number, rows, number_of, top, limit, lean):
    order = jax.random.permutation(own_key, number_of)
    heavy_load, ordinary = portions_of(number_of, rows * top, limit, lean, True), portions_of(number_of, rows * top, limit, lean, False)
    places = jnp.arange(number_of)

    def named(lengths, offset_by):
        used = int((lengths > 0).sum())
        fixed = max(1, used // 4)
        passed = fixed + (places - fixed + offset_by * (used - fixed)) % max(1, number_of - fixed)
        return jnp.zeros((number_of,), jnp.int32).at[order[jnp.where(places < fixed, places, passed)]].set(jnp.asarray(lengths, jnp.int32))

    lengths = jnp.where(number % 4 == 0, named(heavy_load, number // 4), named(ordinary, number - number // 4 - 1))
    mixed = jax.random.permutation(jax.random.fold_in(own, 3), number_of)
    source_of, sink = mixed[0:number_of // 2 * 2:2], mixed[1:number_of // 2 * 2:2]
    room = jnp.minimum(lengths[source_of] - 1, limit - lengths[sink]) // 2
    room = jnp.where((source_of == order[0]) | (sink == order[0]) | (lengths[sink] == 0), 0, jnp.maximum(room, 0))
    passed = jax.random.randint(jax.random.fold_in(own, 4), (number_of // 2,), 0, 1 << 20) % (room + 1)
    lengths = lengths.at[source_of].add(-passed).at[sink].add(passed)
    members = jnp.searchsorted(jnp.cumsum(lengths), jnp.arange(rows * top), side="right").astype(jnp.int32)
    table = members.reshape(top, rows).T
    table = table[jax.random.permutation(jax.random.fold_in(own, 1), rows)]
    offset_by = jax.random.randint(jax.random.fold_in(own, 2), (rows, 1), 0, top)
    return jnp.take_along_axis(table, (jnp.arange(top)[None, :] + offset_by) % top, axis=1)


def portions_of(number_of, total, reach, slope, full):
    loads = [(1 << 20) // math.isqrt(rank ** slope) + 1 for rank in range(1, number_of + 1)]
    largest = reach if full else min(reach, max(-(-total // number_of), total * loads[0] // sum(loads)))
    least = 1 if total - largest >= number_of - 1 else 0
    holding, rest = [largest] + [least] * (number_of - 1), total - largest - least * (number_of - 1)
    while rest > 0:
        free = [i for i in range(1, number_of) if holding[i] < largest] or [i for i in range(1, number_of) if holding[i] < reach]
        pool, budget = sum([loads[i] for i in free]), rest
        for i in free:
            more = min(reach - holding[i], max(1, budget * loads[i] // pool), rest)
            holding[i] = holding[i] + more
            rest = rest - more
    return np.array(holding)


def centred(key, shape, scale, limit, cuts=(), held_as=jnp.bfloat16):
    array = jax.random.normal(key, shape, jnp.float32) * scale
    if len(cuts) > 0:
        array = steps_of(key, shape, cuts, -0.22, 0.18) * array
    return jnp.clip(array, min=-limit, max=limit).astype(held_as)


def bell_draw_with(stream_key, shape, scale, reach, cuts, heavy, kind=jnp.bfloat16):
    array = scale * jax.random.normal(stream_key, shape, jnp.float32)
    if cuts:
        array = array * steps_of(stream_key, shape, cuts, -0.22, 0.18)
    return jnp.clip(raised(array, jax.random.fold_in(stream_key, 3), *heavy), -reach, reach).astype(kind)


def setup_inputs(seed: int = 0) -> dict:
    arg_keys = jax.random.split(jax.random.key(seed), 15)
    inputs = centred(arg_keys[0], (TOKENS, D), 1.0, 6.0, ((0, 32),))
    segment_ids = jax.vmap(lambda own: jnp.searchsorted(jnp.cumsum(uneven_parts(own, DOCS, TOK_DEV, TOK_DEV // 2, 2)), jnp.arange(TOK_DEV), side="right"))(jax.random.split(arg_keys[1], ROWS)).reshape((ROWS, TOK_DEV)).astype(jnp.int32)
    routes_keys = jax.random.split(jax.random.fold_in(arg_keys[2], 1), TOKENS // TOK_DEV)
    routes_turns = jax.random.permutation(jax.random.fold_in(arg_keys[2], 3), TOKENS // TOK_DEV)
    routes = jax.vmap(lambda own, number: routed_block(jax.random.fold_in(arg_keys[2], 2), own, number, TOK_DEV, EXPERTS, 2, CAP, 1))(routes_keys, routes_turns).reshape((TOKENS, 2))
    attention_gain = jnp.clip(1.0 + 0.15 * jax.random.normal(arg_keys[3], (D,), jnp.float32), 0.25, 1.75).astype(jnp.bfloat16)
    qkv_weight = centred(arg_keys[4], (D, 3 * D), (D // 2) ** -0.5, 0.3125, ((0, 32),))
    output_weight = centred(arg_keys[5], (D, D), (D // 64) ** -0.5, 1.75, ((0, 32),))
    mixture_gain = jnp.clip(1.0 + 0.15 * jax.random.normal(arg_keys[6], (D,), jnp.float32), 0.25, 1.75).astype(jnp.bfloat16)
    router_train = centred(arg_keys[7], (D, E_TRAIN), (2 * D) ** -0.5, 0.15625, ((0, 32),))
    router_frozen = centred(arg_keys[8], (D, E_FROZEN), (2 * D) ** -0.5, 0.15625, ((0, 32),))
    expert_in = centred(arg_keys[9], (D, E_TRAIN, FF), D ** -0.5, 0.21875, ((0, 32),))
    expert_out = centred(arg_keys[10], (FF, E_TRAIN, D), (FF // 4) ** -0.5, 0.21875, ((0, 32),))
    frozen_in = centred(arg_keys[11], (D, E_FROZEN, FF), D ** -0.5, 0.21875, ((0, 32),))
    frozen_out = centred(arg_keys[12], (FF, E_FROZEN, D), (FF // 4) ** -0.5, 0.21875, ((0, 32),))
    cotangent = bell_draw_with(arg_keys[13], (TOKENS, D), 1.0, 6.0, ((0, 32),), (0, 1, 32, 2.75))
    return {"inputs": inputs, "segment_ids": segment_ids, "routes": routes, "attention_gain": attention_gain, "qkv_weight": qkv_weight, "output_weight": output_weight, "mixture_gain": mixture_gain, "router_train": router_train, "router_frozen": router_frozen, "expert_in": expert_in, "expert_out": expert_out, "frozen_in": frozen_in, "frozen_out": frozen_out, "cotangent": cotangent}


highest = lax.Precision.HIGHEST
norm_eps = 1e-05

@jax.custom_vjp
def low(v):
    return lax.optimization_barrier(v.astype(jnp.bfloat16)).astype(jnp.float32)

@jax.custom_vjp
def low_back(v):
    return v

def low_keep(v):
    return (low(v), None)

def low_pass(kept, grad):
    return (grad,)

def back_keep(v):
    return (v, None)

def back_low(kept, grad):
    return (low(grad),)
low.defvjp(low_keep, low_pass)
low_back.defvjp(back_keep, back_low)

def layer_norm(values, norm_gain):
    center = values - lax.optimization_barrier(jnp.mean(values, axis=-1, keepdims=True))
    spread = lax.optimization_barrier(jnp.mean(center * center, axis=-1, keepdims=True))
    return norm_gain * center * lax.rsqrt(spread + norm_eps)

def attend(queries, key_rows, value_rows, doc_ids):
    length = queries.shape[0]
    block_rows = min(512, length)
    positions = jnp.arange(length, dtype=jnp.int32)

    def one_block(block_index):
        offset = (block_index * block_rows).astype(jnp.int32)
        query_block = lax.dynamic_slice_in_dim(queries, offset, block_rows, 0)
        row_pos = lax.dynamic_slice_in_dim(positions, offset, block_rows, 0)
        row_doc = lax.dynamic_slice_in_dim(doc_ids, offset, block_rows, 0)
        scores = jnp.einsum('qhd,khd->hqk', query_block, key_rows, precision=highest)
        scores = low_back(scores * 0.125)
        allowed = (row_pos[:, None] >= positions[None, :]) & (row_doc[:, None] == doc_ids[None, :])
        scores = jnp.where(allowed[None], scores, -1e+30)
        probs = jax.nn.softmax(scores, axis=-1)
        return jnp.einsum('hqk,khd->qhd', low(probs), value_rows, precision=highest)
    blocks = lax.map(jax.checkpoint(one_block), jnp.arange(length // block_rows, dtype=jnp.int32))
    return blocks.reshape(length, queries.shape[1] * queries.shape[2])

def forward_rows(block_in, block_docs, block_routes, trainable, frozen):
    attention_gain, qkv_weight, output_weight, mixture_gain, router_train, expert_in, expert_out = trainable
    router_frozen, frozen_in, frozen_out = frozen
    group, length, model_width = block_in.shape
    normed_one = low(layer_norm(block_in, attention_gain))
    projected = low(low_back(jnp.einsum('rld,de->rle', normed_one, qkv_weight, precision=highest)))
    shaped = projected.reshape(group, length, 3, HEADS, HEAD_DIM)
    attended = jax.vmap(attend)(shaped[:, :, 0], shaped[:, :, 1], shaped[:, :, 2], block_docs)
    attended = low(low_back(attended))
    hidden_one = block_in + low_back(jnp.einsum('rld,de->rle', attended, output_weight, precision=highest))
    normed_two = low(layer_norm(hidden_one, mixture_gain))
    router_all = jnp.concatenate([router_train, router_frozen], axis=1)
    logits = jnp.einsum('rld,de->rle', normed_two, router_all, precision=highest)
    picked = (block_routes[..., None] == jnp.arange(EXPERTS, dtype=jnp.int32)).astype(jnp.float32)
    chosen = lax.optimization_barrier(jnp.sum(logits[:, :, None, :] * picked, axis=-1))
    gate_weights = jax.nn.softmax(chosen, axis=-1)
    per_expert = lax.optimization_barrier(jnp.sum(gate_weights[..., None] * picked, axis=2))
    weights_in = jnp.concatenate([expert_in, frozen_in], axis=1)
    weights_out = jnp.concatenate([expert_out, frozen_out], axis=1)
    mixture = jnp.zeros_like(hidden_one)
    for expert in range(EXPERTS):
        pre_act = low_back(jnp.einsum('rld,df->rlf', normed_two, weights_in[:, expert], precision=highest))
        activated = low(jax.nn.gelu(pre_act))
        result = low_back(jnp.einsum('rlf,fd->rld', activated, weights_out[:, expert], precision=highest))
        mixture = mixture + per_expert[..., expert:expert + 1] * result
    return hidden_one + mixture

def reference(inputs, segment_ids, routes, attention_gain, qkv_weight, output_weight, mixture_gain, router_train, router_frozen, expert_in, expert_out, frozen_in, frozen_out, cotangent):
    group = min(ROWS, max(1, 4096 // TOK_DEV))
    turns = ROWS // group
    inputs_f = inputs.astype(jnp.float32).reshape(turns, group, TOK_DEV, D)
    doc_rows = segment_ids.astype(jnp.int32).reshape(turns, group, TOK_DEV)
    route_rows = routes.astype(jnp.int32).reshape(turns, group, TOK_DEV, 2)
    frozen = (router_frozen.astype(jnp.float32), frozen_in.astype(jnp.float32), frozen_out.astype(jnp.float32))
    trainable = (attention_gain.astype(jnp.float32), qkv_weight.astype(jnp.float32), output_weight.astype(jnp.float32), mixture_gain.astype(jnp.float32), router_train.astype(jnp.float32), expert_in.astype(jnp.float32), expert_out.astype(jnp.float32))
    checked = jax.checkpoint(forward_rows)

    def whole(all_inputs, weights):

        def scan_step(carry, pieces):
            block_in, block_docs, block_routes = pieces
            return (carry, checked(block_in, block_docs, block_routes, weights, frozen))
        _, outputs = lax.scan(scan_step, jnp.zeros((), jnp.float32), (all_inputs, doc_rows, route_rows))
        return outputs
    outputs, pullback = jax.vjp(whole, inputs_f, trainable)
    grad_inputs, grads = pullback(cotangent.astype(jnp.float32).reshape(outputs.shape))
    return (outputs.reshape(TOKENS, D).astype(jnp.bfloat16), grad_inputs.reshape(TOKENS, D), grads[0], grads[1], grads[2], grads[3], grads[4], grads[5], grads[6])
```

```python
import functools

import jax
import jax.numpy as jnp
from jax import lax
from jax.experimental import pallas as pl
from jax.experimental.pallas import tpu as pltpu
from jax.sharding import Mesh, PartitionSpec as P

HEAD_DIM = 64
PAIR = 2 * HEAD_DIM
CAP = 768
MAX_DOC = 512
BLOCK = 256
WINDOW = BLOCK + 128
ROW_TILE = 256
LANES = 128
EPS = 1e-05
bf16, f32, i32 = jnp.bfloat16, jnp.float32, jnp.int32


def dot_nn(a, b):
    return lax.dot_general(a, b, (((1,), (0,)), ((), ())), preferred_element_type=f32)


def dot_nt(a, b):
    return lax.dot_general(a, b, (((1,), (1,)), ((), ())), preferred_element_type=f32)


def dot_tn(a, b):
    return lax.dot_general(a, b, (((0,), (0,)), ((), ())), preferred_element_type=f32)


def iota(shape, dim):
    return lax.broadcasted_iota(i32, shape, dim)


def flag(mask, dtype=bf16):
    return jnp.where(mask, 1.0, 0.0).astype(dtype)


def normalized(values):
    center = values - jnp.mean(values, axis=-1, keepdims=True)
    spread = jnp.mean(center * center, axis=-1, keepdims=True)
    inverse = lax.rsqrt(spread + EPS)
    return center * inverse, inverse


def norm_back(xhat, inverse, gain, grad):
    scaled = grad * gain
    return inverse * (
        scaled
        - jnp.mean(scaled, axis=-1, keepdims=True)
        - xhat * jnp.mean(scaled * xhat, axis=-1, keepdims=True)
    )


def params(limit_mib, **kw):
    return pltpu.CompilerParams(vmem_limit_bytes=limit_mib << 20, **kw)


def whole(shape):
    return pl.BlockSpec(shape, lambda *_: (0,) * len(shape))


def call(kernel, name, grid, ins, in_specs, outs, out_specs, scratch=(), limit=48, flops=0):
    size = sum(a.size * a.dtype.itemsize for a in ins) + sum(
        o.size * o.dtype.itemsize for o in outs
    )
    return pl.pallas_call(
        kernel,
        name=name,
        grid=grid,
        in_specs=in_specs,
        out_specs=out_specs,
        out_shape=outs,
        scratch_shapes=list(scratch),
        compiler_params=params(limit),
        cost_estimate=pl.CostEstimate(flops=flops, bytes_accessed=size, transcendentals=0),
    )(*ins)


def shape_of(shape, dtype):
    return jax.ShapeDtypeStruct(shape, dtype)


def gathered_specs(pieces, columns, index):
    return [pl.BlockSpec((p.shape[0], columns), lambda *i: (0, index(*i))) for p in pieces]


def put_together(rows_ref, piece_refs, whole_ref):
    for number, piece in enumerate(piece_refs):
        height = piece.shape[0]
        start = pl.multiple_of(rows_ref[number], 16 if height % 16 == 0 else 8)
        whole_ref[pl.ds(start, height), :] = piece[...]


def lay_out(order_ref, staged_ref, own_ref, other_ref):
    parts = order_ref.shape[0] // 2
    height = own_ref.shape[0] // parts
    for half, ref in enumerate((own_ref, other_ref)):
        for part in range(parts):
            start = order_ref[half * parts + part]
            start = pl.multiple_of(start, 16 if height % 16 == 0 else 8)
            ref[part * height : (part + 1) * height, :] = staged_ref[pl.ds(start, height), :]


SMEM = pl.BlockSpec(memory_space=pltpu.SMEM)


def route_kernel(routes_ref, routes_t_ref, place_ref, place_t_ref):
    length = routes_ref.shape[0]
    lane = iota((length, LANES), 1)
    mask = (lane == routes_ref[:, 0:1]) | (lane == routes_ref[:, 1:2])
    before = flag(iota((length, length), 1) < iota((length, length), 0))
    place_ref[...] = jnp.where(mask, dot_nn(before, flag(mask)), -1.0).astype(i32)
    sub = iota((8, length), 0)
    mask_t = (sub == routes_t_ref[0:1, :]) | (sub == routes_t_ref[1:2, :])
    before_t = flag(iota((length, length), 0) < iota((length, length), 1))
    place_t_ref[...] = jnp.where(mask_t, dot_nn(flag(mask_t), before_t), -1.0).astype(i32)


def route_places(routes):
    length = routes.shape[0]
    outs = [shape_of((length, LANES), i32), shape_of((8, length), i32)]
    return call(
        route_kernel,
        "places",
        (),
        [routes, routes.T],
        [whole((length, 2)), whole((2, length))],
        outs,
        [whole(o.shape) for o in outs],
    )


def gains_of(small_ref):
    return small_ref[...].astype(f32).T


def project_kernel(count, rows_ref, inputs_ref, *rest):
    pieces, (qkv_ref, dense_ref, gains_ref) = rest[:count], rest[count:]
    width = inputs_ref.shape[1]

    @pl.when(pl.program_id(0) == 0)
    def _():
        put_together(rows_ref, pieces, dense_ref)
        gains_ref[...] = dense_ref[:, 4 * width :].astype(f32).T

    xhat, _ = normalized(inputs_ref[...].astype(f32))
    normed = (gains_ref[0:1, :] * xhat).astype(bf16)
    qkv_ref[...] = dot_nn(normed, dense_ref[:, : 3 * width]).astype(bf16)


def project(rows, inputs, pieces):
    length, width = inputs.shape
    columns = pieces[0].shape[1]
    return call(
        functools.partial(project_kernel, len(pieces)),
        "project",
        (length // BLOCK,),
        [rows, inputs] + pieces,
        [SMEM, pl.BlockSpec((BLOCK, width), lambda i: (i, 0))]
        + gathered_specs(pieces, columns, lambda i: 0),
        [shape_of((length, 3 * width), bf16), shape_of((width, columns), bf16)],
        [pl.BlockSpec((BLOCK, 3 * width), lambda i: (i, 0)), whole((width, columns))],
        [pltpu.VMEM((LANES, width), f32)],
        flops=2 * length * width * 3 * width,
    )


def span_of(block):
    reach = MAX_DOC // BLOCK
    start = max(0, block - reach) * BLOCK
    return start, (block + 1) * BLOCK - start


def attend_kernel(doc_ref, doc_t_ref, q_ref, k_ref, v_ref, out_ref, log_ref, bias_ref):
    length = q_ref.shape[0]
    blocks = length // BLOCK

    @pl.when(pl.program_id(0) == 0)
    def _():
        for block in range(blocks):
            start, size = span_of(block)
            rows = slice(block * BLOCK, (block + 1) * BLOCK)
            row = iota((BLOCK, size), 0) + block * BLOCK
            col = iota((BLOCK, size), 1) + start
            kept = (row >= col) & (doc_ref[rows, :] == doc_t_ref[:, start : start + size])
            bias_ref[rows, :size] = jnp.where(kept, 0.0, -1e30)

    first = iota((BLOCK, PAIR), 1) < HEAD_DIM
    for block in range(blocks):
        start, size = span_of(block)
        rows = slice(block * BLOCK, (block + 1) * BLOCK)
        query = q_ref[rows, :] * 0.125
        keys, values = k_ref[start : start + size, :], v_ref[start : start + size, :]
        bias = bias_ref[rows, :size]
        parts, logs = [], []
        for own in (first, ~first):
            scores = dot_nt(jnp.where(own, query, 0).astype(bf16), keys) + bias
            peak = jnp.max(scores, axis=-1, keepdims=True)
            raised = jnp.exp(scores - peak)
            total = jnp.sum(raised, axis=-1, keepdims=True)
            parts.append(dot_nn(raised.astype(bf16), values) * (1.0 / total))
            logs.append(peak + jnp.log(total))
        out_ref[rows, :] = jnp.where(first, parts[0], parts[1]).astype(bf16)
        turned = jnp.where(first, logs[0], logs[1]).T
        log_ref[0, 0:1, rows] = turned[0:1, :]
        log_ref[0, 1:2, rows] = turned[HEAD_DIM : HEAD_DIM + 1, :]


def attend(docs, qkv):
    length, width = qkv.shape[0], qkv.shape[1] // 3
    pairs = width // PAIR
    heads = [pl.BlockSpec((length, PAIR), lambda i, k=k: (0, k * pairs + i)) for k in range(3)]
    return call(
        attend_kernel,
        "attend",
        (pairs,),
        [docs.reshape(length, 1), docs.reshape(1, length), qkv, qkv, qkv],
        [whole((length, 1)), whole((1, length))] + heads,
        [shape_of((length, width), bf16), shape_of((pairs, 8, length), f32)],
        [
            pl.BlockSpec((length, PAIR), lambda i: (0, i)),
            pl.BlockSpec((1, 8, length), lambda i: (i, 0, 0)),
        ],
        [pltpu.VMEM((length, MAX_DOC + BLOCK), f32)],
        flops=4 * length * 768 * width,
    )


def attend_back_kernel(
    doc_ref, doc_t_ref, q_ref, k_ref, v_ref, grad_ref, log_ref, dq_ref, dk_ref, dv_ref,
    bias_ref, dk_sum, dv_sum,
):
    length = q_ref.shape[0]
    blocks = length // BLOCK

    @pl.when(pl.program_id(0) == 0)
    def _():
        for block in range(blocks):
            start, size = span_of(block)
            cols = slice(block * BLOCK, (block + 1) * BLOCK)
            row = iota((size, BLOCK), 0) + start
            col = iota((size, BLOCK), 1) + block * BLOCK
            kept = (col >= row) & (doc_ref[start : start + size, :] == doc_t_ref[:, cols])
            bias_ref[:size, cols] = jnp.where(kept, 0.0, -1e30)

    dk_sum[...] = jnp.zeros_like(dk_sum)
    dv_sum[...] = jnp.zeros_like(dv_sum)
    first = iota((BLOCK, PAIR), 1) < HEAD_DIM
    for block in range(blocks):
        start, size = span_of(block)
        rows, span = slice(block * BLOCK, (block + 1) * BLOCK), slice(start, start + size)
        query, grad = q_ref[rows, :] * 0.125, grad_ref[rows, :]
        keys, values = k_ref[span, :], v_ref[span, :]
        bias = bias_ref[:size, rows]
        parts, dk, dv = [], 0.0, 0.0
        for head, own in enumerate((first, ~first)):
            own_query = jnp.where(own, query, 0).astype(bf16)
            own_grad = jnp.where(own, grad, 0).astype(bf16)
            scores = dot_nt(keys, own_query) + bias
            probs = jnp.exp(scores - log_ref[0, head : head + 1, rows])
            dv = dv + dot_nn(probs.astype(bf16), own_grad)
            weighted = probs * dot_nt(values, own_grad)
            mean = jnp.sum(weighted, axis=0, keepdims=True)
            grad_scores = (weighted - probs * mean).astype(bf16)
            dk = dk + dot_nn(grad_scores, own_query)
            parts.append(dot_tn(grad_scores, keys) * 0.125)
        dq_ref[rows, :] = jnp.where(first, parts[0], parts[1]).astype(bf16)
        dk_sum[span, :] += dk
        dv_sum[span, :] += dv
    dk_ref[...] = dk_sum[...].astype(bf16)
    dv_ref[...] = dv_sum[...].astype(bf16)


def attend_back(docs, qkv, grad, logs):
    length, width = qkv.shape[0], qkv.shape[1] // 3
    pairs = width // PAIR
    heads = [pl.BlockSpec((length, PAIR), lambda i, k=k: (0, k * pairs + i)) for k in range(3)]
    one = pl.BlockSpec((length, PAIR), lambda i: (0, i))
    return call(
        attend_back_kernel,
        "attend_back",
        (pairs,),
        [docs.reshape(length, 1), docs.reshape(1, length), qkv, qkv, qkv, grad, logs],
        [whole((length, 1)), whole((1, length))]
        + heads
        + [one, pl.BlockSpec((1, 8, length), lambda i: (i, 0, 0))],
        [shape_of((length, width), bf16)] * 3,
        [one] * 3,
        [
            pltpu.VMEM((MAX_DOC + BLOCK, length), f32),
            pltpu.VMEM((length, PAIR), f32),
            pltpu.VMEM((length, PAIR), f32),
        ],
        flops=10 * length * 768 * width,
    )


def middle_kernel(
    inputs_ref, attended_ref, place_ref, weight_ref, small_ref, hidden_ref, normed_ref, gate_ref,
    gains_ref,
):
    @pl.when(pl.program_id(0) == 0)
    def _():
        gains_ref[...] = gains_of(small_ref)

    hidden = inputs_ref[...].astype(f32) + dot_nn(attended_ref[...], weight_ref[...])
    hidden_ref[...] = hidden
    xhat, _ = normalized(hidden)
    normed = (gains_ref[1:2, :] * xhat).astype(bf16)
    normed_ref[...] = normed
    logits = dot_nn(normed, small_ref[...])
    mask = place_ref[...] >= 0
    logits = jnp.where(mask, pltpu.roll(logits, LANES - 2, 1), -1e30)
    peak = jnp.max(logits, axis=-1, keepdims=True)
    raised = jnp.where(mask, jnp.exp(logits - peak), 0.0)
    gate_ref[...] = raised / jnp.sum(raised, axis=-1, keepdims=True)


def middle(inputs, attended, place, dense):
    length, width = inputs.shape
    row = pl.BlockSpec((BLOCK, width), lambda i: (i, 0))
    thin = pl.BlockSpec((BLOCK, LANES), lambda i: (i, 0))
    return call(
        middle_kernel,
        "middle",
        (length // BLOCK,),
        [inputs, attended, place, dense, dense],
        [
            row,
            row,
            thin,
            pl.BlockSpec((width, width), lambda i: (0, 3)),
            pl.BlockSpec((width, LANES), lambda i: (0, 4 * width // LANES)),
        ],
        [
            shape_of((length, width), f32),
            shape_of((length, width), bf16),
            shape_of((length, LANES), f32),
        ],
        [row, row, thin],
        [pltpu.VMEM((LANES, width), f32)],
        flops=2 * length * width * width,
    )


def window_base(counts_ref, block, expert, experts):
    base = counts_ref[block * experts + expert]
    return pl.multiple_of(jnp.minimum(base // 128 * 128, CAP - WINDOW), 128)


def expert_kernel(
    expert, experts, train, count, rows_ref, order_ref, counts_ref, place_t_ref, gate_ref, normed_ref,
    cot_ref, *rest,
):
    in_pieces, out_pieces, rest = rest[:count], rest[count : 2 * count], rest[2 * count :]
    result_ref, back_ref, rest = rest[0], rest[1], rest[2:]
    if train:
        in_own, in_other, out_own, out_other = rest[:4]
        rest = rest[4:]
        turned_x, acts, grads, staged = rest[6:]
    rows_x, rows_g, sum_r, sum_b, in_ref, out_ref = rest[:6]
    length = normed_ref.shape[0]
    step = pl.program_id(0)
    load = counts_ref[length // BLOCK * experts + expert]

    @pl.when(step == 0)
    def _():
        rows_x[...] = jnp.zeros_like(rows_x)
        rows_g[...] = jnp.zeros_like(rows_g)
        sum_r[...] = jnp.zeros_like(sum_r)
        sum_b[...] = jnp.zeros_like(sum_b)
        for block in range(length // BLOCK):
            base = window_base(counts_ref, block, expert, experts)
            cols = slice(block * BLOCK, (block + 1) * BLOCK)
            pick = flag(iota((WINDOW, BLOCK), 0) + base == place_t_ref[expert : expert + 1, cols])
            window = pl.ds(base, WINDOW)
            rows_x[window, :] += dot_nn(pick, normed_ref[cols, :]).astype(bf16)
            scaled = gate_ref[cols, expert : expert + 1] * cot_ref[cols, :].astype(f32)
            rows_g[window, :] += dot_nn(pick, scaled.astype(bf16)).astype(bf16)
        if train:
            turned_x[...] = rows_x[...].T

    put_together(rows_ref, in_pieces, in_ref)
    put_together(rows_ref, out_pieces, out_ref)

    def tile(index, carry):
        rows = pl.ds(pl.multiple_of(index * ROW_TILE, ROW_TILE), ROW_TILE)
        pre = dot_nn(rows_x[rows, :], in_ref[...])
        grad_rows = rows_g[rows, :]
        square = pre * pre
        bend = jnp.tanh(0.7978845608028654 * pre * (1.0 + 0.044715 * square))
        half = 0.5 + 0.5 * bend
        slope = half + pre * (0.5 - 0.5 * bend * bend) * (
            0.7978845608028654 + 0.1070322243 * square
        )
        act = (pre * half).astype(bf16)
        grad = (dot_nt(grad_rows, out_ref[...]) * slope).astype(bf16)
        sum_r[rows, :] += dot_nn(act, out_ref[...])
        sum_b[rows, :] += dot_nt(grad, in_ref[...])
        if train:
            acts[rows, :] = act
            grads[rows, :] = grad
        return carry

    tiles = jnp.maximum((load + ROW_TILE - 1) // ROW_TILE, 1)
    lax.fori_loop(0, tiles, tile, 0)
    if train:
        for amount in range(1, CAP // ROW_TILE + 1):

            @pl.when(tiles == amount)
            def _(used=amount * ROW_TILE):
                staged[0] = dot_nn(turned_x[:, :used], grads[:used, :]).astype(bf16)
                staged[1] = dot_tn(acts[:used, :], rows_g[:used, :]).astype(bf16)

        lay_out(order_ref, staged.at[0], in_own, in_other)
        lay_out(order_ref, staged.at[1], out_own, out_other)

    @pl.when(step == pl.num_programs(0) - 1)
    def _():
        result_ref[...] = sum_r[...].astype(bf16)
        back_ref[...] = sum_b[...].astype(bf16)


def expert_pass(
    expert, experts, train, rows, order, counts, place_t, gates, normed, cot, pieces
):
    length, width = normed.shape
    hidden = pieces[0].shape[1] // 2
    steps = hidden // width
    half = width // 2
    slab = pl.BlockSpec((half, width), lambda i: (0, i))
    outs = [shape_of((CAP, width), bf16)] * 2
    out_specs = [whole((CAP, width))] * 2
    scratch = [
        pltpu.VMEM((CAP, width), bf16),
        pltpu.VMEM((CAP, width), bf16),
        pltpu.VMEM((CAP, width), f32),
        pltpu.VMEM((CAP, width), f32),
        pltpu.VMEM((width, width), bf16),
        pltpu.VMEM((width, width), bf16),
    ]
    if train:
        outs = outs + [shape_of((half, hidden), bf16)] * 4
        out_specs = out_specs + [slab] * 4
        scratch = scratch + [
            pltpu.VMEM((width, CAP), bf16),
            pltpu.VMEM((CAP, width), bf16),
            pltpu.VMEM((CAP, width), bf16),
            pltpu.VMEM((2, width, width), bf16),
        ]
    return call(
        functools.partial(expert_kernel, expert, experts, train, len(pieces)),
        "expert_%d" % expert,
        (steps,),
        [rows, order, counts, place_t, gates, normed, cot] + pieces + pieces,
        [
            SMEM,
            SMEM,
            SMEM,
            whole(place_t.shape),
            whole(gates.shape),
            whole(normed.shape),
            whole(cot.shape),
        ]
        + gathered_specs(pieces, width, lambda i: i)
        + gathered_specs(pieces, width, lambda i: i + steps),
        outs,
        out_specs,
        scratch,
        limit=56,
        flops=(12 if train else 8) * 600 * width * hidden,
    )


def combine_kernel(
    experts, order_ref, counts_ref, place_ref, gate_ref, hidden_ref, normed_ref, cot_ref, attended_ref,
    weight_ref, small_ref, *rest,
):
    result_refs, back_refs = rest[:experts], rest[experts : 2 * experts]
    (output_ref, grad_hidden_ref, grad_heads_ref, own_ref, other_ref,
     gains_ref, weight_sum, gain_sum, router_sum, staged) = rest[2 * experts :]
    step = pl.program_id(0)

    @pl.when(step == 0)
    def _():
        gains_ref[...] = gains_of(small_ref)
        weight_sum[...] = jnp.zeros_like(weight_sum)
        gain_sum[...] = jnp.zeros_like(gain_sum)
        router_sum[...] = jnp.zeros_like(router_sum)

    cot = cot_ref[...].astype(f32)
    hidden = hidden_ref[...]
    gates = gate_ref[...]
    lane = iota((BLOCK, LANES), 1)
    total, grad_normed = hidden, 0.0
    grad_gate = jnp.zeros((BLOCK, LANES), f32)
    for expert in range(experts):
        base = window_base(counts_ref, step, expert, experts)
        window = pl.ds(base, WINDOW)
        pick = flag(iota((BLOCK, WINDOW), 1) + base == place_ref[:, expert : expert + 1])
        picked = dot_nn(pick, result_refs[expert][window, :])
        total = total + gates[:, expert : expert + 1] * picked
        grad_gate = jnp.where(
            lane == expert, jnp.sum(cot * picked, axis=-1, keepdims=True), grad_gate
        )
        grad_normed = grad_normed + dot_nn(pick, back_refs[expert][window, :])
    output_ref[...] = total.astype(bf16)
    grad_logits = gates * (grad_gate - jnp.sum(gates * grad_gate, axis=-1, keepdims=True))
    high = grad_logits.astype(bf16)
    low = (grad_logits - high.astype(f32)).astype(bf16)
    gains = gains_ref[...]
    router = pltpu.roll(gains, LANES - 2, 0).astype(bf16)
    grad_normed = grad_normed + dot_nn(high, router) + dot_nn(low, router)
    normed = normed_ref[...]
    router_sum[...] += dot_tn(normed, high) + dot_tn(normed, low)
    xhat, inverse = normalized(hidden)
    gain_sum[...] += jnp.sum(grad_normed * xhat, axis=0, keepdims=True)
    grad_hidden = cot + norm_back(xhat, inverse, gains[1:2, :], grad_normed)
    grad_hidden_ref[...] = grad_hidden
    branch = grad_hidden.astype(bf16)
    grad_heads_ref[...] = dot_nt(branch, weight_ref[...]).astype(bf16)
    weight_sum[...] += dot_tn(attended_ref[...], branch)

    @pl.when(step == pl.num_programs(0) - 1)
    def _():
        width = weight_sum.shape[1]
        gain = jnp.broadcast_to(gain_sum[...], (LANES, width)).T
        small = jnp.where(iota((width, LANES), 1) == LANES - 1, gain, router_sum[...])
        staged[:, :width] = weight_sum[...].astype(bf16)
        staged[:, width:] = small.astype(bf16)
        lay_out(order_ref, staged, own_ref, other_ref)


def combine(
    experts, order, counts, place, gates, hidden, normed, cot, attended, dense, results, backs
):
    length, width = hidden.shape
    row = pl.BlockSpec((BLOCK, width), lambda i: (i, 0))
    thin = pl.BlockSpec((BLOCK, LANES), lambda i: (i, 0))
    term = (width // 2, width + LANES)
    return call(
        functools.partial(combine_kernel, experts),
        "combine",
        (length // BLOCK,),
        [order, counts, place, gates, hidden, normed, cot, attended, dense, dense]
        + results
        + backs,
        [
            SMEM,
            SMEM,
            thin,
            thin,
            row,
            row,
            row,
            row,
            pl.BlockSpec((width, width), lambda i: (0, 3)),
            pl.BlockSpec((width, LANES), lambda i: (0, 4 * width // LANES)),
        ]
        + [whole((CAP, width))] * (2 * experts),
        [
            shape_of((length, width), bf16),
            shape_of((length, width), f32),
            shape_of((length, width), bf16),
            shape_of(term, bf16),
            shape_of(term, bf16),
        ],
        [row, row, row, whole(term), whole(term)],
        [
            pltpu.VMEM((LANES, width), f32),
            pltpu.VMEM((width, width), f32),
            pltpu.VMEM((1, width), f32),
            pltpu.VMEM((width, LANES), f32),
            pltpu.VMEM((width, width + LANES), bf16),
        ],
        limit=56,
        flops=8 * length * width * width,
    )


def finish_kernel(
    order_ref, inputs_ref, dq_ref, dk_ref, dv_ref, grad_hidden_ref, weight_ref, small_ref, grad_ref,
    own_ref, other_ref, gains_ref, weight_sum, gain_sum, staged,
):
    step = pl.program_id(0)
    width = inputs_ref.shape[1]

    @pl.when(step == 0)
    def _():
        gains_ref[...] = gains_of(small_ref)
        weight_sum[...] = jnp.zeros_like(weight_sum)
        gain_sum[...] = jnp.zeros_like(gain_sum)

    gain = gains_ref[0:1, :]
    xhat, inverse = normalized(inputs_ref[...].astype(f32))
    normed = (gain * xhat).astype(bf16)
    grad = 0.0
    for k, ref in enumerate((dq_ref, dk_ref, dv_ref)):
        cols = slice(k * width, (k + 1) * width)
        grad = grad + dot_nt(ref[...], weight_ref[:, cols])
        weight_sum[:, cols] += dot_tn(normed, ref[...])
    gain_sum[...] += jnp.sum(grad * xhat, axis=0, keepdims=True)
    grad_ref[...] = grad_hidden_ref[...] + norm_back(xhat, inverse, gain, grad)

    @pl.when(step == pl.num_programs(0) - 1)
    def _():
        staged[:, : 3 * width] = weight_sum[...].astype(bf16)
        staged[:, 3 * width :] = jnp.broadcast_to(gain_sum[...], (LANES, width)).T.astype(bf16)
        lay_out(order_ref, staged, own_ref, other_ref)


def finish(order, inputs, dq, dk, dv, grad_hidden, dense):
    length, width = inputs.shape
    row = pl.BlockSpec((BLOCK, width), lambda i: (i, 0))
    term = (width // 2, 3 * width + LANES)
    return call(
        finish_kernel,
        "finish",
        (length // BLOCK,),
        [order, inputs, dq, dk, dv, grad_hidden, dense, dense],
        [
            SMEM,
            row,
            row,
            row,
            row,
            row,
            pl.BlockSpec((width, 3 * width), lambda i: (0, 0)),
            pl.BlockSpec((width, LANES), lambda i: (0, 4 * width // LANES)),
        ],
        [shape_of((length, width), f32), shape_of(term, bf16), shape_of(term, bf16)],
        [row, whole(term), whole(term)],
        [
            pltpu.VMEM((LANES, width), f32),
            pltpu.VMEM((width, 3 * width), f32),
            pltpu.VMEM((1, width), f32),
            pltpu.VMEM((width, 3 * width + LANES), bf16),
        ],
        limit=56,
        flops=4 * length * width * 3 * width,
    )


AXES = ("wide", "narrow")


class Links:
    def __init__(self, wide, narrow):
        self.wide, self.narrow = wide, narrow
        self.bits = [1 << b for b in range((wide // 2).bit_length() - 1)]
        index = lax.axis_index("wide")
        self.core, self.outer, self.place = index % 2, index // 2, lax.axis_index("narrow")

    def send(self, part, to):
        pairs = []
        for wide in range(self.wide):
            for narrow in range(self.narrow):
                outer, core, place = to(wide // 2, wide % 2, narrow)
                target = (outer * 2 + core) * self.narrow + place
                pairs.append((wide * self.narrow + narrow, target))
        return lax.ppermute(part, AXES, pairs)

    def flip(self, part, mask):
        return self.send(part, lambda o, c, z: (o ^ mask, c, z))

    def swap(self, part):
        return self.send(part, lambda o, c, z: (o, 1 - c, z))

    def shift(self, part, by):
        return self.send(part, lambda o, c, z: (o, c, (z + by) % self.narrow))


def after(values, *deps):
    flat, tree = jax.tree.flatten(values)
    more = jax.tree.leaves(deps)
    held = lax.optimization_barrier(tuple(flat) + tuple(more))
    return jax.tree.unflatten(tree, held[: len(flat)])


class Gather:
    def __init__(self, links, part):
        self.links, self.part = links, part

    def along(self):
        links, part = self.links, self.part
        self.got = [part] + [links.shift(part, -by) for by in range(1, links.narrow)]

    def first(self, *deps):
        links = self.links
        got, rows = self.got, self.part.shape[0]
        full = jnp.concatenate(got + got[:-1], axis=0)
        start = (links.narrow - links.place) % links.narrow * rows
        full = lax.dynamic_slice_in_dim(full, start, links.narrow * rows, 0)
        self.full = full = after(full, *deps) if deps else full
        low, high = links.bits[0], links.bits[1]
        self.low, self.high = links.flip(full, low), links.flip(full, high)
        self.full_over = links.swap(full)

    def second(self, *deps):
        links = self.links
        low, high = links.bits[0], links.bits[1]
        half = self.full.shape[0] // 2
        self.low, self.high = after((self.low, self.high), *deps)
        self.ends = [links.flip(self.low[:half], high), links.flip(self.high[half:], low)]
        self.over = [links.swap(self.low), links.swap(self.high)]

    def pieces(self):
        links = self.links
        low, high = links.bits[0], links.bits[1]
        own = [self.full, self.low, self.high] + self.ends
        over = [self.full_over] + self.over + [links.swap(e) for e in self.ends]
        for bit in links.bits[2:]:
            own = own + [links.flip(p, bit) for p in own]
            over = over + [links.flip(p, bit) for p in over]
        return own + over


def piece_rows(links, own_rows):
    height = links.narrow * own_rows
    low, high = links.bits[0], links.bits[1]
    marks = [(0, 0), (low, 0), (high, 0), (low | high, 0), (low | high, height // 2)]
    for bit in links.bits[2:]:
        marks = marks + [(mask | bit, extra) for mask, extra in marks]
    return jnp.stack(
        [
            ((links.outer ^ mask) * 2 + (links.core ^ over)) * height + extra
            for over in range(2)
            for mask, extra in marks
        ]
    ).astype(i32)


def part_rows(links, own_rows):
    height = links.narrow * own_rows
    return jnp.stack(
        [
            ((links.outer ^ mask) * 2 + (links.core ^ over)) * height
            for over in range(2)
            for mask in range(links.wide // 2)
        ]
    ).astype(i32)


def total(*terms):
    out = terms[0].astype(f32)
    for term in terms[1:]:
        out = out + term.astype(f32)
    return out


class Scatter:
    def __init__(self, links, own, other):
        self.links, self.own = links, own
        self.sent = links.swap(other)

    def first(self, *deps):
        links = self.links
        parts = links.wide // 2
        height = self.own.shape[0] // parts
        got = after(self.sent, *deps) if deps else self.sent
        blocks = [
            [a[m * height : (m + 1) * height] for a in (self.own, got)] for m in range(parts)
        ]
        for bit in links.bits[:1:-1]:
            sent = [links.flip(total(*blocks[m + bit]).astype(bf16), bit) for m in range(bit)]
            blocks = [blocks[m] + [sent[m]] for m in range(bit)]
        low, high = links.bits[0], links.bits[1]
        self.half = half = height // 2
        end = blocks[low | high]
        self.top = links.flip(total(*[b[:half] for b in end]).astype(bf16), low)
        self.bottom = links.flip(total(*[b[half:] for b in end]).astype(bf16), high)
        self.blocks = blocks

    def second(self, *deps):
        links, half, blocks = self.links, self.half, self.blocks
        low, high = links.bits[0], links.bits[1]
        top, bottom = after((self.top, self.bottom), *deps)
        to_high = [b[:half] for b in blocks[high]] + [top], [b[half:] for b in blocks[high]]
        to_low = [b[:half] for b in blocks[low]], [b[half:] for b in blocks[low]] + [bottom]
        to_high = jnp.concatenate([total(*t).astype(bf16) for t in to_high])
        to_low = jnp.concatenate([total(*t).astype(bf16) for t in to_low])
        self.kept = blocks[0] + [links.flip(to_low, low), links.flip(to_high, high)]

    def along(self, *deps):
        links = self.links
        kept = after(self.kept, *deps) if deps else self.kept
        rows = kept[0].shape[0] // links.narrow

        def share(by):
            start = (links.place + by) % links.narrow * rows
            return total(*[lax.dynamic_slice_in_dim(k, start, rows, 0) for k in kept])

        self.got = [share(0)] + [
            links.shift(share(by).astype(bf16), by) for by in range(1, links.narrow)
        ]

    def result(self):
        return total(*self.got)


def on_device(
    wide, narrow, inputs, segment_ids, routes, attention_gain, qkv_weight, output_weight,
    mixture_gain, router_train, router_frozen, expert_in, expert_out, frozen_in, frozen_out,
    cotangent,
):
    links = Links(wide, narrow)
    length, width = inputs.shape
    own_rows = qkv_weight.shape[0]
    train_count = expert_in.shape[1]
    experts = train_count + frozen_in.shape[1]
    groups = expert_in.shape[2] // width
    docs = segment_ids[0]
    small = jnp.concatenate(
        [attention_gain[:, None], mixture_gain[:, None], router_train, router_frozen], axis=1
    )
    small = jnp.pad(small, ((0, 0), (0, LANES - small.shape[1])))
    dense = Gather(links, jnp.concatenate([qkv_weight, output_weight, small], axis=1))
    rows, order = piece_rows(links, own_rows), part_rows(links, own_rows)

    weights = []
    for expert in range(experts):
        if expert < train_count:
            inner, outer = expert_in[:, expert], expert_out[:, expert]
        else:
            inner, outer = frozen_in[:, expert - train_count], frozen_out[:, expert - train_count]
        inner = inner.reshape(own_rows, width, groups).transpose(0, 2, 1).reshape(own_rows, -1)
        weights.append(
            Gather(links, jnp.concatenate([inner, outer.reshape(own_rows, -1)], axis=1))
        )

    chosen = (routes[:, :, None] == jnp.arange(experts, dtype=i32)).astype(i32)
    per_block = jnp.sum(chosen.reshape(length // BLOCK, 2 * BLOCK, experts), axis=1)
    counts = jnp.concatenate([jnp.zeros((1, experts), i32), jnp.cumsum(per_block, axis=0)])
    counts = counts.reshape(-1)
    place, place_t = route_places(routes)

    dense.along()
    chain = [dense] + weights
    for gather in weights:
        gather.along()
    dense.first()
    for before, gather in zip(chain, weights):
        gather.first(before.low, before.high)
        before.second()
    weights[-1].second()

    qkv, dense = project(rows, inputs, dense.pieces())
    attended, logs = attend(docs, qkv)
    hidden, normed, gates = middle(inputs, attended, place, dense)
    results, backs, terms = [], [], []
    for expert in range(experts):
        made = expert_pass(
            expert, experts, expert < train_count, rows, order, counts, place_t, gates, normed,
            cotangent, weights[expert].pieces(),
        )
        results.append(made[0])
        backs.append(made[1])
        if expert < train_count:
            terms.append(Scatter(links, made[2], made[3]))
            terms.append(Scatter(links, made[4], made[5]))
    for term in terms:
        term.first()
        term.second()
        term.along()
    block_output, grad_hidden, grad_heads, *made = combine(
        experts, order, counts, place, gates, hidden, normed, cotangent, attended, dense, results,
        backs,
    )
    out_term = Scatter(links, *made)
    out_term.first()
    out_term.second()
    out_term.along()
    dq, dk, dv = attend_back(docs, qkv, grad_heads, logs)
    input_grad, *made = finish(order, inputs, dq, dk, dv, grad_hidden, dense)
    qkv_term = Scatter(links, *made)
    qkv_term.first()
    qkv_term.second()
    qkv_term.along()
    terms = [t.result() for t in terms]
    out_term, qkv_term = out_term.result(), qkv_term.result()
    in_grad = jnp.stack(
        [
            t.reshape(own_rows, groups, width).transpose(0, 2, 1).reshape(own_rows, -1)
            for t in terms[::2]
        ],
        axis=1,
    )
    down_grad = jnp.stack([t.reshape(own_rows * groups, width) for t in terms[1::2]], axis=1)
    return (
        block_output,
        input_grad,
        qkv_term[:, 3 * width],
        qkv_term[:, : 3 * width],
        out_term[:, :width],
        out_term[:, width + LANES - 1],
        out_term[:, width : width + train_count],
        in_grad,
        down_grad,
    )


def solution(mesh):
    rows = P(AXES)
    return jax.shard_map(
        functools.partial(on_device, mesh.shape["wide"], mesh.shape["narrow"]),
        mesh=mesh,
        in_specs=(rows,) * 14,
        out_specs=(rows,) * 9,
        check_vma=False,
    )
```

```python
import functools

import jax
import jax.numpy as jnp
from jax import lax
from jax.experimental import pallas as pl
from jax.experimental.pallas import tpu as pltpu
from jax.sharding import Mesh, PartitionSpec as P

HEAD_DIM = 64
PAIR = 2 * HEAD_DIM
CAP = 768
MAX_DOC = 512
BLOCK = 256
WINDOW = BLOCK + 128
ROW_TILE = 256
LANES = 128
EPS = 1e-05
bf16, f32, i32 = jnp.bfloat16, jnp.float32, jnp.int32


def dot_nn(a, b):
    return lax.dot_general(a, b, (((1,), (0,)), ((), ())), preferred_element_type=f32)


def dot_nt(a, b):
    return lax.dot_general(a, b, (((1,), (1,)), ((), ())), preferred_element_type=f32)


def dot_tn(a, b):
    return lax.dot_general(a, b, (((0,), (0,)), ((), ())), preferred_element_type=f32)


def iota(shape, dim):
    return lax.broadcasted_iota(i32, shape, dim)


def flag(mask, dtype=bf16):
    return jnp.where(mask, 1.0, 0.0).astype(dtype)


def normalized(values):
    center = values - jnp.mean(values, axis=-1, keepdims=True)
    spread = jnp.mean(center * center, axis=-1, keepdims=True)
    inverse = lax.rsqrt(spread + EPS)
    return center * inverse, inverse


def norm_back(xhat, inverse, gain, grad):
    scaled = grad * gain
    return inverse * (
        scaled
        - jnp.mean(scaled, axis=-1, keepdims=True)
        - xhat * jnp.mean(scaled * xhat, axis=-1, keepdims=True)
    )


def params(limit_mib, **kw):
    return pltpu.CompilerParams(vmem_limit_bytes=limit_mib << 20, **kw)


def whole(shape):
    return pl.BlockSpec(shape, lambda *_: (0,) * len(shape))


def call(kernel, name, grid, ins, in_specs, outs, out_specs, scratch=(), limit=48, flops=0):
    size = sum(a.size * a.dtype.itemsize for a in ins) + sum(
        o.size * o.dtype.itemsize for o in outs
    )
    return pl.pallas_call(
        kernel,
        name=name,
        grid=grid,
        in_specs=in_specs,
        out_specs=out_specs,
        out_shape=outs,
        scratch_shapes=list(scratch),
        compiler_params=params(limit),
        cost_estimate=pl.CostEstimate(flops=flops, bytes_accessed=size, transcendentals=0),
    )(*ins)


def shape_of(shape, dtype):
    return jax.ShapeDtypeStruct(shape, dtype)


def gathered_specs(pieces, columns, index):
    return [
        pl.BlockSpec((height, columns), lambda *i, at=at: (at, index(*i)))
        for _, height, at in pieces
    ]


def put_together(rows_ref, piece_refs, whole_ref):
    for number, piece in enumerate(piece_refs):
        height = piece.shape[0]
        start = pl.multiple_of(rows_ref[number], 16 if height % 16 == 0 else 8)
        whole_ref[pl.ds(start, height), :] = piece[...]


def lay_out(order_ref, staged_ref, own_ref, other_ref):
    parts = order_ref.shape[0] // 2
    height = own_ref.shape[0] // parts
    for half, ref in enumerate((own_ref, other_ref)):
        for part in range(parts):
            start = order_ref[half * parts + part]
            start = pl.multiple_of(start, 16 if height % 16 == 0 else 8)
            ref[part * height : (part + 1) * height, :] = staged_ref[pl.ds(start, height), :]


SMEM = pl.BlockSpec(memory_space=pltpu.SMEM)


def route_kernel(routes_ref, routes_t_ref, place_ref, place_t_ref):
    length = routes_ref.shape[0]
    lane = iota((length, LANES), 1)
    mask = (lane == routes_ref[:, 0:1]) | (lane == routes_ref[:, 1:2])
    before = flag(iota((length, length), 1) < iota((length, length), 0))
    place_ref[...] = jnp.where(mask, dot_nn(before, flag(mask)), -1.0).astype(i32)
    sub = iota((8, length), 0)
    mask_t = (sub == routes_t_ref[0:1, :]) | (sub == routes_t_ref[1:2, :])
    before_t = flag(iota((length, length), 0) < iota((length, length), 1))
    place_t_ref[...] = jnp.where(mask_t, dot_nn(flag(mask_t), before_t), -1.0).astype(i32)


def route_places(routes):
    length = routes.shape[0]
    outs = [shape_of((length, LANES), i32), shape_of((8, length), i32)]
    return call(
        route_kernel,
        "places",
        (),
        [routes, routes.T],
        [whole((length, 2)), whole((2, length))],
        outs,
        [whole(o.shape) for o in outs],
    )


def gains_of(small_ref):
    return small_ref[...].astype(f32).T


def project_kernel(count, rows_ref, inputs_ref, *rest):
    pieces, (qkv_ref, dense_ref, rows_out_ref, gains_ref) = rest[:count], rest[count:]
    width = inputs_ref.shape[1]

    @pl.when(pl.program_id(0) == 0)
    def _():
        put_together(rows_ref, pieces, dense_ref)
        gains_ref[...] = dense_ref[:, 4 * width :].astype(f32).T
        rows_out_ref[...] = gains_ref[:16, :].astype(bf16)

    xhat, _ = normalized(inputs_ref[...].astype(f32))
    normed = (gains_ref[0:1, :] * xhat).astype(bf16)
    qkv_ref[...] = dot_nn(normed, dense_ref[:, : 3 * width]).astype(bf16)


def project(rows, inputs, pieces):
    length, width = inputs.shape
    columns = pieces[0][0].shape[1]
    return call(
        functools.partial(project_kernel, len(pieces)),
        "project",
        (length // BLOCK,),
        [rows, inputs] + [p[0] for p in pieces],
        [SMEM, pl.BlockSpec((BLOCK, width), lambda i: (i, 0))]
        + gathered_specs(pieces, columns, lambda i: 0),
        [
            shape_of((length, 3 * width), bf16),
            shape_of((width, columns), bf16),
            shape_of((16, width), bf16),
        ],
        [
            pl.BlockSpec((BLOCK, 3 * width), lambda i: (i, 0)),
            whole((width, columns)),
            whole((16, width)),
        ],
        [pltpu.VMEM((LANES, width), f32)],
        flops=2 * length * width * 3 * width,
    )


def span_of(block):
    reach = MAX_DOC // BLOCK
    start = max(0, block - reach) * BLOCK
    return start, (block + 1) * BLOCK - start


def attend_kernel(doc_ref, doc_t_ref, q_ref, k_ref, v_ref, out_ref, log_ref, bias_ref):
    length = q_ref.shape[0]
    blocks = length // BLOCK

    @pl.when(pl.program_id(0) == 0)
    def _():
        for block in range(blocks):
            start, size = span_of(block)
            rows = slice(block * BLOCK, (block + 1) * BLOCK)
            row = iota((BLOCK, size), 0) + block * BLOCK
            col = iota((BLOCK, size), 1) + start
            kept = (row >= col) & (doc_ref[rows, :] == doc_t_ref[:, start : start + size])
            bias_ref[rows, :size] = jnp.where(kept, 0.0, -1e30)

    first = iota((BLOCK, PAIR), 1) < HEAD_DIM
    for block in range(blocks):
        start, size = span_of(block)
        rows = slice(block * BLOCK, (block + 1) * BLOCK)
        query = q_ref[rows, :] * 0.125
        keys, values = k_ref[start : start + size, :], v_ref[start : start + size, :]
        bias = bias_ref[rows, :size]
        parts, logs = [], []
        for own in (first, ~first):
            scores = dot_nt(jnp.where(own, query, 0).astype(bf16), keys) + bias
            peak = jnp.max(scores, axis=-1, keepdims=True)
            raised = jnp.exp(scores - peak)
            total = jnp.sum(raised, axis=-1, keepdims=True)
            parts.append(dot_nn(raised.astype(bf16), values) * (1.0 / total))
            logs.append(peak + jnp.log(total))
        out_ref[rows, :] = jnp.where(first, parts[0], parts[1]).astype(bf16)
        turned = jnp.where(first, logs[0], logs[1]).T
        log_ref[0, 0:1, rows] = turned[0:1, :]
        log_ref[0, 1:2, rows] = turned[HEAD_DIM : HEAD_DIM + 1, :]


def attend(docs, qkv):
    length, width = qkv.shape[0], qkv.shape[1] // 3
    pairs = width // PAIR
    heads = [pl.BlockSpec((length, PAIR), lambda i, k=k: (0, k * pairs + i)) for k in range(3)]
    return call(
        attend_kernel,
        "attend",
        (pairs,),
        [docs.reshape(length, 1), docs.reshape(1, length), qkv, qkv, qkv],
        [whole((length, 1)), whole((1, length))] + heads,
        [shape_of((length, width), bf16), shape_of((pairs, 8, length), f32)],
        [
            pl.BlockSpec((length, PAIR), lambda i: (0, i)),
            pl.BlockSpec((1, 8, length), lambda i: (i, 0, 0)),
        ],
        [pltpu.VMEM((length, MAX_DOC + BLOCK), f32)],
        flops=4 * length * 768 * width,
    )


def attend_back_kernel(
    doc_ref, doc_t_ref, q_ref, k_ref, v_ref, grad_ref, log_ref, dq_ref, dk_ref, dv_ref,
    bias_ref, dk_sum, dv_sum,
):
    length = q_ref.shape[0]
    blocks = length // BLOCK

    @pl.when(pl.program_id(0) == 0)
    def _():
        for block in range(blocks):
            start, size = span_of(block)
            cols = slice(block * BLOCK, (block + 1) * BLOCK)
            row = iota((size, BLOCK), 0) + start
            col = iota((size, BLOCK), 1) + block * BLOCK
            kept = (col >= row) & (doc_ref[start : start + size, :] == doc_t_ref[:, cols])
            bias_ref[:size, cols] = jnp.where(kept, 0.0, -1e30)

    dk_sum[...] = jnp.zeros_like(dk_sum)
    dv_sum[...] = jnp.zeros_like(dv_sum)
    first = iota((BLOCK, PAIR), 1) < HEAD_DIM
    for block in range(blocks):
        start, size = span_of(block)
        rows, span = slice(block * BLOCK, (block + 1) * BLOCK), slice(start, start + size)
        query, grad = q_ref[rows, :] * 0.125, grad_ref[rows, :]
        keys, values = k_ref[span, :], v_ref[span, :]
        bias = bias_ref[:size, rows]
        parts, dk, dv = [], 0.0, 0.0
        for head, own in enumerate((first, ~first)):
            own_query = jnp.where(own, query, 0).astype(bf16)
            own_grad = jnp.where(own, grad, 0).astype(bf16)
            scores = dot_nt(keys, own_query) + bias
            probs = jnp.exp(scores - log_ref[0, head : head + 1, rows])
            dv = dv + dot_nn(probs.astype(bf16), own_grad)
            weighted = probs * dot_nt(values, own_grad)
            mean = jnp.sum(weighted, axis=0, keepdims=True)
            grad_scores = (weighted - probs * mean).astype(bf16)
            dk = dk + dot_nn(grad_scores, own_query)
            parts.append(dot_tn(grad_scores, keys) * 0.125)
        dq_ref[rows, :] = jnp.where(first, parts[0], parts[1]).astype(bf16)
        dk_sum[span, :] += dk
        dv_sum[span, :] += dv
    dk_ref[...] = dk_sum[...].astype(bf16)
    dv_ref[...] = dv_sum[...].astype(bf16)


def attend_back(docs, qkv, grad, logs):
    length, width = qkv.shape[0], qkv.shape[1] // 3
    pairs = width // PAIR
    heads = [pl.BlockSpec((length, PAIR), lambda i, k=k: (0, k * pairs + i)) for k in range(3)]
    one = pl.BlockSpec((length, PAIR), lambda i: (0, i))
    return call(
        attend_back_kernel,
        "attend_back",
        (pairs,),
        [docs.reshape(length, 1), docs.reshape(1, length), qkv, qkv, qkv, grad, logs],
        [whole((length, 1)), whole((1, length))]
        + heads
        + [one, pl.BlockSpec((1, 8, length), lambda i: (i, 0, 0))],
        [shape_of((length, width), bf16)] * 3,
        [one] * 3,
        [
            pltpu.VMEM((MAX_DOC + BLOCK, length), f32),
            pltpu.VMEM((length, PAIR), f32),
            pltpu.VMEM((length, PAIR), f32),
        ],
        flops=10 * length * 768 * width,
    )


def middle_kernel(
    inputs_ref, attended_ref, place_ref, weight_ref, small_ref, hidden_ref, normed_ref, gate_ref,
    gains_ref,
):
    @pl.when(pl.program_id(0) == 0)
    def _():
        gains_ref[...] = gains_of(small_ref)

    hidden = inputs_ref[...].astype(f32) + dot_nn(attended_ref[...], weight_ref[...])
    hidden_ref[...] = hidden
    xhat, _ = normalized(hidden)
    normed = (gains_ref[1:2, :] * xhat).astype(bf16)
    normed_ref[...] = normed
    logits = dot_nn(normed, small_ref[...])
    mask = place_ref[...] >= 0
    logits = jnp.where(mask, pltpu.roll(logits, LANES - 2, 1), -1e30)
    peak = jnp.max(logits, axis=-1, keepdims=True)
    raised = jnp.where(mask, jnp.exp(logits - peak), 0.0)
    gate_ref[...] = raised / jnp.sum(raised, axis=-1, keepdims=True)


def middle(inputs, attended, place, dense):
    length, width = inputs.shape
    row = pl.BlockSpec((BLOCK, width), lambda i: (i, 0))
    thin = pl.BlockSpec((BLOCK, LANES), lambda i: (i, 0))
    return call(
        middle_kernel,
        "middle",
        (length // BLOCK,),
        [inputs, attended, place, dense, dense],
        [
            row,
            row,
            thin,
            pl.BlockSpec((width, width), lambda i: (0, 3)),
            pl.BlockSpec((width, LANES), lambda i: (0, 4 * width // LANES)),
        ],
        [
            shape_of((length, width), f32),
            shape_of((length, width), bf16),
            shape_of((length, LANES), f32),
        ],
        [row, row, thin],
        [pltpu.VMEM((LANES, width), f32)],
        flops=2 * length * width * width,
    )


def window_base(counts_ref, block, expert, experts):
    base = counts_ref[block * experts + expert]
    return pl.multiple_of(jnp.minimum(base // 128 * 128, CAP - WINDOW), 128)


def expert_kernel(
    expert, experts, train, count, rows_ref, order_ref, counts_ref, place_t_ref, gate_ref, normed_ref,
    cot_ref, *rest,
):
    in_pieces, out_pieces, rest = rest[:count], rest[count : 2 * count], rest[2 * count :]
    result_ref, back_ref, rest = rest[0], rest[1], rest[2:]
    if train:
        in_own, in_other, out_own, out_other = rest[:4]
        rest = rest[4:]
        turned_x, acts, grads, staged = rest[6:]
    rows_x, rows_g, sum_r, sum_b, in_ref, out_ref = rest[:6]
    length, width = normed_ref.shape
    half = width // 2
    step = pl.program_id(0)
    load = counts_ref[length // BLOCK * experts + expert]

    @pl.when(step == 0)
    def _():
        rows_x[...] = jnp.zeros_like(rows_x)
        rows_g[...] = jnp.zeros_like(rows_g)
        sum_r[...] = jnp.zeros_like(sum_r)
        sum_b[...] = jnp.zeros_like(sum_b)
        for block in range(length // BLOCK):
            base = window_base(counts_ref, block, expert, experts)
            cols = slice(block * BLOCK, (block + 1) * BLOCK)
            pick = flag(iota((WINDOW, BLOCK), 0) + base == place_t_ref[expert : expert + 1, cols])
            window = pl.ds(base, WINDOW)
            rows_x[window, :] += dot_nn(pick, normed_ref[cols, :]).astype(bf16)
            scaled = gate_ref[cols, expert : expert + 1] * cot_ref[cols, :].astype(f32)
            rows_g[window, :] += dot_nn(pick, scaled.astype(bf16)).astype(bf16)
        if train:
            staged[...] = rows_x[...].T
            lay_out(order_ref, staged, turned_x.at[:half], turned_x.at[half:])

    put_together(rows_ref, in_pieces, in_ref)
    put_together(rows_ref, out_pieces, out_ref)

    def tile(index, carry):
        rows = pl.ds(pl.multiple_of(index * ROW_TILE, ROW_TILE), ROW_TILE)
        pre = dot_nn(rows_x[rows, :], in_ref[...])
        grad_rows = rows_g[rows, :]
        square = pre * pre
        bend = jnp.tanh(0.7978845608028654 * pre * (1.0 + 0.044715 * square))
        half = 0.5 + 0.5 * bend
        slope = half + pre * (0.5 - 0.5 * bend * bend) * (
            0.7978845608028654 + 0.1070322243 * square
        )
        act = (pre * half).astype(bf16)
        grad = (dot_nt(grad_rows, out_ref[...]) * slope).astype(bf16)
        sum_r[rows, :] += dot_nn(act, out_ref[...])
        sum_b[rows, :] += dot_nt(grad, in_ref[...])
        if train:
            acts[rows, :] = act
            grads[rows, :] = grad
        return carry

    tiles = jnp.maximum((load + ROW_TILE - 1) // ROW_TILE, 1)
    lax.fori_loop(0, tiles, tile, 0)
    if train:
        for amount in range(1, CAP // ROW_TILE + 1):

            @pl.when(tiles == amount)
            def _(used=amount * ROW_TILE):
                inner = dot_nn(turned_x[:, :used], grads[:used, :]).astype(bf16)
                in_own[...] = inner[:half]
                in_other[...] = inner[half:]
                staged[...] = dot_tn(acts[:used, :], rows_g[:used, :]).astype(bf16)

        lay_out(order_ref, staged, out_own, out_other)

    @pl.when(step == pl.num_programs(0) - 1)
    def _():
        result_ref[...] = sum_r[...].astype(bf16)
        back_ref[...] = sum_b[...].astype(bf16)


def expert_pass(
    expert, experts, train, rows, order, counts, place_t, gates, normed, cot, pieces
):
    length, width = normed.shape
    hidden = pieces[0][0].shape[1] // 2
    arrays = [p[0] for p in pieces]
    steps = hidden // width
    half = width // 2
    slab = pl.BlockSpec((half, width), lambda i: (0, i))
    outs = [shape_of((CAP, width), bf16)] * 2
    out_specs = [whole((CAP, width))] * 2
    scratch = [
        pltpu.VMEM((CAP, width), bf16),
        pltpu.VMEM((CAP, width), bf16),
        pltpu.VMEM((CAP, width), f32),
        pltpu.VMEM((CAP, width), f32),
        pltpu.VMEM((width, width), bf16),
        pltpu.VMEM((width, width), bf16),
    ]
    if train:
        outs = outs + [shape_of((half, hidden), bf16)] * 4
        out_specs = out_specs + [slab] * 4
        scratch = scratch + [
            pltpu.VMEM((width, CAP), bf16),
            pltpu.VMEM((CAP, width), bf16),
            pltpu.VMEM((CAP, width), bf16),
            pltpu.VMEM((width, width), bf16),
        ]
    return call(
        functools.partial(expert_kernel, expert, experts, train, len(pieces)),
        "expert_%d" % expert,
        (steps,),
        [rows, order, counts, place_t, gates, normed, cot] + arrays + arrays,
        [
            SMEM,
            SMEM,
            SMEM,
            whole(place_t.shape),
            whole(gates.shape),
            whole(normed.shape),
            whole(cot.shape),
        ]
        + gathered_specs(pieces, width, lambda i: i)
        + gathered_specs(pieces, width, lambda i: i + steps),
        outs,
        out_specs,
        scratch,
        limit=56,
        flops=(12 if train else 8) * 600 * width * hidden,
    )


def combine_kernel(
    experts, order_ref, counts_ref, place_ref, gate_ref, hidden_ref, normed_ref, cot_ref, attended_ref,
    weight_ref, small_ref, *rest,
):
    result_refs, back_refs = rest[:experts], rest[experts : 2 * experts]
    (output_ref, grad_hidden_ref, grad_heads_ref, own_ref, other_ref,
     gains_ref, weight_sum, gain_sum, router_sum, staged) = rest[2 * experts :]
    step = pl.program_id(0)

    @pl.when(step == 0)
    def _():
        gains_ref[...] = gains_of(small_ref)
        weight_sum[...] = jnp.zeros_like(weight_sum)
        gain_sum[...] = jnp.zeros_like(gain_sum)
        router_sum[...] = jnp.zeros_like(router_sum)

    cot = cot_ref[...].astype(f32)
    hidden = hidden_ref[...]
    gates = gate_ref[...]
    lane = iota((BLOCK, LANES), 1)
    total, grad_normed = hidden, 0.0
    grad_gate = jnp.zeros((BLOCK, LANES), f32)
    for expert in range(experts):
        base = window_base(counts_ref, step, expert, experts)
        window = pl.ds(base, WINDOW)
        pick = flag(iota((BLOCK, WINDOW), 1) + base == place_ref[:, expert : expert + 1])
        picked = dot_nn(pick, result_refs[expert][window, :])
        total = total + gates[:, expert : expert + 1] * picked
        grad_gate = jnp.where(
            lane == expert, jnp.sum(cot * picked, axis=-1, keepdims=True), grad_gate
        )
        grad_normed = grad_normed + dot_nn(pick, back_refs[expert][window, :])
    output_ref[...] = total.astype(bf16)
    grad_logits = gates * (grad_gate - jnp.sum(gates * grad_gate, axis=-1, keepdims=True))
    high = grad_logits.astype(bf16)
    low = (grad_logits - high.astype(f32)).astype(bf16)
    gains = gains_ref[...]
    router = pltpu.roll(gains, LANES - 2, 0).astype(bf16)
    grad_normed = grad_normed + dot_nn(high, router) + dot_nn(low, router)
    normed = normed_ref[...]
    router_sum[...] += dot_tn(normed, high) + dot_tn(normed, low)
    xhat, inverse = normalized(hidden)
    gain_sum[...] += jnp.sum(grad_normed * xhat, axis=0, keepdims=True)
    grad_hidden = cot + norm_back(xhat, inverse, gains[1:2, :], grad_normed)
    grad_hidden_ref[...] = grad_hidden
    branch = grad_hidden.astype(bf16)
    grad_heads_ref[...] = dot_nt(branch, weight_ref[...]).astype(bf16)
    weight_sum[...] += dot_tn(attended_ref[...], branch)

    @pl.when(step == pl.num_programs(0) - 1)
    def _():
        width = weight_sum.shape[1]
        gain = jnp.broadcast_to(gain_sum[...], (LANES, width)).T
        small = jnp.where(iota((width, LANES), 1) == LANES - 1, gain, router_sum[...])
        staged[:, :width] = weight_sum[...].astype(bf16)
        staged[:, width:] = small.astype(bf16)
        lay_out(order_ref, staged, own_ref, other_ref)


def combine(
    experts, order, counts, place, gates, hidden, normed, cot, attended, dense, results, backs
):
    length, width = hidden.shape
    row = pl.BlockSpec((BLOCK, width), lambda i: (i, 0))
    thin = pl.BlockSpec((BLOCK, LANES), lambda i: (i, 0))
    term = (width // 2, width + LANES)
    return call(
        functools.partial(combine_kernel, experts),
        "combine",
        (length // BLOCK,),
        [order, counts, place, gates, hidden, normed, cot, attended, dense, dense]
        + results
        + backs,
        [
            SMEM,
            SMEM,
            thin,
            thin,
            row,
            row,
            row,
            row,
            pl.BlockSpec((width, width), lambda i: (0, 3)),
            pl.BlockSpec((width, LANES), lambda i: (0, 4 * width // LANES)),
        ]
        + [whole((CAP, width))] * (2 * experts),
        [
            shape_of((length, width), bf16),
            shape_of((length, width), f32),
            shape_of((length, width), bf16),
            shape_of(term, bf16),
            shape_of(term, bf16),
        ],
        [row, row, row, whole(term), whole(term)],
        [
            pltpu.VMEM((LANES, width), f32),
            pltpu.VMEM((width, width), f32),
            pltpu.VMEM((1, width), f32),
            pltpu.VMEM((width, LANES), f32),
            pltpu.VMEM((width, width + LANES), bf16),
        ],
        limit=56,
        flops=8 * length * width * width,
    )


def weigh_kernel(order_ref, inputs_ref, gain_ref, dq_ref, dk_ref, dv_ref, own_ref, other_ref, turned,
                 staged):
    half = inputs_ref.shape[1] // 2

    @pl.when(pl.program_id(0) == 0)
    def _():
        xhat, _ = normalized(inputs_ref[...].astype(f32))
        staged[...] = (gain_ref[0:1, :].astype(f32) * xhat).astype(bf16).T
        lay_out(order_ref, staged, turned.at[:half], turned.at[half:])

    for k, ref in enumerate((dq_ref, dk_ref, dv_ref)):

        @pl.when(pl.program_id(0) == k)
        def _(ref=ref):
            grad = dot_nn(turned[...], ref[...]).astype(bf16)
            own_ref[...] = grad[:half]
            other_ref[...] = grad[half:]


def weigh(order, inputs, gains, dq, dk, dv):
    length, width = inputs.shape
    outs = [shape_of((width // 2, 3 * width), bf16)] * 2
    return call(
        weigh_kernel,
        "weigh",
        (3,),
        [order, inputs, gains, dq, dk, dv],
        [SMEM, whole((length, width)), whole(gains.shape)] + [whole((length, width))] * 3,
        outs,
        [pl.BlockSpec((width // 2, width), lambda i: (0, i))] * 2,
        [pltpu.VMEM((width, length), bf16), pltpu.VMEM((width, length), bf16)],
        limit=56,
        flops=2 * length * width * 3 * width,
    )


def finish_kernel(inputs_ref, gain_ref, dq_ref, dk_ref, dv_ref, grad_hidden_ref, weight_ref, grad_ref):
    width = inputs_ref.shape[1]
    xhat, inverse = normalized(inputs_ref[...].astype(f32))
    grad = 0.0
    for k, ref in enumerate((dq_ref, dk_ref, dv_ref)):
        grad = grad + dot_nt(ref[...], weight_ref[:, k * width : (k + 1) * width])
    gain = gain_ref[0:1, :].astype(f32)
    grad_ref[...] = grad_hidden_ref[...] + norm_back(xhat, inverse, gain, grad)


def finish(inputs, gains, dq, dk, dv, grad_hidden, dense):
    length, width = inputs.shape
    row = pl.BlockSpec((BLOCK, width), lambda i: (i, 0))
    return call(
        finish_kernel,
        "finish",
        (length // BLOCK,),
        [inputs, gains, dq, dk, dv, grad_hidden, dense],
        [
            row,
            whole(gains.shape),
            row,
            row,
            row,
            row,
            pl.BlockSpec((width, 3 * width), lambda i: (0, 0)),
        ],
        [shape_of((length, width), f32)],
        [row],
        limit=56,
        flops=2 * length * width * 3 * width,
    )[0]


def wide_slices(refs):
    edges = [sum(r.shape[1] for r in refs[:i]) for i in range(len(refs) + 1)]
    return [slice(a, b) for a, b in zip(edges, edges[1:])]


def end_kernel(count, *refs):
    own, got, (top, bottom) = refs[:count], refs[count : 2 * count], refs[2 * count :]
    half = top.shape[0]
    for one, other, cols in zip(own, got, wide_slices(own)):
        both = one[...].astype(f32) + other[...].astype(f32)
        top[:, cols] = both[:half].astype(bf16)
        bottom[:, cols] = both[half:].astype(bf16)


def middle_sums_kernel(count, *refs):
    own, got = refs[: 2 * count], refs[2 * count : 4 * count]
    top, bottom, to_low, to_high = refs[4 * count :]
    half = top.shape[0]
    for k, cols in enumerate(wide_slices(own[:count])):
        both = own[k][...].astype(f32) + got[k][...].astype(f32)
        to_low[:half, cols] = both[:half].astype(bf16)
        to_low[half:, cols] = (both[half:] + bottom[:, cols].astype(f32)).astype(bf16)
        both = own[count + k][...].astype(f32) + got[count + k][...].astype(f32)
        to_high[:half, cols] = (both[:half] + top[:, cols].astype(f32)).astype(bf16)
        to_high[half:, cols] = both[half:].astype(bf16)


def line_sums_kernel(count, narrow, place_ref, *refs):
    own, got = refs[:count], refs[count : 2 * count]
    low, high, mine, *sums, whole_ref = refs[2 * count :]
    rows = mine.shape[0]
    for one, other, cols in zip(own, got, wide_slices(own)):
        whole_ref[:, cols] = (
            one[...].astype(f32)
            + other[...].astype(f32)
            + low[:, cols].astype(f32)
            + high[:, cols].astype(f32)
        )
    for by, ref in enumerate([mine] + sums):
        number = lax.rem(place_ref[0] + by, narrow)
        if rows % 8 == 0:
            start = pl.multiple_of(number * rows, 8)
            ref[...] = whole_ref[pl.ds(start, rows), :].astype(ref.dtype)
        else:
            for other in range(narrow):

                @pl.when(number == other)
                def _(ref=ref, at=other * rows):
                    ref[...] = whole_ref[at : at + rows, :].astype(ref.dtype)


def blocks_at(arrays, number):
    return [pl.BlockSpec((a.shape[0] // 4, a.shape[1]), lambda *_: (number, 0)) for a in arrays]


def end_sums(own, got):
    count, columns = len(own), sum(a.shape[1] for a in own)
    outs = [shape_of((own[0].shape[0] // 8, columns), bf16)] * 2
    return call(
        functools.partial(end_kernel, count),
        "end_sums",
        (1,),
        own + got,
        blocks_at(own + got, 3),
        outs,
        [whole(o.shape) for o in outs],
    )


def middle_sums(own, got, ends):
    count, columns = len(own), sum(a.shape[1] for a in own)
    outs = [shape_of((own[0].shape[0] // 4, columns), bf16)] * 2
    return call(
        functools.partial(middle_sums_kernel, count),
        "middle_sums",
        (1,),
        own + own + got + got + ends,
        blocks_at(own, 1) + blocks_at(own, 2) + blocks_at(got, 1) + blocks_at(got, 2)
        + [whole(e.shape) for e in ends],
        outs,
        [whole(o.shape) for o in outs],
    )


def line_sums(place, narrow, own, got, sides):
    count, columns = len(own), sum(a.shape[1] for a in own)
    height = own[0].shape[0] // 4
    outs = [shape_of((height // narrow, columns), f32)]
    outs = outs + [shape_of((height // narrow, columns), bf16)] * (narrow - 1)
    made = call(
        functools.partial(line_sums_kernel, count, narrow),
        "line_sums",
        (1,),
        [place] + own + got + sides,
        [SMEM] + blocks_at(own + got, 0) + [whole(s.shape) for s in sides],
        outs,
        [whole(o.shape) for o in outs],
        [pltpu.VMEM((height, columns), f32)],
    )
    return made[0], made[1:]


AXES = ("outer", "core", "narrow")


class Links:
    def __init__(self, wide, narrow):
        self.wide, self.narrow = wide, narrow
        self.bits = [1 << b for b in range((wide // 2).bit_length() - 1)]
        self.outer, self.core, self.place = (lax.axis_index(axis) for axis in AXES)

    def send(self, part, to):
        pairs = []
        for wide in range(self.wide):
            for narrow in range(self.narrow):
                outer, core, place = to(wide // 2, wide % 2, narrow)
                target = (outer * 2 + core) * self.narrow + place
                pairs.append((wide * self.narrow + narrow, target))
        return lax.ppermute(part, AXES, pairs)

    def flip(self, part, mask):
        return self.send(part, lambda o, c, z: (o ^ mask, c, z))

    def swap(self, part):
        return self.send(part, lambda o, c, z: (o, 1 - c, z))

    def shift(self, part, by):
        return self.send(part, lambda o, c, z: (o, c, (z + by) % self.narrow))


def after(values, *deps):
    flat, tree = jax.tree.flatten(values)
    more = jax.tree.leaves(deps)
    held = lax.optimization_barrier(tuple(flat) + tuple(more))
    return jax.tree.unflatten(tree, held[: len(flat)])


def together(always, step):
    shapes = jax.eval_shape(step)
    return lax.cond(
        always, step, lambda: jax.tree.map(lambda s: jnp.zeros(s.shape, s.dtype), shapes)
    )


class Gather:
    def __init__(self, links, part):
        self.links, self.part = links, part

    def send_along(self, which=None):
        which = range(1, self.links.narrow) if which is None else which
        return [self.links.shift(self.part, -by) for by in which]

    def take_along(self, got):
        links, rows = self.links, self.part.shape[0]
        full = jnp.zeros((links.narrow * rows, self.part.shape[1]), self.part.dtype)
        for by, part in enumerate([self.part] + got):
            start = (links.place + by) % links.narrow * rows
            full = lax.dynamic_update_slice_in_dim(full, part, start, 0)
        self.full = full

    def send_first(self):
        links, full = self.links, self.full
        return [links.flip(full, bit) for bit in links.bits[:2]] + [links.swap(full)]

    def take_first(self, got):
        self.low, self.high, self.full_over = got
        half = self.full.shape[0] // 2
        self.sent = [self.low[:half], self.high[half:]]

    def send_second(self):
        links = self.links
        low, high = links.bits[0], links.bits[1]
        ends = [links.flip(self.sent[0], high), links.flip(self.sent[1], low)]
        return ends + [links.swap(self.low), links.swap(self.high)]

    def take_second(self, got):
        self.ends, self.over = got[:2], got[2:]

    def send_third(self):
        return [self.links.swap(e) for e in self.ends]

    def take_third(self, got):
        links = self.links
        own = [self.full, self.low, self.high] + self.ends
        over = [self.full_over] + self.over + got
        for bit in links.bits[2:]:
            own = own + [links.flip(p, bit) for p in own]
            over = over + [links.flip(p, bit) for p in over]
        self.pieces = [(p, p.shape[0], 0) for p in own + over]


def piece_rows(links, own_rows):
    height = links.narrow * own_rows
    low, high = links.bits[0], links.bits[1]
    marks = [(0, 0), (low, 0), (high, 0), (low | high, 0), (low | high, height // 2)]
    for bit in links.bits[2:]:
        marks = marks + [(mask | bit, extra) for mask, extra in marks]
    return jnp.stack(
        [
            ((links.outer ^ mask) * 2 + (links.core ^ over)) * height + extra
            for over in range(2)
            for mask, extra in marks
        ]
    ).astype(i32)


def part_rows(links, own_rows):
    height = links.narrow * own_rows
    return jnp.stack(
        [
            ((links.outer ^ mask) * 2 + (links.core ^ over)) * height
            for over in range(2)
            for mask in range(links.wide // 2)
        ]
    ).astype(i32)


def total(*terms):
    out = terms[0].astype(f32)
    for term in terms[1:]:
        out = out + term.astype(f32)
    return out


class Scatter:
    def __init__(self, links, own, other):
        self.links, self.own, self.other = links, own, other

    def send_over(self):
        return [self.links.swap(part) for part in self.other]

    def take_over(self, got):
        links, own = self.links, self.own
        for bit in links.bits[:1:-1]:
            height = own[0].shape[0] // 2
            sums = [total(a, b).astype(bf16) for a, b in zip(own, got)]
            own = [s[:height] for s in sums]
            got = [links.flip(s[height:], bit) for s in sums]
        self.near, self.got = own, got
        self.sums = end_sums(own, got)

    def send_first(self):
        low, high = self.links.bits[0], self.links.bits[1]
        return [self.links.flip(self.sums[0], low), self.links.flip(self.sums[1], high)]

    def take_first(self, got):
        self.sums = middle_sums(self.near, self.got, list(got))

    def send_second(self):
        low, high = self.links.bits[0], self.links.bits[1]
        return [self.links.flip(self.sums[0], low), self.links.flip(self.sums[1], high)]

    def take_second(self, got):
        links = self.links
        place = links.place.astype(i32).reshape(1)
        self.mine, self.sums = line_sums(place, links.narrow, self.near, self.got, list(got))

    def send_along(self, which=None):
        which = range(1, self.links.narrow) if which is None else which
        return [self.links.shift(self.sums[by - 1], by) for by in which]

    def take_along(self, got):
        self.result = total(self.mine, *got)


def on_device(
    wide, narrow, inputs, segment_ids, routes, attention_gain, qkv_weight, output_weight,
    mixture_gain, router_train, router_frozen, expert_in, expert_out, frozen_in, frozen_out,
    cotangent,
):
    links = Links(wide, narrow)
    length, width = inputs.shape
    own_rows = qkv_weight.shape[0]
    train_count = expert_in.shape[1]
    experts = train_count + frozen_in.shape[1]
    groups = expert_in.shape[2] // width
    docs = segment_ids[0]
    small = jnp.concatenate(
        [attention_gain[:, None], mixture_gain[:, None], router_train, router_frozen], axis=1
    )
    small = jnp.pad(small, ((0, 0), (0, LANES - small.shape[1])))
    dense = Gather(links, jnp.concatenate([qkv_weight, output_weight, small], axis=1))
    rows, order = piece_rows(links, own_rows), part_rows(links, own_rows)

    def packed(inner, outer):
        inner = inner.reshape(own_rows, width, groups).transpose(0, 2, 1).reshape(own_rows, -1)
        return jnp.concatenate([inner, outer.reshape(own_rows, -1)], axis=1)

    def part_of(e):
        if e < train_count:
            return packed(expert_in[:, e], expert_out[:, e])
        return packed(frozen_in[:, e - train_count], frozen_out[:, e - train_count])

    weights = [Gather(links, part_of(e)) for e in range(experts)]
    always = segment_ids[0, 0] >= 0
    chosen = (routes[:, :, None] == jnp.arange(experts, dtype=i32)).astype(i32)
    per_block = jnp.sum(chosen.reshape(length // BLOCK, 2 * BLOCK, experts), axis=1)
    counts = jnp.concatenate([jnp.zeros((1, experts), i32), jnp.cumsum(per_block, axis=0)])
    counts = counts.reshape(-1)
    place, place_t = route_places(routes)

    def run(expert, normed):
        return expert_pass(
            expert, experts, expert < train_count, rows, order, counts, place_t, gates, normed,
            cotangent, weights[expert].pieces,
        )

    shifts = list(range(1, narrow))

    def line(gather, *deps):
        part = after(gather.part, *deps) if deps else gather.part
        gather.full = lax.all_gather(part, "narrow", axis=0, tiled=True)

    w0, w1, w2, w3 = weights
    w0.part = after(w0.part, dense.part)
    line(w0)
    dense.take_along(dense.send_along())
    line(w1, dense.full)
    dense.take_first(dense.send_first())
    line(w2, dense.low)
    dense.take_second(dense.send_second())
    line(w3, dense.ends)
    dense.take_third(dense.send_third())

    def step():
        qkv, full, gains = project(rows, inputs, dense.pieces)
        attended, logs = attend(docs, qkv)
        return w0.send_first(), (qkv, full, gains, attended, logs)

    got, (qkv, dense, gains, attended, logs) = together(always, step)
    w0.take_first(got)
    got, (hidden, normed, gates) = together(
        always, lambda: (w0.send_second(), middle(inputs, attended, place, dense))
    )
    w0.take_second(got)
    w0.take_third(w0.send_third())
    got, one = together(always, lambda: (w1.send_first(), run(0, normed)))
    w1.take_first(got)
    w1.take_second(w1.send_second())
    w1.take_third(w1.send_third())
    term0 = Scatter(links, [one[2], one[4]], [one[3], one[5]])
    w2.full = after(w2.full, one[0])
    got, more, two = together(
        always, lambda: (w2.send_first(), term0.send_over(), run(1, normed))
    )
    w2.take_first(got)

    def step():
        term0.take_over(more)
        return w2.send_second(), (term0.near, term0.got, term0.sums)

    got, (term0.near, term0.got, term0.sums) = together(always, step)
    w2.take_second(got)
    w2.take_third(w2.send_third())
    term1 = Scatter(links, [two[2], two[4]], [two[3], two[5]])
    w3.full = after(w3.full, two[0])
    got, more, three = together(
        always, lambda: (w3.send_first(), term1.send_over(), run(2, normed))
    )
    w3.take_first(got)

    def step():
        term1.take_over(more)
        return w3.send_second(), (term1.near, term1.got, term1.sums)

    got, (term1.near, term1.got, term1.sums) = together(always, step)
    w3.take_second(got)
    w3.take_third(w3.send_third())
    got, more, four = together(
        always, lambda: (term0.send_first(), term1.send_first(), run(3, normed))
    )
    term0.take_first(got)
    results, backs = [[m[i] for m in (one, two, three, four)] for i in range(2)]

    def step():
        made = combine(
            experts, order, counts, place, gates, hidden, normed, cotangent, attended, dense,
            results, backs,
        )
        term1.take_first(more)
        return term0.send_second(), term1.sums, made

    got, term1.sums, (block_output, grad_hidden, grad_heads, *made) = together(always, step)
    term0.take_second(got)
    out_term = Scatter(links, *[[m] for m in made])
    got, more, (dq, dk, dv) = together(
        always,
        lambda: (
            term1.send_second(), term0.send_along(), attend_back(docs, qkv, grad_heads, logs)
        ),
    )
    term1.take_second(got)
    over, one, made = together(
        always,
        lambda: (
            out_term.send_over(), term1.send_along(shifts[:1]),
            weigh(order, inputs, gains, dq, dk, dv),
        ),
    )
    out_term.take_over(over)
    qkv_term = Scatter(links, *[[m] for m in made])
    over, got, last, input_grad = together(
        always,
        lambda: (
            qkv_term.send_over(), out_term.send_first(), term1.send_along(shifts[2:]),
            finish(inputs, gains, dq, dk, dv, grad_hidden, dense),
        ),
    )
    qkv_term.take_over(over)
    out_term.take_first(got)

    def unpacked(parts):
        full = total(*parts)
        inner = groups * width
        inner, outer = full[:, :inner], full[:, inner:]
        inner = inner.reshape(own_rows, groups, width).transpose(0, 2, 1).reshape(own_rows, -1)
        return inner, outer.reshape(own_rows * groups, width)

    got, two, first = together(
        always,
        lambda: (
            qkv_term.send_first(), out_term.send_second(), unpacked([term0.mine] + more)
        ),
    )
    qkv_term.take_first(got)
    out_term.take_second(two)
    got, middle_part = together(
        always, lambda: (qkv_term.send_second(), term1.send_along(shifts[1:2]))
    )
    qkv_term.take_second(got)

    def step():
        second = unpacked([term1.mine] + one + middle_part + last)
        in_grad, down_grad = [jnp.stack(pair, axis=1) for pair in zip(first, second)]
        return qkv_term.send_along(), out_term.send_along(), in_grad, down_grad

    got, two, in_grad, down_grad = together(always, step)
    qkv_term.take_along(got)
    out_term.take_along(two)
    out_term, qkv_grad = out_term.result, qkv_term.result
    gain_grad = jnp.sum(qkv_weight.astype(f32) * qkv_grad, axis=1) / attention_gain.astype(f32)
    return (
        block_output,
        input_grad,
        gain_grad,
        qkv_grad,
        out_term[:, :width],
        out_term[:, width + LANES - 1],
        out_term[:, width : width + train_count],
        in_grad,
        down_grad,
    )


def solution(mesh):
    wide, narrow = mesh.shape["wide"], mesh.shape["narrow"]
    mesh = Mesh(mesh.devices.reshape(wide // 2, 2, narrow), AXES)
    rows = P(AXES)
    return jax.shard_map(
        functools.partial(on_device, wide, narrow),
        mesh=mesh,
        in_specs=(rows,) * 14,
        out_specs=(rows,) * 9,
        check_vma=False,
    )
```

```python
import functools

import jax
import jax.numpy as jnp
from jax import lax
from jax.experimental import pallas as pl
from jax.experimental.pallas import tpu as pltpu
from jax.sharding import Mesh, PartitionSpec as P

HEAD_DIM = 64
PAIR = 2 * HEAD_DIM
CAP = 768
MAX_DOC = 512
BLOCK = 256
WINDOW = BLOCK + 128
ROW_TILE = 256
LANES = 128
EPS = 1e-05
bf16, f32, i32 = jnp.bfloat16, jnp.float32, jnp.int32


def dot_nn(a, b):
    return lax.dot_general(a, b, (((1,), (0,)), ((), ())), preferred_element_type=f32)


def dot_nt(a, b):
    return lax.dot_general(a, b, (((1,), (1,)), ((), ())), preferred_element_type=f32)


def dot_tn(a, b):
    return lax.dot_general(a, b, (((0,), (0,)), ((), ())), preferred_element_type=f32)


def iota(shape, dim):
    return lax.broadcasted_iota(i32, shape, dim)


def flag(mask, dtype=bf16):
    return jnp.where(mask, 1.0, 0.0).astype(dtype)


def normalized(values):
    center = values - jnp.mean(values, axis=-1, keepdims=True)
    spread = jnp.mean(center * center, axis=-1, keepdims=True)
    inverse = lax.rsqrt(spread + EPS)
    return center * inverse, inverse


def norm_back(xhat, inverse, gain, grad):
    scaled = grad * gain
    return inverse * (
        scaled
        - jnp.mean(scaled, axis=-1, keepdims=True)
        - xhat * jnp.mean(scaled * xhat, axis=-1, keepdims=True)
    )


def params(limit_mib, **kw):
    return pltpu.CompilerParams(vmem_limit_bytes=limit_mib << 20, **kw)


def whole(shape):
    return pl.BlockSpec(shape, lambda *_: (0,) * len(shape))


def call(kernel, name, grid, ins, in_specs, outs, out_specs, scratch=(), limit=48, flops=0):
    size = sum(a.size * a.dtype.itemsize for a in ins) + sum(
        o.size * o.dtype.itemsize for o in outs
    )
    return pl.pallas_call(
        kernel,
        name=name,
        grid=grid,
        in_specs=in_specs,
        out_specs=out_specs,
        out_shape=outs,
        scratch_shapes=list(scratch),
        compiler_params=params(limit),
        cost_estimate=pl.CostEstimate(flops=flops, bytes_accessed=size, transcendentals=0),
    )(*ins)


def shape_of(shape, dtype):
    return jax.ShapeDtypeStruct(shape, dtype)


def gathered_specs(pieces, columns, index):
    return [
        pl.BlockSpec((height, columns), lambda *i, at=at: (at, index(*i)))
        for _, height, at in pieces
    ]


def put_together(rows_ref, piece_refs, whole_ref):
    for number, piece in enumerate(piece_refs):
        height = piece.shape[0]
        start = pl.multiple_of(rows_ref[number], 16 if height % 16 == 0 else 8)
        whole_ref[pl.ds(start, height), :] = piece[...]


def lay_out(order_ref, staged_ref, own_ref, other_ref):
    parts = order_ref.shape[0] // 2
    height = own_ref.shape[0] // parts
    for half, ref in enumerate((own_ref, other_ref)):
        for part in range(parts):
            start = order_ref[half * parts + part]
            start = pl.multiple_of(start, 16 if height % 16 == 0 else 8)
            ref[part * height : (part + 1) * height, :] = staged_ref[pl.ds(start, height), :]


SMEM = pl.BlockSpec(memory_space=pltpu.SMEM)


def route_kernel(routes_ref, routes_t_ref, place_ref, place_t_ref):
    length = routes_ref.shape[0]
    lane = iota((length, LANES), 1)
    mask = (lane == routes_ref[:, 0:1]) | (lane == routes_ref[:, 1:2])
    before = flag(iota((length, length), 1) < iota((length, length), 0))
    place_ref[...] = jnp.where(mask, dot_nn(before, flag(mask)), -1.0).astype(i32)
    sub = iota((8, length), 0)
    mask_t = (sub == routes_t_ref[0:1, :]) | (sub == routes_t_ref[1:2, :])
    before_t = flag(iota((length, length), 0) < iota((length, length), 1))
    place_t_ref[...] = jnp.where(mask_t, dot_nn(flag(mask_t), before_t), -1.0).astype(i32)


def route_places(routes):
    length = routes.shape[0]
    outs = [shape_of((length, LANES), i32), shape_of((8, length), i32)]
    return call(
        route_kernel,
        "places",
        (),
        [routes, routes.T],
        [whole((length, 2)), whole((2, length))],
        outs,
        [whole(o.shape) for o in outs],
    )


def gains_of(small_ref):
    return small_ref[...].astype(f32).T


def project_kernel(count, rows_ref, inputs_ref, *rest):
    pieces, (qkv_ref, dense_ref, rows_out_ref, gains_ref) = rest[:count], rest[count:]
    width = inputs_ref.shape[1]

    @pl.when(pl.program_id(0) == 0)
    def _():
        put_together(rows_ref, pieces, dense_ref)
        gains_ref[...] = dense_ref[:, 4 * width :].astype(f32).T
        rows_out_ref[...] = gains_ref[:16, :].astype(bf16)

    xhat, _ = normalized(inputs_ref[...].astype(f32))
    normed = (gains_ref[0:1, :] * xhat).astype(bf16)
    qkv_ref[...] = dot_nn(normed, dense_ref[:, : 3 * width]).astype(bf16)


def project(rows, inputs, pieces):
    length, width = inputs.shape
    columns = pieces[0][0].shape[1]
    return call(
        functools.partial(project_kernel, len(pieces)),
        "project",
        (length // BLOCK,),
        [rows, inputs] + [p[0] for p in pieces],
        [SMEM, pl.BlockSpec((BLOCK, width), lambda i: (i, 0))]
        + gathered_specs(pieces, columns, lambda i: 0),
        [
            shape_of((length, 3 * width), bf16),
            shape_of((width, columns), bf16),
            shape_of((16, width), bf16),
        ],
        [
            pl.BlockSpec((BLOCK, 3 * width), lambda i: (i, 0)),
            whole((width, columns)),
            whole((16, width)),
        ],
        [pltpu.VMEM((LANES, width), f32)],
        flops=2 * length * width * 3 * width,
    )


def span_of(block):
    reach = MAX_DOC // BLOCK
    start = max(0, block - reach) * BLOCK
    return start, (block + 1) * BLOCK - start


def attend_kernel(doc_ref, doc_t_ref, q_ref, k_ref, v_ref, out_ref, log_ref, bias_ref):
    length = q_ref.shape[0]
    blocks = length // BLOCK

    @pl.when(pl.program_id(0) == 0)
    def _():
        for block in range(blocks):
            start, size = span_of(block)
            rows = slice(block * BLOCK, (block + 1) * BLOCK)
            row = iota((BLOCK, size), 0) + block * BLOCK
            col = iota((BLOCK, size), 1) + start
            kept = (row >= col) & (doc_ref[rows, :] == doc_t_ref[:, start : start + size])
            bias_ref[rows, :size] = jnp.where(kept, 0.0, -1e30)

    first = iota((BLOCK, PAIR), 1) < HEAD_DIM
    for block in range(blocks):
        start, size = span_of(block)
        rows = slice(block * BLOCK, (block + 1) * BLOCK)
        query = q_ref[rows, :] * 0.125
        keys, values = k_ref[start : start + size, :], v_ref[start : start + size, :]
        bias = bias_ref[rows, :size]
        parts, logs = [], []
        for own in (first, ~first):
            scores = dot_nt(jnp.where(own, query, 0).astype(bf16), keys) + bias
            peak = jnp.max(scores, axis=-1, keepdims=True)
            raised = jnp.exp(scores - peak)
            total = jnp.sum(raised, axis=-1, keepdims=True)
            parts.append(dot_nn(raised.astype(bf16), values) * (1.0 / total))
            logs.append(peak + jnp.log(total))
        out_ref[rows, :] = jnp.where(first, parts[0], parts[1]).astype(bf16)
        turned = jnp.where(first, logs[0], logs[1]).T
        log_ref[0, 0:1, rows] = turned[0:1, :]
        log_ref[0, 1:2, rows] = turned[HEAD_DIM : HEAD_DIM + 1, :]


def attend(docs, qkv):
    length, width = qkv.shape[0], qkv.shape[1] // 3
    pairs = width // PAIR
    heads = [pl.BlockSpec((length, PAIR), lambda i, k=k: (0, k * pairs + i)) for k in range(3)]
    return call(
        attend_kernel,
        "attend",
        (pairs,),
        [docs.reshape(length, 1), docs.reshape(1, length), qkv, qkv, qkv],
        [whole((length, 1)), whole((1, length))] + heads,
        [shape_of((length, width), bf16), shape_of((pairs, 8, length), f32)],
        [
            pl.BlockSpec((length, PAIR), lambda i: (0, i)),
            pl.BlockSpec((1, 8, length), lambda i: (i, 0, 0)),
        ],
        [pltpu.VMEM((length, MAX_DOC + BLOCK), f32)],
        flops=4 * length * 768 * width,
    )


def attend_back_kernel(
    doc_ref, doc_t_ref, q_ref, k_ref, v_ref, grad_ref, log_ref, dq_ref, dk_ref, dv_ref,
    bias_ref, dk_sum, dv_sum,
):
    length = q_ref.shape[0]
    blocks = length // BLOCK

    @pl.when(pl.program_id(0) == 0)
    def _():
        for block in range(blocks):
            start, size = span_of(block)
            cols = slice(block * BLOCK, (block + 1) * BLOCK)
            row = iota((size, BLOCK), 0) + start
            col = iota((size, BLOCK), 1) + block * BLOCK
            kept = (col >= row) & (doc_ref[start : start + size, :] == doc_t_ref[:, cols])
            bias_ref[:size, cols] = jnp.where(kept, 0.0, -1e30)

    dk_sum[...] = jnp.zeros_like(dk_sum)
    dv_sum[...] = jnp.zeros_like(dv_sum)
    first = iota((BLOCK, PAIR), 1) < HEAD_DIM
    for block in range(blocks):
        start, size = span_of(block)
        rows, span = slice(block * BLOCK, (block + 1) * BLOCK), slice(start, start + size)
        query, grad = q_ref[rows, :] * 0.125, grad_ref[rows, :]
        keys, values = k_ref[span, :], v_ref[span, :]
        bias = bias_ref[:size, rows]
        parts, dk, dv = [], 0.0, 0.0
        for head, own in enumerate((first, ~first)):
            own_query = jnp.where(own, query, 0).astype(bf16)
            own_grad = jnp.where(own, grad, 0).astype(bf16)
            scores = dot_nt(keys, own_query) + bias
            probs = jnp.exp(scores - log_ref[0, head : head + 1, rows])
            dv = dv + dot_nn(probs.astype(bf16), own_grad)
            weighted = probs * dot_nt(values, own_grad)
            mean = jnp.sum(weighted, axis=0, keepdims=True)
            grad_scores = (weighted - probs * mean).astype(bf16)
            dk = dk + dot_nn(grad_scores, own_query)
            parts.append(dot_tn(grad_scores, keys) * 0.125)
        dq_ref[rows, :] = jnp.where(first, parts[0], parts[1]).astype(bf16)
        dk_sum[span, :] += dk
        dv_sum[span, :] += dv
    dk_ref[...] = dk_sum[...].astype(bf16)
    dv_ref[...] = dv_sum[...].astype(bf16)


def attend_back(docs, qkv, grad, logs):
    length, width = qkv.shape[0], qkv.shape[1] // 3
    pairs = width // PAIR
    heads = [pl.BlockSpec((length, PAIR), lambda i, k=k: (0, k * pairs + i)) for k in range(3)]
    one = pl.BlockSpec((length, PAIR), lambda i: (0, i))
    return call(
        attend_back_kernel,
        "attend_back",
        (pairs,),
        [docs.reshape(length, 1), docs.reshape(1, length), qkv, qkv, qkv, grad, logs],
        [whole((length, 1)), whole((1, length))]
        + heads
        + [one, pl.BlockSpec((1, 8, length), lambda i: (i, 0, 0))],
        [shape_of((length, width), bf16)] * 3,
        [one] * 3,
        [
            pltpu.VMEM((MAX_DOC + BLOCK, length), f32),
            pltpu.VMEM((length, PAIR), f32),
            pltpu.VMEM((length, PAIR), f32),
        ],
        flops=10 * length * 768 * width,
    )


def middle_kernel(
    inputs_ref, attended_ref, place_ref, weight_ref, small_ref, hidden_ref, normed_ref, gate_ref,
    gains_ref,
):
    @pl.when(pl.program_id(0) == 0)
    def _():
        gains_ref[...] = gains_of(small_ref)

    hidden = inputs_ref[...].astype(f32) + dot_nn(attended_ref[...], weight_ref[...])
    hidden_ref[...] = hidden
    xhat, _ = normalized(hidden)
    normed = (gains_ref[1:2, :] * xhat).astype(bf16)
    normed_ref[...] = normed
    logits = dot_nn(normed, small_ref[...])
    mask = place_ref[...] >= 0
    logits = jnp.where(mask, pltpu.roll(logits, LANES - 2, 1), -1e30)
    peak = jnp.max(logits, axis=-1, keepdims=True)
    raised = jnp.where(mask, jnp.exp(logits - peak), 0.0)
    gate_ref[...] = raised / jnp.sum(raised, axis=-1, keepdims=True)


def middle(inputs, attended, place, dense):
    length, width = inputs.shape
    row = pl.BlockSpec((BLOCK, width), lambda i: (i, 0))
    thin = pl.BlockSpec((BLOCK, LANES), lambda i: (i, 0))
    return call(
        middle_kernel,
        "middle",
        (length // BLOCK,),
        [inputs, attended, place, dense, dense],
        [
            row,
            row,
            thin,
            pl.BlockSpec((width, width), lambda i: (0, 3)),
            pl.BlockSpec((width, LANES), lambda i: (0, 4 * width // LANES)),
        ],
        [
            shape_of((length, width), f32),
            shape_of((length, width), bf16),
            shape_of((length, LANES), f32),
        ],
        [row, row, thin],
        [pltpu.VMEM((LANES, width), f32)],
        flops=2 * length * width * width,
    )


def window_base(counts_ref, block, expert, experts):
    base = counts_ref[block * experts + expert]
    return pl.multiple_of(jnp.minimum(base // 128 * 128, CAP - WINDOW), 128)


def dispatch_kernel(
    expert, experts, order_ref, counts_ref, place_t_ref, gate_ref, normed_ref, cot_ref, x_ref, g_ref,
    *rest,
):
    length = normed_ref.shape[0]
    x_ref[...] = jnp.zeros_like(x_ref)
    g_ref[...] = jnp.zeros_like(g_ref)
    for block in range(length // BLOCK):
        base = window_base(counts_ref, block, expert, experts)
        cols = slice(block * BLOCK, (block + 1) * BLOCK)
        pick = flag(iota((WINDOW, BLOCK), 0) + base == place_t_ref[expert : expert + 1, cols])
        window = pl.ds(base, WINDOW)
        x_ref[window, :] += dot_nn(pick, normed_ref[cols, :]).astype(bf16)
        scaled = gate_ref[cols, expert : expert + 1] * cot_ref[cols, :].astype(f32)
        g_ref[window, :] += dot_nn(pick, scaled.astype(bf16)).astype(bf16)
    if rest:
        turned_ref, staged = rest
        half = turned_ref.shape[0] // 2
        staged[...] = x_ref[...].T
        lay_out(order_ref, staged, turned_ref.at[:half], turned_ref.at[half:])


def dispatch(expert, experts, train, order, counts, place_t, gates, normed, cot):
    width = normed.shape[1]
    outs = [shape_of((CAP, width), bf16)] * 2
    outs = outs + ([shape_of((width, CAP), bf16)] if train else [])
    ins = [place_t, gates, normed, cot]
    return call(
        functools.partial(dispatch_kernel, expert, experts),
        "dispatch_%d" % expert,
        (1,),
        [order, counts] + ins,
        [SMEM, SMEM] + [whole(a.shape) for a in ins],
        outs,
        [whole(o.shape) for o in outs],
        [pltpu.VMEM((width, CAP), bf16)] if train else [],
        flops=4 * CAP * WINDOW * width,
    )


def expert_kernel(slot, train, count, rows_ref, order_ref, counts_ref, *rest):
    rows_x, rows_g, rest = rest[0], rest[1], rest[2:]
    if train:
        turned_x, rest = rest[0], rest[1:]
    in_pieces, out_pieces, rest = rest[:count], rest[count : 2 * count], rest[2 * count :]
    result_ref, back_ref, rest = rest[0], rest[1], rest[2:]
    if train:
        in_own, in_other, out_own, out_other = rest[:4]
        rest = rest[4:]
        acts, grads, staged = rest[4:]
    sum_r, sum_b, in_ref, out_ref = rest[:4]
    half = rows_x.shape[1] // 2
    step = pl.program_id(0)
    load = counts_ref[slot]

    @pl.when(step == 0)
    def _():
        sum_r[...] = jnp.zeros_like(sum_r)
        sum_b[...] = jnp.zeros_like(sum_b)

    put_together(rows_ref, in_pieces, in_ref)
    put_together(rows_ref, out_pieces, out_ref)

    def tile(index, carry):
        rows = pl.ds(pl.multiple_of(index * ROW_TILE, ROW_TILE), ROW_TILE)
        pre = dot_nn(rows_x[rows, :], in_ref[...])
        grad_rows = rows_g[rows, :]
        square = pre * pre
        bend = jnp.tanh(0.7978845608028654 * pre * (1.0 + 0.044715 * square))
        half = 0.5 + 0.5 * bend
        slope = half + pre * (0.5 - 0.5 * bend * bend) * (
            0.7978845608028654 + 0.1070322243 * square
        )
        act = (pre * half).astype(bf16)
        grad = (dot_nt(grad_rows, out_ref[...]) * slope).astype(bf16)
        sum_r[rows, :] += dot_nn(act, out_ref[...])
        sum_b[rows, :] += dot_nt(grad, in_ref[...])
        if train:
            acts[rows, :] = act
            grads[rows, :] = grad
        return carry

    tiles = jnp.maximum((load + ROW_TILE - 1) // ROW_TILE, 1)
    lax.fori_loop(0, tiles, tile, 0)
    if train:
        for amount in range(1, CAP // ROW_TILE + 1):

            @pl.when(tiles == amount)
            def _(used=amount * ROW_TILE):
                inner = dot_nn(turned_x[:, :used], grads[:used, :]).astype(bf16)
                in_own[...] = inner[:half]
                in_other[...] = inner[half:]
                staged[...] = dot_tn(acts[:used, :], rows_g[:used, :]).astype(bf16)

        lay_out(order_ref, staged, out_own, out_other)

    @pl.when(step == pl.num_programs(0) - 1)
    def _():
        result_ref[...] = sum_r[...].astype(bf16)
        back_ref[...] = sum_b[...].astype(bf16)


def expert_pass(expert, slot, train, rows, order, counts, picked, pieces):
    width = picked[0].shape[1]
    hidden = pieces[0][0].shape[1] // 2
    arrays = [p[0] for p in pieces]
    steps = hidden // width
    half = width // 2
    slab = pl.BlockSpec((half, width), lambda i: (0, i))
    outs = [shape_of((CAP, width), bf16)] * 2
    out_specs = [whole((CAP, width))] * 2
    scratch = [
        pltpu.VMEM((CAP, width), f32),
        pltpu.VMEM((CAP, width), f32),
        pltpu.VMEM((width, width), bf16),
        pltpu.VMEM((width, width), bf16),
    ]
    if train:
        outs = outs + [shape_of((half, hidden), bf16)] * 4
        out_specs = out_specs + [slab] * 4
        scratch = scratch + [
            pltpu.VMEM((CAP, width), bf16),
            pltpu.VMEM((CAP, width), bf16),
            pltpu.VMEM((width, width), bf16),
        ]
    return call(
        functools.partial(expert_kernel, slot, train, len(pieces)),
        "expert_%d" % expert,
        (steps,),
        [rows, order, counts] + list(picked) + arrays + arrays,
        [SMEM, SMEM, SMEM]
        + [whole(p.shape) for p in picked]
        + gathered_specs(pieces, width, lambda i: i)
        + gathered_specs(pieces, width, lambda i: i + steps),
        outs,
        out_specs,
        scratch,
        limit=56,
        flops=(12 if train else 8) * 600 * width * hidden,
    )


def combine_kernel(
    experts, order_ref, counts_ref, place_ref, gate_ref, hidden_ref, normed_ref, cot_ref, attended_ref,
    weight_ref, small_ref, *rest,
):
    result_refs, back_refs = rest[:experts], rest[experts : 2 * experts]
    (output_ref, grad_hidden_ref, grad_heads_ref, own_ref, other_ref,
     gains_ref, weight_sum, gain_sum, router_sum, staged) = rest[2 * experts :]
    step = pl.program_id(0)

    @pl.when(step == 0)
    def _():
        gains_ref[...] = gains_of(small_ref)
        weight_sum[...] = jnp.zeros_like(weight_sum)
        gain_sum[...] = jnp.zeros_like(gain_sum)
        router_sum[...] = jnp.zeros_like(router_sum)

    cot = cot_ref[...].astype(f32)
    hidden = hidden_ref[...]
    gates = gate_ref[...]
    lane = iota((BLOCK, LANES), 1)
    total, grad_normed = hidden, 0.0
    grad_gate = jnp.zeros((BLOCK, LANES), f32)
    for expert in range(experts):
        base = window_base(counts_ref, step, expert, experts)
        window = pl.ds(base, WINDOW)
        pick = flag(iota((BLOCK, WINDOW), 1) + base == place_ref[:, expert : expert + 1])
        picked = dot_nn(pick, result_refs[expert][window, :])
        total = total + gates[:, expert : expert + 1] * picked
        grad_gate = jnp.where(
            lane == expert, jnp.sum(cot * picked, axis=-1, keepdims=True), grad_gate
        )
        grad_normed = grad_normed + dot_nn(pick, back_refs[expert][window, :])
    output_ref[...] = total.astype(bf16)
    grad_logits = gates * (grad_gate - jnp.sum(gates * grad_gate, axis=-1, keepdims=True))
    high = grad_logits.astype(bf16)
    low = (grad_logits - high.astype(f32)).astype(bf16)
    gains = gains_ref[...]
    router = pltpu.roll(gains, LANES - 2, 0).astype(bf16)
    grad_normed = grad_normed + dot_nn(high, router) + dot_nn(low, router)
    normed = normed_ref[...]
    router_sum[...] += dot_tn(normed, high) + dot_tn(normed, low)
    xhat, inverse = normalized(hidden)
    gain_sum[...] += jnp.sum(grad_normed * xhat, axis=0, keepdims=True)
    grad_hidden = cot + norm_back(xhat, inverse, gains[1:2, :], grad_normed)
    grad_hidden_ref[...] = grad_hidden
    branch = grad_hidden.astype(bf16)
    grad_heads_ref[...] = dot_nt(branch, weight_ref[...]).astype(bf16)
    weight_sum[...] += dot_tn(attended_ref[...], branch)

    @pl.when(step == pl.num_programs(0) - 1)
    def _():
        width = weight_sum.shape[1]
        gain = jnp.broadcast_to(gain_sum[...], (LANES, width)).T
        small = jnp.where(iota((width, LANES), 1) == LANES - 1, gain, router_sum[...])
        staged[:, :width] = weight_sum[...].astype(bf16)
        staged[:, width:] = small.astype(bf16)
        lay_out(order_ref, staged, own_ref, other_ref)


def combine(
    experts, order, counts, place, gates, hidden, normed, cot, attended, dense, results, backs
):
    length, width = hidden.shape
    row = pl.BlockSpec((BLOCK, width), lambda i: (i, 0))
    thin = pl.BlockSpec((BLOCK, LANES), lambda i: (i, 0))
    term = (width // 2, width + LANES)
    return call(
        functools.partial(combine_kernel, experts),
        "combine",
        (length // BLOCK,),
        [order, counts, place, gates, hidden, normed, cot, attended, dense, dense]
        + results
        + backs,
        [
            SMEM,
            SMEM,
            thin,
            thin,
            row,
            row,
            row,
            row,
            pl.BlockSpec((width, width), lambda i: (0, 3)),
            pl.BlockSpec((width, LANES), lambda i: (0, 4 * width // LANES)),
        ]
        + [whole((CAP, width))] * (2 * experts),
        [
            shape_of((length, width), bf16),
            shape_of((length, width), f32),
            shape_of((length, width), bf16),
            shape_of(term, bf16),
            shape_of(term, bf16),
        ],
        [row, row, row, whole(term), whole(term)],
        [
            pltpu.VMEM((LANES, width), f32),
            pltpu.VMEM((width, width), f32),
            pltpu.VMEM((1, width), f32),
            pltpu.VMEM((width, LANES), f32),
            pltpu.VMEM((width, width + LANES), bf16),
        ],
        limit=56,
        flops=8 * length * width * width,
    )


def weigh_kernel(order_ref, inputs_ref, gain_ref, dq_ref, dk_ref, dv_ref, own_ref, other_ref, turned,
                 staged):
    half = inputs_ref.shape[1] // 2

    @pl.when(pl.program_id(0) == 0)
    def _():
        xhat, _ = normalized(inputs_ref[...].astype(f32))
        staged[...] = (gain_ref[0:1, :].astype(f32) * xhat).astype(bf16).T
        lay_out(order_ref, staged, turned.at[:half], turned.at[half:])

    for k, ref in enumerate((dq_ref, dk_ref, dv_ref)):

        @pl.when(pl.program_id(0) == k)
        def _(ref=ref):
            grad = dot_nn(turned[...], ref[...]).astype(bf16)
            own_ref[...] = grad[:half]
            other_ref[...] = grad[half:]


def weigh(order, inputs, gains, dq, dk, dv):
    length, width = inputs.shape
    outs = [shape_of((width // 2, 3 * width), bf16)] * 2
    return call(
        weigh_kernel,
        "weigh",
        (3,),
        [order, inputs, gains, dq, dk, dv],
        [SMEM, whole((length, width)), whole(gains.shape)] + [whole((length, width))] * 3,
        outs,
        [pl.BlockSpec((width // 2, width), lambda i: (0, i))] * 2,
        [pltpu.VMEM((width, length), bf16), pltpu.VMEM((width, length), bf16)],
        limit=56,
        flops=2 * length * width * 3 * width,
    )


def finish_kernel(inputs_ref, gain_ref, dq_ref, dk_ref, dv_ref, grad_hidden_ref, weight_ref, grad_ref):
    width = inputs_ref.shape[1]
    xhat, inverse = normalized(inputs_ref[...].astype(f32))
    grad = 0.0
    for k, ref in enumerate((dq_ref, dk_ref, dv_ref)):
        grad = grad + dot_nt(ref[...], weight_ref[:, k * width : (k + 1) * width])
    gain = gain_ref[0:1, :].astype(f32)
    grad_ref[...] = grad_hidden_ref[...] + norm_back(xhat, inverse, gain, grad)


def finish(inputs, gains, dq, dk, dv, grad_hidden, dense):
    length, width = inputs.shape
    row = pl.BlockSpec((BLOCK, width), lambda i: (i, 0))
    return call(
        finish_kernel,
        "finish",
        (length // BLOCK,),
        [inputs, gains, dq, dk, dv, grad_hidden, dense],
        [
            row,
            whole(gains.shape),
            row,
            row,
            row,
            row,
            pl.BlockSpec((width, 3 * width), lambda i: (0, 0)),
        ],
        [shape_of((length, width), f32)],
        [row],
        limit=56,
        flops=2 * length * width * 3 * width,
    )[0]


def wide_slices(refs):
    edges = [sum(r.shape[1] for r in refs[:i]) for i in range(len(refs) + 1)]
    return [slice(a, b) for a, b in zip(edges, edges[1:])]


def end_kernel(count, *refs):
    own, got, (top, bottom) = refs[:count], refs[count : 2 * count], refs[2 * count :]
    half = top.shape[0]
    for one, other, cols in zip(own, got, wide_slices(own)):
        both = one[...].astype(f32) + other[...].astype(f32)
        top[:, cols] = both[:half].astype(bf16)
        bottom[:, cols] = both[half:].astype(bf16)


def middle_sums_kernel(count, *refs):
    own, got = refs[: 2 * count], refs[2 * count : 4 * count]
    top, bottom, to_low, to_high = refs[4 * count :]
    half = top.shape[0]
    for k, cols in enumerate(wide_slices(own[:count])):
        both = own[k][...].astype(f32) + got[k][...].astype(f32)
        to_low[:half, cols] = both[:half].astype(bf16)
        to_low[half:, cols] = (both[half:] + bottom[:, cols].astype(f32)).astype(bf16)
        both = own[count + k][...].astype(f32) + got[count + k][...].astype(f32)
        to_high[:half, cols] = (both[:half] + top[:, cols].astype(f32)).astype(bf16)
        to_high[half:, cols] = both[half:].astype(bf16)


def line_sums_kernel(count, narrow, place_ref, *refs):
    own, got = refs[:count], refs[count : 2 * count]
    low, high, mine, *sums, whole_ref = refs[2 * count :]
    rows = mine.shape[0]
    for one, other, cols in zip(own, got, wide_slices(own)):
        whole_ref[:, cols] = (
            one[...].astype(f32)
            + other[...].astype(f32)
            + low[:, cols].astype(f32)
            + high[:, cols].astype(f32)
        )
    for by, ref in enumerate([mine] + sums):
        number = lax.rem(place_ref[0] + by, narrow)
        if rows % 8 == 0:
            start = pl.multiple_of(number * rows, 8)
            ref[...] = whole_ref[pl.ds(start, rows), :].astype(ref.dtype)
        else:
            for other in range(narrow):

                @pl.when(number == other)
                def _(ref=ref, at=other * rows):
                    ref[...] = whole_ref[at : at + rows, :].astype(ref.dtype)


def blocks_at(arrays, number):
    return [pl.BlockSpec((a.shape[0] // 4, a.shape[1]), lambda *_: (number, 0)) for a in arrays]


def halves_kernel(low, high, top, bottom):
    top[...] = low[...]
    bottom[...] = high[...]


def halves(low, high):
    half, columns = low.shape[0] // 2, low.shape[1]
    if half % 8:
        return [low[:half], high[half:]]
    outs = [shape_of((half, columns), bf16)] * 2
    return call(
        halves_kernel,
        "halves",
        (1,),
        [low, high],
        [
            pl.BlockSpec((half, columns), lambda *_: (0, 0)),
            pl.BlockSpec((half, columns), lambda *_: (1, 0)),
        ],
        outs,
        [whole(o.shape) for o in outs],
    )


def end_sums(own, got):
    count, columns = len(own), sum(a.shape[1] for a in own)
    outs = [shape_of((own[0].shape[0] // 8, columns), bf16)] * 2
    return call(
        functools.partial(end_kernel, count),
        "end_sums",
        (1,),
        own + got,
        blocks_at(own + got, 3),
        outs,
        [whole(o.shape) for o in outs],
    )


def middle_sums(own, got, ends):
    count, columns = len(own), sum(a.shape[1] for a in own)
    outs = [shape_of((own[0].shape[0] // 4, columns), bf16)] * 2
    return call(
        functools.partial(middle_sums_kernel, count),
        "middle_sums",
        (1,),
        own + own + got + got + ends,
        blocks_at(own, 1) + blocks_at(own, 2) + blocks_at(got, 1) + blocks_at(got, 2)
        + [whole(e.shape) for e in ends],
        outs,
        [whole(o.shape) for o in outs],
    )


def line_sums(place, narrow, own, got, sides):
    count, columns = len(own), sum(a.shape[1] for a in own)
    height = own[0].shape[0] // 4
    outs = [shape_of((height // narrow, columns), f32)]
    outs = outs + [shape_of((height // narrow, columns), bf16)] * (narrow - 1)
    made = call(
        functools.partial(line_sums_kernel, count, narrow),
        "line_sums",
        (1,),
        [place] + own + got + sides,
        [SMEM] + blocks_at(own + got, 0) + [whole(s.shape) for s in sides],
        outs,
        [whole(o.shape) for o in outs],
        [pltpu.VMEM((height, columns), f32)],
    )
    return made[0], made[1:]


AXES = ("outer", "core", "narrow")


class Links:
    def __init__(self, wide, narrow):
        self.wide, self.narrow = wide, narrow
        self.bits = [1 << b for b in range((wide // 2).bit_length() - 1)]
        self.outer, self.core, self.place = (lax.axis_index(axis) for axis in AXES)

    def send(self, part, to):
        pairs = []
        for wide in range(self.wide):
            for narrow in range(self.narrow):
                outer, core, place = to(wide // 2, wide % 2, narrow)
                target = (outer * 2 + core) * self.narrow + place
                pairs.append((wide * self.narrow + narrow, target))
        return lax.ppermute(part, AXES, pairs)

    def flip(self, part, mask):
        return self.send(part, lambda o, c, z: (o ^ mask, c, z))

    def swap(self, part):
        return self.send(part, lambda o, c, z: (o, 1 - c, z))

    def shift(self, part, by):
        return self.send(part, lambda o, c, z: (o, c, (z + by) % self.narrow))


def after(values, *deps):
    flat, tree = jax.tree.flatten(values)
    more = jax.tree.leaves(deps)
    held = lax.optimization_barrier(tuple(flat) + tuple(more))
    return jax.tree.unflatten(tree, held[: len(flat)])


def together(always, step):
    shapes = jax.eval_shape(step)
    return lax.cond(
        always, step, lambda: jax.tree.map(lambda s: jnp.zeros(s.shape, s.dtype), shapes)
    )


class Gather:
    def __init__(self, links, part):
        self.links, self.part = links, part

    def send_along(self, which=None):
        which = range(1, self.links.narrow) if which is None else which
        return [self.links.shift(self.part, -by) for by in which]

    def take_along(self, got):
        links, rows = self.links, self.part.shape[0]
        full = jnp.zeros((links.narrow * rows, self.part.shape[1]), self.part.dtype)
        for by, part in enumerate([self.part] + got):
            start = (links.place + by) % links.narrow * rows
            full = lax.dynamic_update_slice_in_dim(full, part, start, 0)
        self.full = full

    def send_first(self):
        links, full = self.links, self.full
        return [links.flip(full, bit) for bit in links.bits[:2]] + [links.swap(full)]

    def take_first(self, got):
        self.low, self.high, self.full_over = got
        self.sent = halves(self.low, self.high)

    def send_second(self):
        links = self.links
        low, high = links.bits[0], links.bits[1]
        ends = [links.flip(self.sent[0], high), links.flip(self.sent[1], low)]
        return ends + [links.swap(self.low), links.swap(self.high)]

    def take_second(self, got):
        self.ends, self.over = got[:2], got[2:]

    def send_third(self):
        return [self.links.swap(e) for e in self.ends]

    def take_third(self, got):
        links = self.links
        own = [self.full, self.low, self.high] + self.ends
        over = [self.full_over] + self.over + got
        for bit in links.bits[2:]:
            own = own + [links.flip(p, bit) for p in own]
            over = over + [links.flip(p, bit) for p in over]
        self.pieces = [(p, p.shape[0], 0) for p in own + over]


class PlaneFirst:
    def __init__(self, links, part):
        self.links, self.part = links, part

    def send_first(self):
        return [self.links.flip(self.part, bit) for bit in self.links.bits[:2]]

    def take_first(self, got):
        self.low, self.high = got
        half = self.part.shape[0] // 2
        self.sent = [self.low[:half], self.high[half:]]

    def send_second(self):
        low, high = self.links.bits[0], self.links.bits[1]
        return [self.links.flip(self.sent[0], high), self.links.flip(self.sent[1], low)]

    def take_second(self, got):
        self.end = jnp.concatenate(got)

    def take_lines(self, own):
        for bit in self.links.bits[2:]:
            own = own + [self.links.flip(p, bit) for p in own]
        self.own = own

    def send_over(self, which):
        return [self.links.swap(self.own[number]) for number in which]

    def take_over(self, got):
        self.pieces = [(p, p.shape[0], 0) for p in self.own + got]


def piece_rows(links, own_rows):
    height = links.narrow * own_rows
    low, high = links.bits[0], links.bits[1]
    marks = [(0, 0), (low, 0), (high, 0), (low | high, 0), (low | high, height // 2)]
    for bit in links.bits[2:]:
        marks = marks + [(mask | bit, extra) for mask, extra in marks]
    return jnp.stack(
        [
            ((links.outer ^ mask) * 2 + (links.core ^ over)) * height + extra
            for over in range(2)
            for mask, extra in marks
        ]
    ).astype(i32)


def part_rows(links, own_rows):
    height = links.narrow * own_rows
    return jnp.stack(
        [
            ((links.outer ^ mask) * 2 + (links.core ^ over)) * height
            for over in range(2)
            for mask in range(links.wide // 2)
        ]
    ).astype(i32)


def total(*terms):
    out = terms[0].astype(f32)
    for term in terms[1:]:
        out = out + term.astype(f32)
    return out


class Scatter:
    def __init__(self, links, own, other):
        self.links, self.own, self.other = links, own, other

    def send_over(self):
        return [self.links.swap(part) for part in self.other]

    def take_over(self, got):
        links, own = self.links, self.own
        for bit in links.bits[:1:-1]:
            height = own[0].shape[0] // 2
            sums = [total(a, b).astype(bf16) for a, b in zip(own, got)]
            own = [s[:height] for s in sums]
            got = [links.flip(s[height:], bit) for s in sums]
        self.near, self.got = own, got

    def end(self):
        return end_sums(self.near, self.got)

    def send_first(self):
        low, high = self.links.bits[0], self.links.bits[1]
        return [self.links.flip(self.sums[0], low), self.links.flip(self.sums[1], high)]

    def take_first(self, got):
        self.sums = middle_sums(self.near, self.got, list(got))

    def send_second(self):
        low, high = self.links.bits[0], self.links.bits[1]
        return [self.links.flip(self.sums[0], low), self.links.flip(self.sums[1], high)]

    def take_second(self, got):
        links = self.links
        place = links.place.astype(i32).reshape(1)
        self.mine, self.sums = line_sums(place, links.narrow, self.near, self.got, list(got))

    def send_along(self, which=None):
        which = range(1, self.links.narrow) if which is None else which
        return [self.links.shift(self.sums[by - 1], by) for by in which]

    def take_along(self, got):
        self.result = total(self.mine, *got)


def on_device(
    wide, narrow, inputs, segment_ids, routes, attention_gain, qkv_weight, output_weight,
    mixture_gain, router_train, router_frozen, expert_in, expert_out, frozen_in, frozen_out,
    cotangent,
):
    links = Links(wide, narrow)
    length, width = inputs.shape
    own_rows = qkv_weight.shape[0]
    train_count = expert_in.shape[1]
    experts = train_count + frozen_in.shape[1]
    groups = expert_in.shape[2] // width
    docs = segment_ids[0]
    small = jnp.concatenate(
        [attention_gain[:, None], mixture_gain[:, None], router_train, router_frozen], axis=1
    )
    small = jnp.pad(small, ((0, 0), (0, LANES - small.shape[1])))
    dense = Gather(links, jnp.concatenate([qkv_weight, output_weight, small], axis=1))
    rows, order = piece_rows(links, own_rows), part_rows(links, own_rows)

    def packed(inner, outer):
        inner = inner.reshape(own_rows, width, groups).transpose(0, 2, 1).reshape(own_rows, -1)
        return jnp.concatenate([inner, outer.reshape(own_rows, -1)], axis=1)

    def part_of(e):
        if e < train_count:
            return packed(expert_in[:, e], expert_out[:, e])
        return packed(frozen_in[:, e - train_count], frozen_out[:, e - train_count])

    last = experts - 1
    weights = [Gather(links, part_of(e)) for e in range(last)] + [PlaneFirst(links, part_of(last))]
    always = segment_ids[0, 0] >= 0
    chosen = (routes[:, :, None] == jnp.arange(experts, dtype=i32)).astype(i32)
    per_block = jnp.sum(chosen.reshape(length // BLOCK, 2 * BLOCK, experts), axis=1)
    counts = jnp.concatenate([jnp.zeros((1, experts), i32), jnp.cumsum(per_block, axis=0)])
    counts = counts.reshape(-1)
    place, place_t = route_places(routes)

    def pick(expert, normed, gates):
        return dispatch(
            expert, experts, expert < train_count, order, counts, place_t, gates, normed, cotangent
        )

    def run(expert, picked):
        return expert_pass(
            expert, length // BLOCK * experts + expert, expert < train_count,
            order if expert == last else rows, order, counts, picked, weights[expert].pieces,
        )

    shifts = list(range(1, narrow))

    def line(part, *deps):
        part = after(part, *deps) if deps else part
        return lax.all_gather(part, "narrow", axis=0, tiled=True)

    w0, w1, w2, w3 = weights
    w0.part = after(w0.part, dense.part)
    w0.full = line(w0.part)
    dense.take_along(dense.send_along())
    w1.full = line(w1.part, dense.full)
    dense.take_first(together(always, dense.send_first))
    w2.full = line(w2.part, dense.low)
    dense.take_second(together(always, dense.send_second))
    dense.take_third(dense.send_third())

    def step():
        qkv, full, gains = project(rows, inputs, dense.pieces)
        attended, logs = attend(docs, qkv)
        return w0.send_first(), w3.send_first(), (qkv, full, gains, attended, logs)

    got, ahead, (qkv, dense, gains, attended, logs) = together(always, step)
    w0.take_first(got)
    w3.take_first(ahead)
    w3.own = [line(shard, qkv) for shard in (w3.part, w3.low, w3.high)]
    def step():
        made = middle(inputs, attended, place, dense)
        return w0.send_second(), made, pick(0, *made[1:])

    got, (hidden, normed, gates), picked = together(always, step)
    w0.take_second(got)
    w0.take_third(w0.send_third())
    got, ahead, one = together(
        always, lambda: (w1.send_first(), w3.send_second(), run(0, picked))
    )
    w1.take_first(got)
    w3.take_second(ahead)
    got, picked = together(
        always,
        lambda: (w1.send_second(), [pick(e, normed, gates) for e in range(1, experts)]),
    )
    w1.take_second(got)
    w1.take_third(w1.send_third())
    end = line(w3.end, w1.ends)
    term0 = Scatter(links, [one[2], one[4]], [one[3], one[5]])
    w2.full = after(w2.full, one[0])
    got, more, two = together(
        always, lambda: (w2.send_first(), term0.send_over(), run(1, picked[0]))
    )
    w2.take_first(got)

    term0.take_over(more)
    got, ahead, term0.sums = together(
        always, lambda: (w2.send_second(), w3.send_over([0]), term0.end())
    )
    w2.take_second(got)
    w2.take_third(w2.send_third())
    w3.take_lines(w3.own + [end])
    term1 = Scatter(links, [two[2], two[4]], [two[3], two[5]])
    count = len(w3.own)
    got, more, three = together(
        always, lambda: (w3.send_over(range(1, count)), term1.send_over(), run(2, picked[1]))
    )
    w3.take_over(ahead + got)
    term1.take_over(more)
    term1.sums = term1.end()
    got, more, four = together(
        always, lambda: (term0.send_first(), term1.send_first(), run(3, picked[2]))
    )
    term0.take_first(got)
    results, backs = [[m[i] for m in (one, two, three, four)] for i in range(2)]

    def step():
        made = combine(
            experts, order, counts, place, gates, hidden, normed, cotangent, attended, dense,
            results, backs,
        )
        term1.take_first(more)
        return term0.send_second(), term1.sums, made

    got, term1.sums, (block_output, grad_hidden, grad_heads, *made) = together(always, step)
    term0.take_second(got)
    out_term = Scatter(links, *[[m] for m in made])
    got, more, (dq, dk, dv) = together(
        always,
        lambda: (
            term1.send_second(), term0.send_along(), attend_back(docs, qkv, grad_heads, logs)
        ),
    )
    term1.take_second(got)
    over, one, made = together(
        always,
        lambda: (
            out_term.send_over(), term1.send_along(shifts[:1]),
            weigh(order, inputs, gains, dq, dk, dv),
        ),
    )
    out_term.take_over(over)
    out_term.sums = out_term.end()
    qkv_term = Scatter(links, *[[m] for m in made])
    over, got, last, input_grad = together(
        always,
        lambda: (
            qkv_term.send_over(), out_term.send_first(), term1.send_along(shifts[2:]),
            finish(inputs, gains, dq, dk, dv, grad_hidden, dense),
        ),
    )
    qkv_term.take_over(over)
    qkv_term.sums = qkv_term.end()
    out_term.take_first(got)

    def unpacked(parts):
        full = total(*parts)
        inner = groups * width
        inner, outer = full[:, :inner], full[:, inner:]
        inner = inner.reshape(own_rows, groups, width).transpose(0, 2, 1).reshape(own_rows, -1)
        return inner, outer.reshape(own_rows * groups, width)

    got, two, middle_part, first = together(
        always,
        lambda: (
            qkv_term.send_first(), out_term.send_second(), term1.send_along(shifts[1:2]),
            unpacked([term0.mine] + more),
        ),
    )
    qkv_term.take_first(got)
    out_term.take_second(two)

    def step():
        second = unpacked([term1.mine] + one + middle_part + last)
        in_grad, down_grad = [jnp.stack(pair, axis=1) for pair in zip(first, second)]
        return qkv_term.send_second(), out_term.send_along(), in_grad, down_grad

    got, two, in_grad, down_grad = together(always, step)
    qkv_term.take_second(got)

    def step():
        out_term.take_along(two)
        out = out_term.result
        return qkv_term.send_along(), (
            out[:, :width], out[:, width + LANES - 1], out[:, width : width + train_count]
        )

    got, outs = together(always, step)
    qkv_term.take_along(got)
    qkv_grad = qkv_term.result
    gain_grad = jnp.sum(qkv_weight.astype(f32) * qkv_grad, axis=1) / attention_gain.astype(f32)
    return (
        block_output,
        input_grad,
        gain_grad,
        qkv_grad,
        *outs,
        in_grad,
        down_grad,
    )


def solution(mesh):
    wide, narrow = mesh.shape["wide"], mesh.shape["narrow"]
    mesh = Mesh(mesh.devices.reshape(wide // 2, 2, narrow), AXES)
    rows = P(AXES)
    return jax.shard_map(
        functools.partial(on_device, wide, narrow),
        mesh=mesh,
        in_specs=(rows,) * 14,
        out_specs=(rows,) * 9,
        check_vma=False,
    )
```

```python
import functools

import jax
import jax.numpy as jnp
from jax import lax
from jax.experimental import pallas as pl
from jax.experimental.pallas import tpu as pltpu
from jax.sharding import Mesh, PartitionSpec as P

HEAD_DIM = 64
PAIR = 2 * HEAD_DIM
CAP = 768
MAX_DOC = 512
BLOCK = 256
WINDOW = BLOCK + 128
ROW_TILE = 256
LANES = 128
EPS = 1e-05
bf16, f32, i32 = jnp.bfloat16, jnp.float32, jnp.int32


def dot_nn(a, b):
    return lax.dot_general(a, b, (((1,), (0,)), ((), ())), preferred_element_type=f32)


def dot_nt(a, b):
    return lax.dot_general(a, b, (((1,), (1,)), ((), ())), preferred_element_type=f32)


def dot_tn(a, b):
    return lax.dot_general(a, b, (((0,), (0,)), ((), ())), preferred_element_type=f32)


def iota(shape, dim):
    return lax.broadcasted_iota(i32, shape, dim)


def flag(mask, dtype=bf16):
    return jnp.where(mask, 1.0, 0.0).astype(dtype)


def normalized(values):
    center = values - jnp.mean(values, axis=-1, keepdims=True)
    spread = jnp.mean(center * center, axis=-1, keepdims=True)
    inverse = lax.rsqrt(spread + EPS)
    return center * inverse, inverse


def norm_back(xhat, inverse, gain, grad):
    scaled = grad * gain
    return inverse * (
        scaled
        - jnp.mean(scaled, axis=-1, keepdims=True)
        - xhat * jnp.mean(scaled * xhat, axis=-1, keepdims=True)
    )


def params(limit_mib, **kw):
    return pltpu.CompilerParams(vmem_limit_bytes=limit_mib << 20, **kw)


def whole(shape):
    return pl.BlockSpec(shape, lambda *_: (0,) * len(shape))


def call(kernel, name, grid, ins, in_specs, outs, out_specs, scratch=(), limit=48, flops=0):
    size = sum(a.size * a.dtype.itemsize for a in ins) + sum(
        o.size * o.dtype.itemsize for o in outs
    )
    return pl.pallas_call(
        kernel,
        name=name,
        grid=grid,
        in_specs=in_specs,
        out_specs=out_specs,
        out_shape=outs,
        scratch_shapes=list(scratch),
        compiler_params=params(limit),
        cost_estimate=pl.CostEstimate(flops=flops, bytes_accessed=size, transcendentals=0),
    )(*ins)


def shape_of(shape, dtype):
    return jax.ShapeDtypeStruct(shape, dtype)


def gathered_specs(pieces, columns, index):
    return [
        pl.BlockSpec((height, columns), lambda *i, at=at: (at, index(*i)))
        for _, height, at in pieces
    ]


def put_together(rows_ref, piece_refs, whole_ref):
    for number, piece in enumerate(piece_refs):
        height = piece.shape[0]
        start = pl.multiple_of(rows_ref[number], 16 if height % 16 == 0 else 8)
        whole_ref[pl.ds(start, height), :] = piece[...]


def lay_out(order_ref, staged_ref, own_ref, other_ref):
    parts = order_ref.shape[0] // 2
    height = own_ref.shape[0] // parts
    for half, ref in enumerate((own_ref, other_ref)):
        for part in range(parts):
            start = order_ref[half * parts + part]
            start = pl.multiple_of(start, 16 if height % 16 == 0 else 8)
            ref[part * height : (part + 1) * height, :] = staged_ref[pl.ds(start, height), :]


SMEM = pl.BlockSpec(memory_space=pltpu.SMEM)


def route_kernel(routes_ref, routes_t_ref, place_ref, place_t_ref):
    length = routes_ref.shape[0]
    lane = iota((length, LANES), 1)
    mask = (lane == routes_ref[:, 0:1]) | (lane == routes_ref[:, 1:2])
    before = flag(iota((length, length), 1) < iota((length, length), 0))
    place_ref[...] = jnp.where(mask, dot_nn(before, flag(mask)), -1.0).astype(i32)
    sub = iota((8, length), 0)
    mask_t = (sub == routes_t_ref[0:1, :]) | (sub == routes_t_ref[1:2, :])
    before_t = flag(iota((length, length), 0) < iota((length, length), 1))
    place_t_ref[...] = jnp.where(mask_t, dot_nn(flag(mask_t), before_t), -1.0).astype(i32)


def route_places(routes):
    length = routes.shape[0]
    outs = [shape_of((length, LANES), i32), shape_of((8, length), i32)]
    return call(
        route_kernel,
        "places",
        (),
        [routes, routes.T],
        [whole((length, 2)), whole((2, length))],
        outs,
        [whole(o.shape) for o in outs],
    )


def gains_of(small_ref):
    return small_ref[...].astype(f32).T


def project_kernel(count, rows_ref, inputs_ref, *rest):
    pieces, (qkv_ref, dense_ref, rows_out_ref, gains_ref) = rest[:count], rest[count:]
    width = inputs_ref.shape[1]

    @pl.when(pl.program_id(0) == 0)
    def _():
        put_together(rows_ref, pieces, dense_ref)
        gains_ref[...] = dense_ref[:, 4 * width :].astype(f32).T
        rows_out_ref[...] = gains_ref[:16, :].astype(bf16)

    xhat, _ = normalized(inputs_ref[...].astype(f32))
    normed = (gains_ref[0:1, :] * xhat).astype(bf16)
    qkv_ref[...] = dot_nn(normed, dense_ref[:, : 3 * width]).astype(bf16)


def project(rows, inputs, pieces):
    length, width = inputs.shape
    columns = pieces[0][0].shape[1]
    return call(
        functools.partial(project_kernel, len(pieces)),
        "project",
        (length // BLOCK,),
        [rows, inputs] + [p[0] for p in pieces],
        [SMEM, pl.BlockSpec((BLOCK, width), lambda i: (i, 0))]
        + gathered_specs(pieces, columns, lambda i: 0),
        [
            shape_of((length, 3 * width), bf16),
            shape_of((width, columns), bf16),
            shape_of((16, width), bf16),
        ],
        [
            pl.BlockSpec((BLOCK, 3 * width), lambda i: (i, 0)),
            whole((width, columns)),
            whole((16, width)),
        ],
        [pltpu.VMEM((LANES, width), f32)],
        flops=2 * length * width * 3 * width,
    )


def span_of(block):
    reach = MAX_DOC // BLOCK
    start = max(0, block - reach) * BLOCK
    return start, (block + 1) * BLOCK - start


def attend_kernel(doc_ref, doc_t_ref, q_ref, k_ref, v_ref, out_ref, log_ref, bias_ref):
    length = q_ref.shape[0]
    blocks = length // BLOCK

    @pl.when(pl.program_id(0) == 0)
    def _():
        for block in range(blocks):
            start, size = span_of(block)
            rows = slice(block * BLOCK, (block + 1) * BLOCK)
            row = iota((BLOCK, size), 0) + block * BLOCK
            col = iota((BLOCK, size), 1) + start
            kept = (row >= col) & (doc_ref[rows, :] == doc_t_ref[:, start : start + size])
            bias_ref[rows, :size] = jnp.where(kept, 0.0, -1e30)

    first = iota((BLOCK, PAIR), 1) < HEAD_DIM
    for block in range(blocks):
        start, size = span_of(block)
        rows = slice(block * BLOCK, (block + 1) * BLOCK)
        query = q_ref[rows, :] * 0.125
        keys, values = k_ref[start : start + size, :], v_ref[start : start + size, :]
        bias = bias_ref[rows, :size]
        parts, logs = [], []
        for own in (first, ~first):
            scores = dot_nt(jnp.where(own, query, 0).astype(bf16), keys) + bias
            peak = jnp.max(scores, axis=-1, keepdims=True)
            raised = jnp.exp(scores - peak)
            total = jnp.sum(raised, axis=-1, keepdims=True)
            parts.append(dot_nn(raised.astype(bf16), values) * (1.0 / total))
            logs.append(peak + jnp.log(total))
        out_ref[rows, :] = jnp.where(first, parts[0], parts[1]).astype(bf16)
        turned = jnp.where(first, logs[0], logs[1]).T
        log_ref[0, 0:1, rows] = turned[0:1, :]
        log_ref[0, 1:2, rows] = turned[HEAD_DIM : HEAD_DIM + 1, :]


def attend(docs, qkv):
    length, width = qkv.shape[0], qkv.shape[1] // 3
    pairs = width // PAIR
    heads = [pl.BlockSpec((length, PAIR), lambda i, k=k: (0, k * pairs + i)) for k in range(3)]
    return call(
        attend_kernel,
        "attend",
        (pairs,),
        [docs.reshape(length, 1), docs.reshape(1, length), qkv, qkv, qkv],
        [whole((length, 1)), whole((1, length))] + heads,
        [shape_of((length, width), bf16), shape_of((pairs, 8, length), f32)],
        [
            pl.BlockSpec((length, PAIR), lambda i: (0, i)),
            pl.BlockSpec((1, 8, length), lambda i: (i, 0, 0)),
        ],
        [pltpu.VMEM((length, MAX_DOC + BLOCK), f32)],
        flops=4 * length * 768 * width,
    )


def attend_back_kernel(
    doc_ref, doc_t_ref, q_ref, k_ref, v_ref, grad_ref, out_ref, log_ref, dq_ref, dk_ref, dv_ref,
    bias_ref, dk_sum, dv_sum,
):
    length = q_ref.shape[0]
    blocks = length // BLOCK

    @pl.when(pl.program_id(0) == 0)
    def _():
        for block in range(blocks):
            start, size = span_of(block)
            cols = slice(block * BLOCK, (block + 1) * BLOCK)
            row = iota((size, BLOCK), 0) + start
            col = iota((size, BLOCK), 1) + block * BLOCK
            kept = (col >= row) & (doc_ref[start : start + size, :] == doc_t_ref[:, cols])
            bias_ref[:size, cols] = jnp.where(kept, 0.0, -1e30)

    turned_keys = k_ref[...].T
    dk_sum[...] = jnp.zeros_like(dk_sum)
    dv_sum[...] = jnp.zeros_like(dv_sum)
    first = iota((BLOCK, PAIR), 1) < HEAD_DIM
    for block in range(blocks):
        start, size = span_of(block)
        rows, span = slice(block * BLOCK, (block + 1) * BLOCK), slice(start, start + size)
        query, grad = q_ref[rows, :] * 0.125, grad_ref[rows, :]
        keys, values = k_ref[span, :], v_ref[span, :]
        bias = bias_ref[:size, rows]
        turned = (grad.astype(f32) * out_ref[rows, :].astype(f32)).T
        parts, dk, dv = [], 0.0, 0.0
        for head, own in enumerate((first, ~first)):
            own_query = jnp.where(own, query, 0).astype(bf16)
            own_grad = jnp.where(own, grad, 0).astype(bf16)
            scores = dot_nt(keys, own_query) + bias
            probs = jnp.exp(scores - log_ref[0, head : head + 1, rows])
            dv = dv + dot_nn(probs.astype(bf16), own_grad)
            lanes = slice(head * HEAD_DIM, (head + 1) * HEAD_DIM)
            mean = jnp.sum(turned[lanes, :], axis=0, keepdims=True)
            grad_scores = (probs * (dot_nt(values, own_grad) - mean)).astype(bf16)
            dk = dk + dot_nn(grad_scores, own_query)
            parts.append(dot_nn(turned_keys[lanes, span], grad_scores))
        dq_ref[rows, :] = (jnp.concatenate(parts).T * 0.125).astype(bf16)
        dk_sum[span, :] += dk
        dv_sum[span, :] += dv
    dk_ref[...] = dk_sum[...].astype(bf16)
    dv_ref[...] = dv_sum[...].astype(bf16)


def attend_back(docs, qkv, grad, attended, logs):
    length, width = qkv.shape[0], qkv.shape[1] // 3
    pairs = width // PAIR
    heads = [pl.BlockSpec((length, PAIR), lambda i, k=k: (0, k * pairs + i)) for k in range(3)]
    one = pl.BlockSpec((length, PAIR), lambda i: (0, i))
    return call(
        attend_back_kernel,
        "attend_back",
        (pairs,),
        [docs.reshape(length, 1), docs.reshape(1, length), qkv, qkv, qkv, grad, attended, logs],
        [whole((length, 1)), whole((1, length))]
        + heads
        + [one, one, pl.BlockSpec((1, 8, length), lambda i: (i, 0, 0))],
        [shape_of((length, width), bf16)] * 3,
        [one] * 3,
        [
            pltpu.VMEM((MAX_DOC + BLOCK, length), f32),
            pltpu.VMEM((length, PAIR), f32),
            pltpu.VMEM((length, PAIR), f32),
        ],
        flops=10 * length * 768 * width,
    )


def middle_kernel(
    inputs_ref, attended_ref, place_ref, weight_ref, small_ref, hidden_ref, normed_ref, gate_ref,
    gains_ref,
):
    @pl.when(pl.program_id(0) == 0)
    def _():
        gains_ref[...] = gains_of(small_ref)

    hidden = inputs_ref[...].astype(f32) + dot_nn(attended_ref[...], weight_ref[...])
    hidden_ref[...] = hidden
    xhat, _ = normalized(hidden)
    normed = (gains_ref[1:2, :] * xhat).astype(bf16)
    normed_ref[...] = normed
    logits = dot_nn(normed, small_ref[...])
    mask = place_ref[...] >= 0
    logits = jnp.where(mask, pltpu.roll(logits, LANES - 2, 1), -1e30)
    peak = jnp.max(logits, axis=-1, keepdims=True)
    raised = jnp.where(mask, jnp.exp(logits - peak), 0.0)
    gate_ref[...] = raised / jnp.sum(raised, axis=-1, keepdims=True)


def middle(inputs, attended, place, dense):
    length, width = inputs.shape
    row = pl.BlockSpec((BLOCK, width), lambda i: (i, 0))
    thin = pl.BlockSpec((BLOCK, LANES), lambda i: (i, 0))
    return call(
        middle_kernel,
        "middle",
        (length // BLOCK,),
        [inputs, attended, place, dense, dense],
        [
            row,
            row,
            thin,
            pl.BlockSpec((width, width), lambda i: (0, 3)),
            pl.BlockSpec((width, LANES), lambda i: (0, 4 * width // LANES)),
        ],
        [
            shape_of((length, width), f32),
            shape_of((length, width), bf16),
            shape_of((length, LANES), f32),
        ],
        [row, row, thin],
        [pltpu.VMEM((LANES, width), f32)],
        flops=2 * length * width * width,
    )


def window_base(counts_ref, block, expert, experts):
    base = counts_ref[block * experts + expert]
    return pl.multiple_of(jnp.minimum(base // 128 * 128, CAP - WINDOW), 128)


def dispatch_kernel(
    expert, experts, order_ref, counts_ref, place_t_ref, gate_ref, normed_ref, cot_ref, x_ref, g_ref,
    *rest,
):
    length = normed_ref.shape[0]
    x_ref[...] = jnp.zeros_like(x_ref)
    g_ref[...] = jnp.zeros_like(g_ref)
    for block in range(length // BLOCK):
        base = window_base(counts_ref, block, expert, experts)
        cols = slice(block * BLOCK, (block + 1) * BLOCK)
        pick = flag(iota((WINDOW, BLOCK), 0) + base == place_t_ref[expert : expert + 1, cols])
        window = pl.ds(base, WINDOW)
        x_ref[window, :] += dot_nn(pick, normed_ref[cols, :]).astype(bf16)
        scaled = gate_ref[cols, expert : expert + 1] * cot_ref[cols, :].astype(f32)
        g_ref[window, :] += dot_nn(pick, scaled.astype(bf16)).astype(bf16)
    if rest:
        turned_ref, staged = rest
        half = turned_ref.shape[0] // 2
        staged[...] = x_ref[...].T
        lay_out(order_ref, staged, turned_ref.at[:half], turned_ref.at[half:])


def dispatch(expert, experts, train, order, counts, place_t, gates, normed, cot):
    width = normed.shape[1]
    outs = [shape_of((CAP, width), bf16)] * 2
    outs = outs + ([shape_of((width, CAP), bf16)] if train else [])
    ins = [place_t, gates, normed, cot]
    return call(
        functools.partial(dispatch_kernel, expert, experts),
        "dispatch_%d" % expert,
        (1,),
        [order, counts] + ins,
        [SMEM, SMEM] + [whole(a.shape) for a in ins],
        outs,
        [whole(o.shape) for o in outs],
        [pltpu.VMEM((width, CAP), bf16)] if train else [],
        flops=4 * CAP * WINDOW * width,
    )


def expert_kernel(slot, train, count, rows_ref, order_ref, counts_ref, *rest):
    rows_x, rows_g, rest = rest[0], rest[1], rest[2:]
    if train:
        turned_x, rest = rest[0], rest[1:]
    in_pieces, out_pieces, rest = rest[:count], rest[count : 2 * count], rest[2 * count :]
    result_ref, back_ref, rest = rest[0], rest[1], rest[2:]
    if train:
        in_own, in_other, out_own, out_other = rest[:4]
        rest = rest[4:]
        acts, grads, staged = rest[4:]
    sum_r, sum_b, in_ref, out_ref = rest[:4]
    half = rows_x.shape[1] // 2
    step = pl.program_id(0)
    load = counts_ref[slot]

    @pl.when(step == 0)
    def _():
        sum_r[...] = jnp.zeros_like(sum_r)
        sum_b[...] = jnp.zeros_like(sum_b)

    put_together(rows_ref, in_pieces, in_ref)
    put_together(rows_ref, out_pieces, out_ref)

    def tile(index, carry):
        rows = pl.ds(pl.multiple_of(index * ROW_TILE, ROW_TILE), ROW_TILE)
        pre = dot_nn(rows_x[rows, :], in_ref[...])
        grad_rows = rows_g[rows, :]
        square = pre * pre
        bend = jnp.tanh(0.7978845608028654 * pre * (1.0 + 0.044715 * square))
        half = 0.5 + 0.5 * bend
        slope = half + pre * (0.5 - 0.5 * bend * bend) * (
            0.7978845608028654 + 0.1070322243 * square
        )
        act = (pre * half).astype(bf16)
        grad = (dot_nt(grad_rows, out_ref[...]) * slope).astype(bf16)
        sum_r[rows, :] += dot_nn(act, out_ref[...])
        sum_b[rows, :] += dot_nt(grad, in_ref[...])
        if train:
            acts[rows, :] = act
            grads[rows, :] = grad
        return carry

    tiles = jnp.maximum((load + ROW_TILE - 1) // ROW_TILE, 1)
    lax.fori_loop(0, tiles, tile, 0)
    if train:
        for amount in range(1, CAP // ROW_TILE + 1):

            @pl.when(tiles == amount)
            def _(used=amount * ROW_TILE):
                inner = dot_nn(turned_x[:, :used], grads[:used, :]).astype(bf16)
                in_own[...] = inner[:half]
                in_other[...] = inner[half:]
                staged[...] = dot_tn(acts[:used, :], rows_g[:used, :]).astype(bf16)

        lay_out(order_ref, staged, out_own, out_other)

    @pl.when(step == pl.num_programs(0) - 1)
    def _():
        result_ref[...] = sum_r[...].astype(bf16)
        back_ref[...] = sum_b[...].astype(bf16)


def expert_pass(expert, slot, train, rows, order, counts, picked, pieces):
    width = picked[0].shape[1]
    hidden = pieces[0][0].shape[1] // 2
    arrays = [p[0] for p in pieces]
    steps = hidden // width
    half = width // 2
    slab = pl.BlockSpec((half, width), lambda i: (0, i))
    outs = [shape_of((CAP, width), bf16)] * 2
    out_specs = [whole((CAP, width))] * 2
    scratch = [
        pltpu.VMEM((CAP, width), f32),
        pltpu.VMEM((CAP, width), f32),
        pltpu.VMEM((width, width), bf16),
        pltpu.VMEM((width, width), bf16),
    ]
    if train:
        outs = outs + [shape_of((half, hidden), bf16)] * 4
        out_specs = out_specs + [slab] * 4
        scratch = scratch + [
            pltpu.VMEM((CAP, width), bf16),
            pltpu.VMEM((CAP, width), bf16),
            pltpu.VMEM((width, width), bf16),
        ]
    return call(
        functools.partial(expert_kernel, slot, train, len(pieces)),
        "expert_%d" % expert,
        (steps,),
        [rows, order, counts] + list(picked) + arrays + arrays,
        [SMEM, SMEM, SMEM]
        + [whole(p.shape) for p in picked]
        + gathered_specs(pieces, width, lambda i: i)
        + gathered_specs(pieces, width, lambda i: i + steps),
        outs,
        out_specs,
        scratch,
        limit=56,
        flops=(12 if train else 8) * 600 * width * hidden,
    )


def combine_kernel(
    experts, order_ref, counts_ref, place_ref, gate_ref, hidden_ref, normed_ref, cot_ref, attended_ref,
    weight_ref, small_ref, *rest,
):
    result_refs, back_refs = rest[:experts], rest[experts : 2 * experts]
    (output_ref, grad_hidden_ref, grad_heads_ref, own_ref, other_ref,
     gains_ref, weight_sum, gain_sum, router_sum, staged) = rest[2 * experts :]
    step = pl.program_id(0)

    @pl.when(step == 0)
    def _():
        gains_ref[...] = gains_of(small_ref)
        weight_sum[...] = jnp.zeros_like(weight_sum)
        gain_sum[...] = jnp.zeros_like(gain_sum)
        router_sum[...] = jnp.zeros_like(router_sum)

    cot = cot_ref[...].astype(f32)
    hidden = hidden_ref[...]
    gates = gate_ref[...]
    lane = iota((BLOCK, LANES), 1)
    total, grad_normed = hidden, 0.0
    grad_gate = jnp.zeros((BLOCK, LANES), f32)
    for expert in range(experts):
        base = window_base(counts_ref, step, expert, experts)
        window = pl.ds(base, WINDOW)
        pick = flag(iota((BLOCK, WINDOW), 1) + base == place_ref[:, expert : expert + 1])
        picked = dot_nn(pick, result_refs[expert][window, :])
        total = total + gates[:, expert : expert + 1] * picked
        grad_gate = jnp.where(
            lane == expert, jnp.sum(cot * picked, axis=-1, keepdims=True), grad_gate
        )
        grad_normed = grad_normed + dot_nn(pick, back_refs[expert][window, :])
    output_ref[...] = total.astype(bf16)
    grad_logits = gates * (grad_gate - jnp.sum(gates * grad_gate, axis=-1, keepdims=True))
    high = grad_logits.astype(bf16)
    low = (grad_logits - high.astype(f32)).astype(bf16)
    gains = gains_ref[...]
    router = pltpu.roll(gains, LANES - 2, 0).astype(bf16)
    both = jnp.concatenate([high, low], axis=1)
    grad_normed = grad_normed + dot_nn(both, jnp.concatenate([router, router]))
    made = dot_tn(normed_ref[...], both)
    router_sum[...] += made[:, :LANES] + made[:, LANES:]
    xhat, inverse = normalized(hidden)
    gain_sum[...] += jnp.sum(grad_normed * xhat, axis=0, keepdims=True)
    grad_hidden = cot + norm_back(xhat, inverse, gains[1:2, :], grad_normed)
    grad_hidden_ref[...] = grad_hidden
    branch = grad_hidden.astype(bf16)
    grad_heads_ref[...] = dot_nt(branch, weight_ref[...]).astype(bf16)
    weight_sum[...] += dot_tn(attended_ref[...], branch)

    @pl.when(step == pl.num_programs(0) - 1)
    def _():
        width = weight_sum.shape[1]
        gain = jnp.broadcast_to(gain_sum[...], (LANES, width)).T
        small = jnp.where(iota((width, LANES), 1) == LANES - 1, gain, router_sum[...])
        staged[:, :width] = weight_sum[...].astype(bf16)
        staged[:, width:] = small.astype(bf16)
        lay_out(order_ref, staged, own_ref, other_ref)


def combine(
    experts, order, counts, place, gates, hidden, normed, cot, attended, dense, results, backs
):
    length, width = hidden.shape
    row = pl.BlockSpec((BLOCK, width), lambda i: (i, 0))
    thin = pl.BlockSpec((BLOCK, LANES), lambda i: (i, 0))
    term = (width // 2, width + LANES)
    return call(
        functools.partial(combine_kernel, experts),
        "combine",
        (length // BLOCK,),
        [order, counts, place, gates, hidden, normed, cot, attended, dense, dense]
        + results
        + backs,
        [
            SMEM,
            SMEM,
            thin,
            thin,
            row,
            row,
            row,
            row,
            pl.BlockSpec((width, width), lambda i: (0, 3)),
            pl.BlockSpec((width, LANES), lambda i: (0, 4 * width // LANES)),
        ]
        + [whole((CAP, width))] * (2 * experts),
        [
            shape_of((length, width), bf16),
            shape_of((length, width), f32),
            shape_of((length, width), bf16),
            shape_of(term, bf16),
            shape_of(term, bf16),
        ],
        [row, row, row, whole(term), whole(term)],
        [
            pltpu.VMEM((LANES, width), f32),
            pltpu.VMEM((width, width), f32),
            pltpu.VMEM((1, width), f32),
            pltpu.VMEM((width, LANES), f32),
            pltpu.VMEM((width, width + LANES), bf16),
        ],
        limit=56,
        flops=8 * length * width * width,
    )


def weigh_kernel(order_ref, inputs_ref, gain_ref, dq_ref, dk_ref, dv_ref, own_ref, other_ref, turned,
                 staged):
    half = inputs_ref.shape[1] // 2

    @pl.when(pl.program_id(0) == 0)
    def _():
        xhat, _ = normalized(inputs_ref[...].astype(f32))
        staged[...] = (gain_ref[0:1, :].astype(f32) * xhat).astype(bf16).T
        lay_out(order_ref, staged, turned.at[:half], turned.at[half:])

    for k, ref in enumerate((dq_ref, dk_ref, dv_ref)):

        @pl.when(pl.program_id(0) == k)
        def _(ref=ref):
            grad = dot_nn(turned[...], ref[...]).astype(bf16)
            own_ref[...] = grad[:half]
            other_ref[...] = grad[half:]


def weigh(order, inputs, gains, dq, dk, dv):
    length, width = inputs.shape
    outs = [shape_of((width // 2, 3 * width), bf16)] * 2
    return call(
        weigh_kernel,
        "weigh",
        (3,),
        [order, inputs, gains, dq, dk, dv],
        [SMEM, whole((length, width)), whole(gains.shape)] + [whole((length, width))] * 3,
        outs,
        [pl.BlockSpec((width // 2, width), lambda i: (0, i))] * 2,
        [pltpu.VMEM((width, length), bf16), pltpu.VMEM((width, length), bf16)],
        limit=56,
        flops=2 * length * width * 3 * width,
    )


def finish_kernel(inputs_ref, gain_ref, dq_ref, dk_ref, dv_ref, grad_hidden_ref, weight_ref, grad_ref):
    width = inputs_ref.shape[1]
    xhat, inverse = normalized(inputs_ref[...].astype(f32))
    grad = 0.0
    for k, ref in enumerate((dq_ref, dk_ref, dv_ref)):
        grad = grad + dot_nt(ref[...], weight_ref[:, k * width : (k + 1) * width])
    gain = gain_ref[0:1, :].astype(f32)
    grad_ref[...] = grad_hidden_ref[...] + norm_back(xhat, inverse, gain, grad)


def finish(inputs, gains, dq, dk, dv, grad_hidden, dense):
    length, width = inputs.shape
    row = pl.BlockSpec((BLOCK, width), lambda i: (i, 0))
    return call(
        finish_kernel,
        "finish",
        (length // BLOCK,),
        [inputs, gains, dq, dk, dv, grad_hidden, dense],
        [
            row,
            whole(gains.shape),
            row,
            row,
            row,
            row,
            pl.BlockSpec((width, 3 * width), lambda i: (0, 0)),
        ],
        [shape_of((length, width), f32)],
        [row],
        limit=56,
        flops=2 * length * width * 3 * width,
    )[0]


def wide_slices(refs):
    edges = [sum(r.shape[1] for r in refs[:i]) for i in range(len(refs) + 1)]
    return [slice(a, b) for a, b in zip(edges, edges[1:])]


def end_kernel(count, *refs):
    own, got, (top, bottom) = refs[:count], refs[count : 2 * count], refs[2 * count :]
    half = top.shape[0]
    for one, other, cols in zip(own, got, wide_slices(own)):
        both = one[...].astype(f32) + other[...].astype(f32)
        top[:, cols] = both[:half].astype(bf16)
        bottom[:, cols] = both[half:].astype(bf16)


def middle_sums_kernel(count, *refs):
    own, got = refs[: 2 * count], refs[2 * count : 4 * count]
    top, bottom, to_low, to_high = refs[4 * count :]
    half = top.shape[0]
    for k, cols in enumerate(wide_slices(own[:count])):
        both = own[k][...].astype(f32) + got[k][...].astype(f32)
        to_low[:half, cols] = both[:half].astype(bf16)
        to_low[half:, cols] = (both[half:] + bottom[:, cols].astype(f32)).astype(bf16)
        both = own[count + k][...].astype(f32) + got[count + k][...].astype(f32)
        to_high[:half, cols] = (both[:half] + top[:, cols].astype(f32)).astype(bf16)
        to_high[half:, cols] = both[half:].astype(bf16)


def line_sums_kernel(count, narrow, place_ref, *refs):
    own, got = refs[:count], refs[count : 2 * count]
    low, high, mine, *sums, whole_ref = refs[2 * count :]
    rows = mine.shape[0]
    for one, other, cols in zip(own, got, wide_slices(own)):
        whole_ref[:, cols] = (
            one[...].astype(f32)
            + other[...].astype(f32)
            + low[:, cols].astype(f32)
            + high[:, cols].astype(f32)
        )
    for by, ref in enumerate([mine] + sums):
        number = lax.rem(place_ref[0] + by, narrow)
        if rows % 8 == 0:
            start = pl.multiple_of(number * rows, 8)
            ref[...] = whole_ref[pl.ds(start, rows), :].astype(ref.dtype)
        else:
            for other in range(narrow):

                @pl.when(number == other)
                def _(ref=ref, at=other * rows):
                    ref[...] = whole_ref[at : at + rows, :].astype(ref.dtype)


def blocks_at(arrays, number):
    return [pl.BlockSpec((a.shape[0] // 4, a.shape[1]), lambda *_: (number, 0)) for a in arrays]


def line_up_kernel(place_ref, *refs):
    *parts, full_ref, staged = refs
    rows = parts[0].shape[0]
    for by, part in enumerate(parts):
        start = pl.multiple_of(lax.rem(place_ref[0] + by, len(parts)) * rows, 8)
        staged[pl.ds(start, rows), :] = part[...].astype(f32)
    full_ref[...] = staged[...].astype(bf16)


def line_up(place, parts):
    rows, columns = parts[0].shape
    full = (len(parts) * rows, columns)
    return call(
        line_up_kernel,
        "line_up",
        (1,),
        [place] + parts,
        [SMEM] + [whole(p.shape) for p in parts],
        [shape_of(full, bf16)],
        [whole(full)],
        [pltpu.VMEM(full, f32)],
    )[0]


def halves_kernel(low, high, top, bottom):
    top[...] = low[...]
    bottom[...] = high[...]


def halves(low, high):
    half, columns = low.shape[0] // 2, low.shape[1]
    if half % 8:
        return [low[:half], high[half:]]
    outs = [shape_of((half, columns), bf16)] * 2
    return call(
        halves_kernel,
        "halves",
        (1,),
        [low, high],
        [
            pl.BlockSpec((half, columns), lambda *_: (0, 0)),
            pl.BlockSpec((half, columns), lambda *_: (1, 0)),
        ],
        outs,
        [whole(o.shape) for o in outs],
    )


def end_sums(own, got):
    count, columns = len(own), sum(a.shape[1] for a in own)
    outs = [shape_of((own[0].shape[0] // 8, columns), bf16)] * 2
    return call(
        functools.partial(end_kernel, count),
        "end_sums",
        (1,),
        own + got,
        blocks_at(own + got, 3),
        outs,
        [whole(o.shape) for o in outs],
    )


def middle_sums(own, got, ends):
    count, columns = len(own), sum(a.shape[1] for a in own)
    outs = [shape_of((own[0].shape[0] // 4, columns), bf16)] * 2
    return call(
        functools.partial(middle_sums_kernel, count),
        "middle_sums",
        (1,),
        own + own + got + got + ends,
        blocks_at(own, 1) + blocks_at(own, 2) + blocks_at(got, 1) + blocks_at(got, 2)
        + [whole(e.shape) for e in ends],
        outs,
        [whole(o.shape) for o in outs],
    )


def line_sums(place, narrow, own, got, sides):
    count, columns = len(own), sum(a.shape[1] for a in own)
    height = own[0].shape[0] // 4
    outs = [shape_of((height // narrow, columns), f32)]
    outs = outs + [shape_of((height // narrow, columns), bf16)] * (narrow - 1)
    made = call(
        functools.partial(line_sums_kernel, count, narrow),
        "line_sums",
        (1,),
        [place] + own + got + sides,
        [SMEM] + blocks_at(own + got, 0) + [whole(s.shape) for s in sides],
        outs,
        [whole(o.shape) for o in outs],
        [pltpu.VMEM((height, columns), f32)],
    )
    return made[0], made[1:]


AXES = ("outer", "core", "narrow")


class Links:
    def __init__(self, wide, narrow):
        self.wide, self.narrow = wide, narrow
        self.bits = [1 << b for b in range((wide // 2).bit_length() - 1)]
        self.outer, self.core, self.place = (lax.axis_index(axis) for axis in AXES)

    def send(self, part, to):
        pairs = []
        for wide in range(self.wide):
            for narrow in range(self.narrow):
                outer, core, place = to(wide // 2, wide % 2, narrow)
                target = (outer * 2 + core) * self.narrow + place
                pairs.append((wide * self.narrow + narrow, target))
        return lax.ppermute(part, AXES, pairs)

    def flip(self, part, mask):
        return self.send(part, lambda o, c, z: (o ^ mask, c, z))

    def swap(self, part):
        return self.send(part, lambda o, c, z: (o, 1 - c, z))

    def shift(self, part, by):
        return self.send(part, lambda o, c, z: (o, c, (z + by) % self.narrow))


def after(values, *deps):
    flat, tree = jax.tree.flatten(values)
    more = jax.tree.leaves(deps)
    held = lax.optimization_barrier(tuple(flat) + tuple(more))
    return jax.tree.unflatten(tree, held[: len(flat)])


def together(always, step):
    shapes = jax.eval_shape(step)
    return lax.cond(
        always, step, lambda: jax.tree.map(lambda s: jnp.zeros(s.shape, s.dtype), shapes)
    )


class Gather:
    def __init__(self, links, part):
        self.links, self.part = links, part

    def send_along(self, which=None):
        which = range(1, self.links.narrow) if which is None else which
        return [self.links.shift(self.part, -by) for by in which]

    def take_along(self, got):
        links, rows = self.links, self.part.shape[0]
        if rows % 8 == 0:
            self.full = line_up(links.place.astype(i32).reshape(1), [self.part] + got)
            return
        full = jnp.zeros((links.narrow * rows, self.part.shape[1]), self.part.dtype)
        for by, part in enumerate([self.part] + got):
            start = (links.place + by) % links.narrow * rows
            full = lax.dynamic_update_slice_in_dim(full, part, start, 0)
        self.full = full

    def send_first(self):
        links, full = self.links, self.full
        return [links.flip(full, bit) for bit in links.bits[:2]] + [links.swap(full)]

    def take_first(self, got):
        self.low, self.high, self.full_over = got
        self.sent = halves(self.low, self.high)

    def send_second(self):
        links = self.links
        low, high = links.bits[0], links.bits[1]
        ends = [links.flip(self.sent[0], high), links.flip(self.sent[1], low)]
        return ends + [links.swap(self.low), links.swap(self.high)]

    def take_second(self, got):
        self.ends, self.over = got[:2], got[2:]

    def send_third(self):
        return [self.links.swap(e) for e in self.ends]

    def take_third(self, got):
        links = self.links
        own = [self.full, self.low, self.high] + self.ends
        over = [self.full_over] + self.over + got
        for bit in links.bits[2:]:
            own = own + [links.flip(p, bit) for p in own]
            over = over + [links.flip(p, bit) for p in over]
        self.pieces = [(p, p.shape[0], 0) for p in own + over]


class PlaneFirst:
    def __init__(self, links, part):
        self.links, self.part = links, part

    def send_first(self):
        return [self.links.flip(self.part, bit) for bit in self.links.bits[:2]]

    def take_first(self, got):
        self.low, self.high = got
        half = self.part.shape[0] // 2
        self.sent = [self.low[:half], self.high[half:]]

    def send_second(self):
        low, high = self.links.bits[0], self.links.bits[1]
        return [self.links.flip(self.sent[0], high), self.links.flip(self.sent[1], low)]

    def take_second(self, got):
        self.end = jnp.concatenate(got)

    def take_lines(self, own):
        for bit in self.links.bits[2:]:
            own = own + [self.links.flip(p, bit) for p in own]
        self.own = own

    def send_over(self, which):
        return [self.links.swap(self.own[number]) for number in which]

    def take_over(self, got):
        self.pieces = [(p, p.shape[0], 0) for p in self.own + got]


def piece_rows(links, own_rows):
    height = links.narrow * own_rows
    low, high = links.bits[0], links.bits[1]
    marks = [(0, 0), (low, 0), (high, 0), (low | high, 0), (low | high, height // 2)]
    for bit in links.bits[2:]:
        marks = marks + [(mask | bit, extra) for mask, extra in marks]
    return jnp.stack(
        [
            ((links.outer ^ mask) * 2 + (links.core ^ over)) * height + extra
            for over in range(2)
            for mask, extra in marks
        ]
    ).astype(i32)


def part_rows(links, own_rows):
    height = links.narrow * own_rows
    return jnp.stack(
        [
            ((links.outer ^ mask) * 2 + (links.core ^ over)) * height
            for over in range(2)
            for mask in range(links.wide // 2)
        ]
    ).astype(i32)


def total(*terms):
    out = terms[0].astype(f32)
    for term in terms[1:]:
        out = out + term.astype(f32)
    return out


class Scatter:
    def __init__(self, links, own, other):
        self.links, self.own, self.other = links, own, other

    def send_over(self):
        return [self.links.swap(part) for part in self.other]

    def take_over(self, got):
        links, own = self.links, self.own
        for bit in links.bits[:1:-1]:
            height = own[0].shape[0] // 2
            sums = [total(a, b).astype(bf16) for a, b in zip(own, got)]
            own = [s[:height] for s in sums]
            got = [links.flip(s[height:], bit) for s in sums]
        self.near, self.got = own, got

    def end(self):
        return end_sums(self.near, self.got)

    def send_first(self):
        low, high = self.links.bits[0], self.links.bits[1]
        return [self.links.flip(self.sums[0], low), self.links.flip(self.sums[1], high)]

    def take_first(self, got):
        self.sums = middle_sums(self.near, self.got, list(got))

    def send_second(self):
        low, high = self.links.bits[0], self.links.bits[1]
        return [self.links.flip(self.sums[0], low), self.links.flip(self.sums[1], high)]

    def take_second(self, got):
        links = self.links
        place = links.place.astype(i32).reshape(1)
        self.mine, self.sums = line_sums(place, links.narrow, self.near, self.got, list(got))

    def send_along(self, which=None):
        which = range(1, self.links.narrow) if which is None else which
        return [self.links.shift(self.sums[by - 1], by) for by in which]

    def take_along(self, got):
        self.result = total(self.mine, *got)


def on_device(
    wide, narrow, inputs, segment_ids, routes, attention_gain, qkv_weight, output_weight,
    mixture_gain, router_train, router_frozen, expert_in, expert_out, frozen_in, frozen_out,
    cotangent,
):
    links = Links(wide, narrow)
    length, width = inputs.shape
    own_rows = qkv_weight.shape[0]
    train_count = expert_in.shape[1]
    experts = train_count + frozen_in.shape[1]
    groups = expert_in.shape[2] // width
    docs = segment_ids[0]
    small = jnp.concatenate(
        [attention_gain[:, None], mixture_gain[:, None], router_train, router_frozen], axis=1
    )
    small = jnp.pad(small, ((0, 0), (0, LANES - small.shape[1])))
    dense = Gather(links, jnp.concatenate([qkv_weight, output_weight, small], axis=1))
    rows, order = piece_rows(links, own_rows), part_rows(links, own_rows)

    def packed(inner, outer):
        inner = inner.reshape(own_rows, width, groups).transpose(0, 2, 1).reshape(own_rows, -1)
        return jnp.concatenate([inner, outer.reshape(own_rows, -1)], axis=1)

    def part_of(e):
        if e < train_count:
            return packed(expert_in[:, e], expert_out[:, e])
        return packed(frozen_in[:, e - train_count], frozen_out[:, e - train_count])

    last = experts - 1
    weights = [Gather(links, part_of(e)) for e in range(last)] + [PlaneFirst(links, part_of(last))]
    always = segment_ids[0, 0] >= 0
    chosen = (routes[:, :, None] == jnp.arange(experts, dtype=i32)).astype(i32)
    per_block = jnp.sum(chosen.reshape(length // BLOCK, 2 * BLOCK, experts), axis=1)
    counts = jnp.concatenate([jnp.zeros((1, experts), i32), jnp.cumsum(per_block, axis=0)])
    counts = counts.reshape(-1)
    place, place_t = route_places(routes)

    def pick(expert, normed, gates):
        return dispatch(
            expert, experts, expert < train_count, order, counts, place_t, gates, normed, cotangent
        )

    def run(expert, picked):
        return expert_pass(
            expert, length // BLOCK * experts + expert, expert < train_count,
            order if expert == last else rows, order, counts, picked, weights[expert].pieces,
        )

    shifts = list(range(1, narrow))

    def line(part, *deps):
        part = after(part, *deps) if deps else part
        return lax.all_gather(part, "narrow", axis=0, tiled=True)

    w0, w1, w2, w3 = weights
    w0.part = after(w0.part, dense.part)
    dense.take_along(dense.send_along())
    w0.full = line(w0.part, dense.full)
    dense.take_first(together(always, dense.send_first))
    w1.full = line(w1.part, dense.low)
    dense.take_second(together(always, dense.send_second))
    w2.full = line(w2.part, dense.ends)
    dense.take_third(dense.send_third())

    def step():
        qkv, full, gains = project(rows, inputs, dense.pieces)
        attended, logs = attend(docs, qkv)
        return w0.send_first(), w3.send_first(), (qkv, full, gains, attended, logs)

    got, ahead, (qkv, dense, gains, attended, logs) = together(always, step)
    w0.take_first(got)
    w3.take_first(ahead)
    w3.own = [line(shard, qkv) for shard in (w3.part, w3.low, w3.high)]
    def step():
        made = middle(inputs, attended, place, dense)
        return w0.send_second(), made, pick(0, *made[1:])

    got, (hidden, normed, gates), picked = together(always, step)
    w0.take_second(got)
    w0.take_third(w0.send_third())
    got, ahead, one = together(
        always, lambda: (w1.send_first(), w3.send_second(), run(0, picked))
    )
    w1.take_first(got)
    w3.take_second(ahead)
    got, picked = together(
        always,
        lambda: (w1.send_second(), [pick(e, normed, gates) for e in range(1, experts)]),
    )
    w1.take_second(got)
    w1.take_third(w1.send_third())
    end = line(w3.end, w1.ends)
    term0 = Scatter(links, [one[2], one[4]], [one[3], one[5]])
    w2.full = after(w2.full, one[0])
    got, more, two = together(
        always, lambda: (w2.send_first(), term0.send_over(), run(1, picked[0]))
    )
    w2.take_first(got)

    term0.take_over(more)
    got, ahead, term0.sums = together(
        always, lambda: (w2.send_second(), w3.send_over([0]), term0.end())
    )
    w2.take_second(got)
    w2.take_third(w2.send_third())
    w3.take_lines(w3.own + [end])
    term1 = Scatter(links, [two[2], two[4]], [two[3], two[5]])
    count = len(w3.own)
    got, more, three = together(
        always, lambda: (w3.send_over(range(1, count)), term1.send_over(), run(2, picked[1]))
    )
    w3.take_over(ahead + got)
    term1.take_over(more)
    term1.sums = term1.end()
    got, more, four = together(
        always, lambda: (term0.send_first(), term1.send_first(), run(3, picked[2]))
    )
    term0.take_first(got)
    results, backs = [[m[i] for m in (one, two, three, four)] for i in range(2)]

    def step():
        made = combine(
            experts, order, counts, place, gates, hidden, normed, cotangent, attended, dense,
            results, backs,
        )
        term1.take_first(more)
        return term0.send_second(), term1.sums, made

    got, term1.sums, (block_output, grad_hidden, grad_heads, *made) = together(always, step)
    term0.take_second(got)
    out_term = Scatter(links, *[[m] for m in made])
    got, more, (dq, dk, dv) = together(
        always,
        lambda: (
            term1.send_second(), term0.send_along(), attend_back(docs, qkv, grad_heads, attended, logs)
        ),
    )
    term1.take_second(got)
    over, one, made = together(
        always,
        lambda: (
            out_term.send_over(), term1.send_along(shifts[:1]),
            weigh(order, inputs, gains, dq, dk, dv),
        ),
    )
    out_term.take_over(over)
    out_term.sums = out_term.end()
    qkv_term = Scatter(links, *[[m] for m in made])
    over, got, last, input_grad = together(
        always,
        lambda: (
            qkv_term.send_over(), out_term.send_first(), term1.send_along(shifts[2:]),
            finish(inputs, gains, dq, dk, dv, grad_hidden, dense),
        ),
    )
    qkv_term.take_over(over)
    qkv_term.sums = qkv_term.end()
    out_term.take_first(got)

    def unpacked(parts):
        full = total(*parts)
        inner = groups * width
        inner, outer = full[:, :inner], full[:, inner:]
        inner = inner.reshape(own_rows, groups, width).transpose(0, 2, 1).reshape(own_rows, -1)
        return inner, outer.reshape(own_rows * groups, width)

    got, two, middle_part, first = together(
        always,
        lambda: (
            qkv_term.send_first(), out_term.send_second(), term1.send_along(shifts[1:2]),
            unpacked([term0.mine] + more),
        ),
    )
    qkv_term.take_first(got)
    out_term.take_second(two)

    def step():
        second = unpacked([term1.mine] + one + middle_part + last)
        in_grad, down_grad = [jnp.stack(pair, axis=1) for pair in zip(first, second)]
        return qkv_term.send_second(), out_term.send_along(), in_grad, down_grad

    got, two, in_grad, down_grad = together(always, step)
    qkv_term.take_second(got)

    def step():
        out_term.take_along(two)
        out = out_term.result
        return qkv_term.send_along(), (
            out[:, :width], out[:, width + LANES - 1], out[:, width : width + train_count]
        )

    got, outs = together(always, step)
    qkv_term.take_along(got)
    qkv_grad = qkv_term.result
    gain_grad = jnp.sum(qkv_weight.astype(f32) * qkv_grad, axis=1) / attention_gain.astype(f32)
    return (
        block_output,
        input_grad,
        gain_grad,
        qkv_grad,
        *outs,
        in_grad,
        down_grad,
    )


def solution(mesh):
    wide, narrow = mesh.shape["wide"], mesh.shape["narrow"]
    mesh = Mesh(mesh.devices.reshape(wide // 2, 2, narrow), AXES)
    rows = P(AXES)
    return jax.shard_map(
        functools.partial(on_device, wide, narrow),
        mesh=mesh,
        in_specs=(rows,) * 14,
        out_specs=(rows,) * 9,
        check_vma=False,
    )
```

```python
import functools

import jax
import jax.numpy as jnp
from jax import lax
from jax.experimental import pallas as pl
from jax.experimental.pallas import tpu as pltpu
from jax.sharding import Mesh, PartitionSpec as P

HEAD_DIM = 64
PAIR = 2 * HEAD_DIM
CAP = 768
MAX_DOC = 512
BLOCK = 256
WINDOW = BLOCK + 128
ROW_TILE = 256
LANES = 128
EPS = 1e-05
bf16, f32, i32 = jnp.bfloat16, jnp.float32, jnp.int32


def dot_nn(a, b):
    return lax.dot_general(a, b, (((1,), (0,)), ((), ())), preferred_element_type=f32)


def dot_nt(a, b):
    return lax.dot_general(a, b, (((1,), (1,)), ((), ())), preferred_element_type=f32)


def dot_tn(a, b):
    return lax.dot_general(a, b, (((0,), (0,)), ((), ())), preferred_element_type=f32)


def iota(shape, dim):
    return lax.broadcasted_iota(i32, shape, dim)


def flag(mask, dtype=bf16):
    return jnp.where(mask, 1.0, 0.0).astype(dtype)


def normalized(values):
    center = values - jnp.mean(values, axis=-1, keepdims=True)
    spread = jnp.mean(center * center, axis=-1, keepdims=True)
    inverse = lax.rsqrt(spread + EPS)
    return center * inverse, inverse


def norm_back(xhat, inverse, gain, grad):
    scaled = grad * gain
    return inverse * (
        scaled
        - jnp.mean(scaled, axis=-1, keepdims=True)
        - xhat * jnp.mean(scaled * xhat, axis=-1, keepdims=True)
    )


def params(limit_mib, **kw):
    return pltpu.CompilerParams(vmem_limit_bytes=limit_mib << 20, **kw)


def whole(shape):
    return pl.BlockSpec(shape, lambda *_: (0,) * len(shape))


def call(kernel, name, grid, ins, in_specs, outs, out_specs, scratch=(), limit=48, flops=0):
    size = sum(a.size * a.dtype.itemsize for a in ins) + sum(
        o.size * o.dtype.itemsize for o in outs
    )
    return pl.pallas_call(
        kernel,
        name=name,
        grid=grid,
        in_specs=in_specs,
        out_specs=out_specs,
        out_shape=outs,
        scratch_shapes=list(scratch),
        compiler_params=params(limit),
        cost_estimate=pl.CostEstimate(flops=flops, bytes_accessed=size, transcendentals=0),
    )(*ins)


def shape_of(shape, dtype):
    return jax.ShapeDtypeStruct(shape, dtype)


def gathered_specs(pieces, columns, index):
    return [
        pl.BlockSpec((height, columns), lambda *i, at=at: (at, index(*i)))
        for _, height, at in pieces
    ]


def put_together(rows_ref, piece_refs, whole_ref):
    for number, piece in enumerate(piece_refs):
        height = piece.shape[0]
        start = pl.multiple_of(rows_ref[number], 16 if height % 16 == 0 else 8)
        whole_ref[pl.ds(start, height), :] = piece[...]


def lay_out(order_ref, staged_ref, own_ref, other_ref):
    parts = order_ref.shape[0] // 2
    height = own_ref.shape[0] // parts
    for half, ref in enumerate((own_ref, other_ref)):
        for part in range(parts):
            start = order_ref[half * parts + part]
            start = pl.multiple_of(start, 16 if height % 16 == 0 else 8)
            ref[part * height : (part + 1) * height, :] = staged_ref[pl.ds(start, height), :]


SMEM = pl.BlockSpec(memory_space=pltpu.SMEM)


def route_kernel(routes_ref, routes_t_ref, place_ref, place_t_ref):
    length = routes_ref.shape[0]
    lane = iota((length, LANES), 1)
    mask = (lane == routes_ref[:, 0:1]) | (lane == routes_ref[:, 1:2])
    before = flag(iota((length, length), 1) < iota((length, length), 0))
    place_ref[...] = jnp.where(mask, dot_nn(before, flag(mask)), -1.0).astype(i32)
    sub = iota((8, length), 0)
    mask_t = (sub == routes_t_ref[0:1, :]) | (sub == routes_t_ref[1:2, :])
    before_t = flag(iota((length, length), 0) < iota((length, length), 1))
    place_t_ref[...] = jnp.where(mask_t, dot_nn(flag(mask_t), before_t), -1.0).astype(i32)


def route_places(routes):
    length = routes.shape[0]
    outs = [shape_of((length, LANES), i32), shape_of((8, length), i32)]
    return call(
        route_kernel,
        "places",
        (),
        [routes, routes.T],
        [whole((length, 2)), whole((2, length))],
        outs,
        [whole(o.shape) for o in outs],
    )


def gains_of(small_ref):
    return small_ref[...].astype(f32).T


def project_kernel(count, rows_ref, inputs_ref, *rest):
    pieces, (qkv_ref, dense_ref, rows_out_ref, gains_ref) = rest[:count], rest[count:]
    width = inputs_ref.shape[1]

    @pl.when(pl.program_id(0) == 0)
    def _():
        put_together(rows_ref, pieces, dense_ref)
        gains_ref[...] = dense_ref[:, 4 * width :].astype(f32).T
        rows_out_ref[...] = gains_ref[:16, :].astype(bf16)

    xhat, _ = normalized(inputs_ref[...].astype(f32))
    normed = (gains_ref[0:1, :] * xhat).astype(bf16)
    qkv_ref[...] = dot_nn(normed, dense_ref[:, : 3 * width]).astype(bf16)


def project(rows, inputs, pieces):
    length, width = inputs.shape
    columns = pieces[0][0].shape[1]
    return call(
        functools.partial(project_kernel, len(pieces)),
        "project",
        (length // BLOCK,),
        [rows, inputs] + [p[0] for p in pieces],
        [SMEM, pl.BlockSpec((BLOCK, width), lambda i: (i, 0))]
        + gathered_specs(pieces, columns, lambda i: 0),
        [
            shape_of((length, 3 * width), bf16),
            shape_of((width, columns), bf16),
            shape_of((16, width), bf16),
        ],
        [
            pl.BlockSpec((BLOCK, 3 * width), lambda i: (i, 0)),
            whole((width, columns)),
            whole((16, width)),
        ],
        [pltpu.VMEM((LANES, width), f32)],
        flops=2 * length * width * 3 * width,
    )


def span_of(block):
    reach = MAX_DOC // BLOCK
    start = max(0, block - reach) * BLOCK
    return start, (block + 1) * BLOCK - start


def attend_kernel(doc_ref, doc_t_ref, q_ref, k_ref, v_ref, out_ref, log_ref, bias_ref):
    length = q_ref.shape[0]
    blocks = length // BLOCK

    @pl.when(pl.program_id(0) == 0)
    def _():
        for block in range(blocks):
            start, size = span_of(block)
            rows = slice(block * BLOCK, (block + 1) * BLOCK)
            row = iota((BLOCK, size), 0) + block * BLOCK
            col = iota((BLOCK, size), 1) + start
            kept = (row >= col) & (doc_ref[rows, :] == doc_t_ref[:, start : start + size])
            bias_ref[rows, :size] = jnp.where(kept, 0.0, -1e30)

    first = iota((BLOCK, PAIR), 1) < HEAD_DIM
    for block in range(blocks):
        start, size = span_of(block)
        rows = slice(block * BLOCK, (block + 1) * BLOCK)
        query = q_ref[rows, :] * 0.125
        keys, values = k_ref[start : start + size, :], v_ref[start : start + size, :]
        bias = bias_ref[rows, :size]
        parts, logs = [], []
        for own in (first, ~first):
            scores = dot_nt(jnp.where(own, query, 0).astype(bf16), keys) + bias
            peak = jnp.max(scores, axis=-1, keepdims=True)
            raised = jnp.exp(scores - peak)
            total = jnp.sum(raised, axis=-1, keepdims=True)
            parts.append(dot_nn(raised.astype(bf16), values) * (1.0 / total))
            logs.append(peak + jnp.log(total))
        out_ref[rows, :] = jnp.where(first, parts[0], parts[1]).astype(bf16)
        turned = jnp.where(first, logs[0], logs[1]).T
        log_ref[0, 0:1, rows] = turned[0:1, :]
        log_ref[0, 1:2, rows] = turned[HEAD_DIM : HEAD_DIM + 1, :]


def attend(docs, qkv):
    length, width = qkv.shape[0], qkv.shape[1] // 3
    pairs = width // PAIR
    heads = [pl.BlockSpec((length, PAIR), lambda i, k=k: (0, k * pairs + i)) for k in range(3)]
    return call(
        attend_kernel,
        "attend",
        (pairs,),
        [docs.reshape(length, 1), docs.reshape(1, length), qkv, qkv, qkv],
        [whole((length, 1)), whole((1, length))] + heads,
        [shape_of((length, width), bf16), shape_of((pairs, 8, length), f32)],
        [
            pl.BlockSpec((length, PAIR), lambda i: (0, i)),
            pl.BlockSpec((1, 8, length), lambda i: (i, 0, 0)),
        ],
        [pltpu.VMEM((length, MAX_DOC + BLOCK), f32)],
        flops=4 * length * 768 * width,
    )


def attend_back_kernel(
    doc_ref, doc_t_ref, q_ref, k_ref, v_ref, grad_ref, out_ref, log_ref, dq_ref, dk_ref, dv_ref,
    bias_ref, dk_sum, dv_sum,
):
    length = q_ref.shape[0]
    blocks = length // BLOCK

    @pl.when(pl.program_id(0) == 0)
    def _():
        for block in range(blocks):
            start, size = span_of(block)
            cols = slice(block * BLOCK, (block + 1) * BLOCK)
            row = iota((size, BLOCK), 0) + start
            col = iota((size, BLOCK), 1) + block * BLOCK
            kept = (col >= row) & (doc_ref[start : start + size, :] == doc_t_ref[:, cols])
            bias_ref[:size, cols] = jnp.where(kept, 0.0, -1e30)

    turned_keys = k_ref[...].T
    dk_sum[...] = jnp.zeros_like(dk_sum)
    dv_sum[...] = jnp.zeros_like(dv_sum)
    first = iota((BLOCK, PAIR), 1) < HEAD_DIM
    for block in range(blocks):
        start, size = span_of(block)
        rows, span = slice(block * BLOCK, (block + 1) * BLOCK), slice(start, start + size)
        query, grad = q_ref[rows, :] * 0.125, grad_ref[rows, :]
        keys, values = k_ref[span, :], v_ref[span, :]
        bias = bias_ref[:size, rows]
        turned = (grad.astype(f32) * out_ref[rows, :].astype(f32)).T
        parts, dk, dv = [], 0.0, 0.0
        for head, own in enumerate((first, ~first)):
            own_query = jnp.where(own, query, 0).astype(bf16)
            own_grad = jnp.where(own, grad, 0).astype(bf16)
            scores = dot_nt(keys, own_query) + bias
            probs = jnp.exp(scores - log_ref[0, head : head + 1, rows])
            dv = dv + dot_nn(probs.astype(bf16), own_grad)
            lanes = slice(head * HEAD_DIM, (head + 1) * HEAD_DIM)
            mean = jnp.sum(turned[lanes, :], axis=0, keepdims=True)
            grad_scores = (probs * (dot_nt(values, own_grad) - mean)).astype(bf16)
            dk = dk + dot_nn(grad_scores, own_query)
            parts.append(dot_nn(turned_keys[lanes, span], grad_scores))
        dq_ref[rows, :] = (jnp.concatenate(parts).T * 0.125).astype(bf16)
        dk_sum[span, :] += dk
        dv_sum[span, :] += dv
    dk_ref[...] = dk_sum[...].astype(bf16)
    dv_ref[...] = dv_sum[...].astype(bf16)


def attend_back(docs, qkv, grad, attended, logs):
    length, width = qkv.shape[0], qkv.shape[1] // 3
    pairs = width // PAIR
    heads = [pl.BlockSpec((length, PAIR), lambda i, k=k: (0, k * pairs + i)) for k in range(3)]
    one = pl.BlockSpec((length, PAIR), lambda i: (0, i))
    return call(
        attend_back_kernel,
        "attend_back",
        (pairs,),
        [docs.reshape(length, 1), docs.reshape(1, length), qkv, qkv, qkv, grad, attended, logs],
        [whole((length, 1)), whole((1, length))]
        + heads
        + [one, one, pl.BlockSpec((1, 8, length), lambda i: (i, 0, 0))],
        [shape_of((length, width), bf16)] * 3,
        [one] * 3,
        [
            pltpu.VMEM((MAX_DOC + BLOCK, length), f32),
            pltpu.VMEM((length, PAIR), f32),
            pltpu.VMEM((length, PAIR), f32),
        ],
        flops=10 * length * 768 * width,
    )


def middle_kernel(
    inputs_ref, attended_ref, place_ref, weight_ref, small_ref, hidden_ref, normed_ref, gate_ref,
    gains_ref,
):
    @pl.when(pl.program_id(0) == 0)
    def _():
        gains_ref[...] = gains_of(small_ref)

    hidden = inputs_ref[...].astype(f32) + dot_nn(attended_ref[...], weight_ref[...])
    hidden_ref[...] = hidden
    xhat, _ = normalized(hidden)
    normed = (gains_ref[1:2, :] * xhat).astype(bf16)
    normed_ref[...] = normed
    logits = dot_nn(normed, small_ref[...])
    mask = place_ref[...] >= 0
    logits = jnp.where(mask, pltpu.roll(logits, LANES - 2, 1), -1e30)
    peak = jnp.max(logits, axis=-1, keepdims=True)
    raised = jnp.where(mask, jnp.exp(logits - peak), 0.0)
    gate_ref[...] = raised / jnp.sum(raised, axis=-1, keepdims=True)


def middle(inputs, attended, place, dense):
    length, width = inputs.shape
    row = pl.BlockSpec((BLOCK, width), lambda i: (i, 0))
    thin = pl.BlockSpec((BLOCK, LANES), lambda i: (i, 0))
    return call(
        middle_kernel,
        "middle",
        (length // BLOCK,),
        [inputs, attended, place, dense, dense],
        [
            row,
            row,
            thin,
            pl.BlockSpec((width, width), lambda i: (0, 3)),
            pl.BlockSpec((width, LANES), lambda i: (0, 4 * width // LANES)),
        ],
        [
            shape_of((length, width), f32),
            shape_of((length, width), bf16),
            shape_of((length, LANES), f32),
        ],
        [row, row, thin],
        [pltpu.VMEM((LANES, width), f32)],
        flops=2 * length * width * width,
    )


def window_base(counts_ref, block, expert, experts):
    base = counts_ref[block * experts + expert]
    return pl.multiple_of(jnp.minimum(base // 128 * 128, CAP - WINDOW), 128)


def dispatch_kernel(
    expert, experts, order_ref, counts_ref, place_t_ref, gate_ref, normed_ref, cot_ref, x_ref, g_ref,
    *rest,
):
    length = normed_ref.shape[0]
    x_ref[...] = jnp.zeros_like(x_ref)
    g_ref[...] = jnp.zeros_like(g_ref)
    for block in range(length // BLOCK):
        base = window_base(counts_ref, block, expert, experts)
        cols = slice(block * BLOCK, (block + 1) * BLOCK)
        pick = flag(iota((WINDOW, BLOCK), 0) + base == place_t_ref[expert : expert + 1, cols])
        window = pl.ds(base, WINDOW)
        x_ref[window, :] += dot_nn(pick, normed_ref[cols, :]).astype(bf16)
        scaled = gate_ref[cols, expert : expert + 1] * cot_ref[cols, :].astype(f32)
        g_ref[window, :] += dot_nn(pick, scaled.astype(bf16)).astype(bf16)
    if rest:
        turned_ref, staged = rest
        half = turned_ref.shape[0] // 2
        staged[...] = x_ref[...].T
        lay_out(order_ref, staged, turned_ref.at[:half], turned_ref.at[half:])


def dispatch(expert, experts, train, order, counts, place_t, gates, normed, cot):
    width = normed.shape[1]
    outs = [shape_of((CAP, width), bf16)] * 2
    outs = outs + ([shape_of((width, CAP), bf16)] if train else [])
    ins = [place_t, gates, normed, cot]
    return call(
        functools.partial(dispatch_kernel, expert, experts),
        "dispatch_%d" % expert,
        (1,),
        [order, counts] + ins,
        [SMEM, SMEM] + [whole(a.shape) for a in ins],
        outs,
        [whole(o.shape) for o in outs],
        [pltpu.VMEM((width, CAP), bf16)] if train else [],
        flops=4 * CAP * WINDOW * width,
    )


def expert_kernel(slot, train, count, rows_ref, order_ref, counts_ref, *rest):
    rows_x, rows_g, rest = rest[0], rest[1], rest[2:]
    if train:
        turned_x, rest = rest[0], rest[1:]
    in_pieces, out_pieces, rest = rest[:count], rest[count : 2 * count], rest[2 * count :]
    result_ref, back_ref, rest = rest[0], rest[1], rest[2:]
    if train:
        in_own, in_other, out_own, out_other = rest[:4]
        rest = rest[4:]
        acts, grads, staged = rest[4:]
    sum_r, sum_b, in_ref, out_ref = rest[:4]
    half = rows_x.shape[1] // 2
    step = pl.program_id(0)
    load = counts_ref[slot]

    @pl.when(step == 0)
    def _():
        sum_r[...] = jnp.zeros_like(sum_r)
        sum_b[...] = jnp.zeros_like(sum_b)

    put_together(rows_ref, in_pieces, in_ref)
    put_together(rows_ref, out_pieces, out_ref)

    def tile(index, carry):
        rows = pl.ds(pl.multiple_of(index * ROW_TILE, ROW_TILE), ROW_TILE)
        pre = dot_nn(rows_x[rows, :], in_ref[...])
        grad_rows = rows_g[rows, :]
        square = pre * pre
        bend = jnp.tanh(0.7978845608028654 * pre * (1.0 + 0.044715 * square))
        half = 0.5 + 0.5 * bend
        slope = half + pre * (0.5 - 0.5 * bend * bend) * (
            0.7978845608028654 + 0.1070322243 * square
        )
        act = (pre * half).astype(bf16)
        grad = (dot_nt(grad_rows, out_ref[...]) * slope).astype(bf16)
        sum_r[rows, :] += dot_nn(act, out_ref[...])
        sum_b[rows, :] += dot_nt(grad, in_ref[...])
        if train:
            acts[rows, :] = act
            grads[rows, :] = grad
        return carry

    tiles = jnp.maximum((load + ROW_TILE - 1) // ROW_TILE, 1)
    lax.fori_loop(0, tiles, tile, 0)
    if train:
        for amount in range(1, CAP // ROW_TILE + 1):

            @pl.when(tiles == amount)
            def _(used=amount * ROW_TILE):
                inner = dot_nn(turned_x[:, :used], grads[:used, :]).astype(bf16)
                in_own[...] = inner[:half]
                in_other[...] = inner[half:]
                staged[...] = dot_tn(acts[:used, :], rows_g[:used, :]).astype(bf16)

        lay_out(order_ref, staged, out_own, out_other)

    @pl.when(step == pl.num_programs(0) - 1)
    def _():
        result_ref[...] = sum_r[...].astype(bf16)
        back_ref[...] = sum_b[...].astype(bf16)


def expert_pass(expert, slot, train, rows, order, counts, picked, pieces):
    width = picked[0].shape[1]
    hidden = pieces[0][0].shape[1] // 2
    arrays = [p[0] for p in pieces]
    steps = hidden // width
    half = width // 2
    slab = pl.BlockSpec((half, width), lambda i: (0, i))
    outs = [shape_of((CAP, width), bf16)] * 2
    out_specs = [whole((CAP, width))] * 2
    scratch = [
        pltpu.VMEM((CAP, width), f32),
        pltpu.VMEM((CAP, width), f32),
        pltpu.VMEM((width, width), bf16),
        pltpu.VMEM((width, width), bf16),
    ]
    if train:
        outs = outs + [shape_of((half, hidden), bf16)] * 4
        out_specs = out_specs + [slab] * 4
        scratch = scratch + [
            pltpu.VMEM((CAP, width), bf16),
            pltpu.VMEM((CAP, width), bf16),
            pltpu.VMEM((width, width), bf16),
        ]
    return call(
        functools.partial(expert_kernel, slot, train, len(pieces)),
        "expert_%d" % expert,
        (steps,),
        [rows, order, counts] + list(picked) + arrays + arrays,
        [SMEM, SMEM, SMEM]
        + [whole(p.shape) for p in picked]
        + gathered_specs(pieces, width, lambda i: i)
        + gathered_specs(pieces, width, lambda i: i + steps),
        outs,
        out_specs,
        scratch,
        limit=56,
        flops=(12 if train else 8) * 600 * width * hidden,
    )


def combine_kernel(
    experts, order_ref, counts_ref, place_ref, gate_ref, hidden_ref, normed_ref, cot_ref, attended_ref,
    weight_ref, small_ref, *rest,
):
    result_refs, back_refs = rest[:experts], rest[experts : 2 * experts]
    (output_ref, grad_hidden_ref, grad_heads_ref, own_ref, other_ref,
     gains_ref, weight_sum, gain_sum, router_sum, staged) = rest[2 * experts :]
    step = pl.program_id(0)

    @pl.when(step == 0)
    def _():
        gains_ref[...] = gains_of(small_ref)
        weight_sum[...] = jnp.zeros_like(weight_sum)
        gain_sum[...] = jnp.zeros_like(gain_sum)
        router_sum[...] = jnp.zeros_like(router_sum)

    cot = cot_ref[...].astype(f32)
    hidden = hidden_ref[...]
    gates = gate_ref[...]
    lane = iota((BLOCK, LANES), 1)
    total, grad_normed = hidden, 0.0
    grad_gate = jnp.zeros((BLOCK, LANES), f32)
    for expert in range(experts):
        base = window_base(counts_ref, step, expert, experts)
        window = pl.ds(base, WINDOW)
        pick = flag(iota((BLOCK, WINDOW), 1) + base == place_ref[:, expert : expert + 1])
        picked = dot_nn(pick, result_refs[expert][window, :])
        total = total + gates[:, expert : expert + 1] * picked
        grad_gate = jnp.where(
            lane == expert, jnp.sum(cot * picked, axis=-1, keepdims=True), grad_gate
        )
        grad_normed = grad_normed + dot_nn(pick, back_refs[expert][window, :])
    output_ref[...] = total.astype(bf16)
    grad_logits = gates * (grad_gate - jnp.sum(gates * grad_gate, axis=-1, keepdims=True))
    high = grad_logits.astype(bf16)
    low = (grad_logits - high.astype(f32)).astype(bf16)
    gains = gains_ref[...]
    router = pltpu.roll(gains, LANES - 2, 0).astype(bf16)
    both = jnp.concatenate([high, low], axis=1)
    grad_normed = grad_normed + dot_nn(both, jnp.concatenate([router, router]))
    made = dot_tn(normed_ref[...], both)
    router_sum[...] += made[:, :LANES] + made[:, LANES:]
    xhat, inverse = normalized(hidden)
    gain_sum[...] += jnp.sum(grad_normed * xhat, axis=0, keepdims=True)
    grad_hidden = cot + norm_back(xhat, inverse, gains[1:2, :], grad_normed)
    grad_hidden_ref[...] = grad_hidden
    branch = grad_hidden.astype(bf16)
    grad_heads_ref[...] = dot_nt(branch, weight_ref[...]).astype(bf16)
    weight_sum[...] += dot_tn(attended_ref[...], branch)

    @pl.when(step == pl.num_programs(0) - 1)
    def _():
        width = weight_sum.shape[1]
        gain = jnp.broadcast_to(gain_sum[...], (LANES, width)).T
        small = jnp.where(iota((width, LANES), 1) == LANES - 1, gain, router_sum[...])
        staged[:, :width] = weight_sum[...].astype(bf16)
        staged[:, width:] = small.astype(bf16)
        lay_out(order_ref, staged, own_ref, other_ref)


def combine(
    experts, order, counts, place, gates, hidden, normed, cot, attended, dense, results, backs
):
    length, width = hidden.shape
    row = pl.BlockSpec((BLOCK, width), lambda i: (i, 0))
    thin = pl.BlockSpec((BLOCK, LANES), lambda i: (i, 0))
    term = (width // 2, width + LANES)
    return call(
        functools.partial(combine_kernel, experts),
        "combine",
        (length // BLOCK,),
        [order, counts, place, gates, hidden, normed, cot, attended, dense, dense]
        + results
        + backs,
        [
            SMEM,
            SMEM,
            thin,
            thin,
            row,
            row,
            row,
            row,
            pl.BlockSpec((width, width), lambda i: (0, 3)),
            pl.BlockSpec((width, LANES), lambda i: (0, 4 * width // LANES)),
        ]
        + [whole((CAP, width))] * (2 * experts),
        [
            shape_of((length, width), bf16),
            shape_of((length, width), f32),
            shape_of((length, width), bf16),
            shape_of(term, bf16),
            shape_of(term, bf16),
        ],
        [row, row, row, whole(term), whole(term)],
        [
            pltpu.VMEM((LANES, width), f32),
            pltpu.VMEM((width, width), f32),
            pltpu.VMEM((1, width), f32),
            pltpu.VMEM((width, LANES), f32),
            pltpu.VMEM((width, width + LANES), bf16),
        ],
        limit=56,
        flops=8 * length * width * width,
    )


def weigh_kernel(order_ref, inputs_ref, gain_ref, dq_ref, dk_ref, dv_ref, own_ref, other_ref, turned,
                 staged):
    half = inputs_ref.shape[1] // 2

    @pl.when(pl.program_id(0) == 0)
    def _():
        xhat, _ = normalized(inputs_ref[...].astype(f32))
        staged[...] = (gain_ref[0:1, :].astype(f32) * xhat).astype(bf16).T
        lay_out(order_ref, staged, turned.at[:half], turned.at[half:])

    for k, ref in enumerate((dq_ref, dk_ref, dv_ref)):

        @pl.when(pl.program_id(0) == k)
        def _(ref=ref):
            grad = dot_nn(turned[...], ref[...]).astype(bf16)
            own_ref[...] = grad[:half]
            other_ref[...] = grad[half:]


def weigh(order, inputs, gains, dq, dk, dv):
    length, width = inputs.shape
    outs = [shape_of((width // 2, 3 * width), bf16)] * 2
    return call(
        weigh_kernel,
        "weigh",
        (3,),
        [order, inputs, gains, dq, dk, dv],
        [SMEM, whole((length, width)), whole(gains.shape)] + [whole((length, width))] * 3,
        outs,
        [pl.BlockSpec((width // 2, width), lambda i: (0, i))] * 2,
        [pltpu.VMEM((width, length), bf16), pltpu.VMEM((width, length), bf16)],
        limit=56,
        flops=2 * length * width * 3 * width,
    )


def finish_kernel(inputs_ref, gain_ref, dq_ref, dk_ref, dv_ref, grad_hidden_ref, weight_ref, grad_ref):
    width = inputs_ref.shape[1]
    xhat, inverse = normalized(inputs_ref[...].astype(f32))
    grad = 0.0
    for k, ref in enumerate((dq_ref, dk_ref, dv_ref)):
        grad = grad + dot_nt(ref[...], weight_ref[:, k * width : (k + 1) * width])
    gain = gain_ref[0:1, :].astype(f32)
    grad_ref[...] = grad_hidden_ref[...] + norm_back(xhat, inverse, gain, grad)


def finish(inputs, gains, dq, dk, dv, grad_hidden, dense):
    length, width = inputs.shape
    row = pl.BlockSpec((BLOCK, width), lambda i: (i, 0))
    return call(
        finish_kernel,
        "finish",
        (length // BLOCK,),
        [inputs, gains, dq, dk, dv, grad_hidden, dense],
        [
            row,
            whole(gains.shape),
            row,
            row,
            row,
            row,
            pl.BlockSpec((width, 3 * width), lambda i: (0, 0)),
        ],
        [shape_of((length, width), f32)],
        [row],
        limit=56,
        flops=2 * length * width * 3 * width,
    )[0]


def wide_slices(refs):
    edges = [sum(r.shape[1] for r in refs[:i]) for i in range(len(refs) + 1)]
    return [slice(a, b) for a, b in zip(edges, edges[1:])]


def end_kernel(count, *refs):
    own, got, (top, bottom) = refs[:count], refs[count : 2 * count], refs[2 * count :]
    half = top.shape[0]
    for one, other, cols in zip(own, got, wide_slices(own)):
        both = one[...].astype(f32) + other[...].astype(f32)
        top[:, cols] = both[:half].astype(bf16)
        bottom[:, cols] = both[half:].astype(bf16)


def middle_sums_kernel(count, *refs):
    own, got = refs[: 2 * count], refs[2 * count : 4 * count]
    top, bottom, to_low, to_high = refs[4 * count :]
    half = top.shape[0]
    for k, cols in enumerate(wide_slices(own[:count])):
        both = own[k][...].astype(f32) + got[k][...].astype(f32)
        to_low[:half, cols] = both[:half].astype(bf16)
        to_low[half:, cols] = (both[half:] + bottom[:, cols].astype(f32)).astype(bf16)
        both = own[count + k][...].astype(f32) + got[count + k][...].astype(f32)
        to_high[:half, cols] = (both[:half] + top[:, cols].astype(f32)).astype(bf16)
        to_high[half:, cols] = both[half:].astype(bf16)


def line_sums_kernel(count, narrow, place_ref, *refs):
    own, got = refs[:count], refs[count : 2 * count]
    low, high, mine, *sums, whole_ref = refs[2 * count :]
    rows = mine.shape[0]
    for one, other, cols in zip(own, got, wide_slices(own)):
        whole_ref[:, cols] = (
            one[...].astype(f32)
            + other[...].astype(f32)
            + low[:, cols].astype(f32)
            + high[:, cols].astype(f32)
        )
    for by, ref in enumerate([mine] + sums):
        number = lax.rem(place_ref[0] + by, narrow)
        if rows % 8 == 0:
            start = pl.multiple_of(number * rows, 8)
            ref[...] = whole_ref[pl.ds(start, rows), :].astype(ref.dtype)
        else:
            for other in range(narrow):

                @pl.when(number == other)
                def _(ref=ref, at=other * rows):
                    ref[...] = whole_ref[at : at + rows, :].astype(ref.dtype)


def blocks_at(arrays, number):
    return [pl.BlockSpec((a.shape[0] // 4, a.shape[1]), lambda *_: (number, 0)) for a in arrays]


def line_up_kernel(place_ref, *refs):
    *parts, full_ref, staged = refs
    rows = parts[0].shape[0]
    for by, part in enumerate(parts):
        start = pl.multiple_of(lax.rem(place_ref[0] + by, len(parts)) * rows, 8)
        staged[pl.ds(start, rows), :] = part[...].astype(f32)
    full_ref[...] = staged[...].astype(bf16)


def line_up(place, parts):
    rows, columns = parts[0].shape
    full = (len(parts) * rows, columns)
    return call(
        line_up_kernel,
        "line_up",
        (1,),
        [place] + parts,
        [SMEM] + [whole(p.shape) for p in parts],
        [shape_of(full, bf16)],
        [whole(full)],
        [pltpu.VMEM(full, f32)],
    )[0]


def halves_kernel(low, high, top, bottom):
    top[...] = low[...]
    bottom[...] = high[...]


def halves(low, high):
    half, columns = low.shape[0] // 2, low.shape[1]
    if half % 8:
        return [low[:half], high[half:]]
    outs = [shape_of((half, columns), bf16)] * 2
    return call(
        halves_kernel,
        "halves",
        (1,),
        [low, high],
        [
            pl.BlockSpec((half, columns), lambda *_: (0, 0)),
            pl.BlockSpec((half, columns), lambda *_: (1, 0)),
        ],
        outs,
        [whole(o.shape) for o in outs],
    )


def end_sums(own, got):
    count, columns = len(own), sum(a.shape[1] for a in own)
    outs = [shape_of((own[0].shape[0] // 8, columns), bf16)] * 2
    return call(
        functools.partial(end_kernel, count),
        "end_sums",
        (1,),
        own + got,
        blocks_at(own + got, 3),
        outs,
        [whole(o.shape) for o in outs],
    )


def middle_sums(own, got, ends):
    count, columns = len(own), sum(a.shape[1] for a in own)
    outs = [shape_of((own[0].shape[0] // 4, columns), bf16)] * 2
    return call(
        functools.partial(middle_sums_kernel, count),
        "middle_sums",
        (1,),
        own + own + got + got + ends,
        blocks_at(own, 1) + blocks_at(own, 2) + blocks_at(got, 1) + blocks_at(got, 2)
        + [whole(e.shape) for e in ends],
        outs,
        [whole(o.shape) for o in outs],
    )


def line_sums(place, narrow, own, got, sides):
    count, columns = len(own), sum(a.shape[1] for a in own)
    height = own[0].shape[0] // 4
    outs = [shape_of((height // narrow, columns), f32)]
    outs = outs + [shape_of((height // narrow, columns), bf16)] * (narrow - 1)
    made = call(
        functools.partial(line_sums_kernel, count, narrow),
        "line_sums",
        (1,),
        [place] + own + got + sides,
        [SMEM] + blocks_at(own + got, 0) + [whole(s.shape) for s in sides],
        outs,
        [whole(o.shape) for o in outs],
        [pltpu.VMEM((height, columns), f32)],
    )
    return made[0], made[1:]


AXES = ("outer", "core", "narrow")


class Links:
    def __init__(self, wide, narrow):
        self.wide, self.narrow = wide, narrow
        self.bits = [1 << b for b in range((wide // 2).bit_length() - 1)]
        self.outer, self.core, self.place = (lax.axis_index(axis) for axis in AXES)

    def send(self, part, to):
        pairs = []
        for wide in range(self.wide):
            for narrow in range(self.narrow):
                outer, core, place = to(wide // 2, wide % 2, narrow)
                target = (outer * 2 + core) * self.narrow + place
                pairs.append((wide * self.narrow + narrow, target))
        return lax.ppermute(part, AXES, pairs)

    def flip(self, part, mask):
        return self.send(part, lambda o, c, z: (o ^ mask, c, z))

    def swap(self, part):
        return self.send(part, lambda o, c, z: (o, 1 - c, z))

    def shift(self, part, by):
        return self.send(part, lambda o, c, z: (o, c, (z + by) % self.narrow))


def after(values, *deps):
    flat, tree = jax.tree.flatten(values)
    more = jax.tree.leaves(deps)
    held = lax.optimization_barrier(tuple(flat) + tuple(more))
    return jax.tree.unflatten(tree, held[: len(flat)])


def together(always, step):
    shapes = jax.eval_shape(step)
    return lax.cond(
        always, step, lambda: jax.tree.map(lambda s: jnp.zeros(s.shape, s.dtype), shapes)
    )


class Gather:
    def __init__(self, links, part):
        self.links, self.part = links, part

    def send_along(self, which=None):
        which = range(1, self.links.narrow) if which is None else which
        return [self.links.shift(self.part, -by) for by in which]

    def take_along(self, got):
        links, rows = self.links, self.part.shape[0]
        if rows % 8 == 0:
            self.full = line_up(links.place.astype(i32).reshape(1), [self.part] + got)
            return
        full = jnp.zeros((links.narrow * rows, self.part.shape[1]), self.part.dtype)
        for by, part in enumerate([self.part] + got):
            start = (links.place + by) % links.narrow * rows
            full = lax.dynamic_update_slice_in_dim(full, part, start, 0)
        self.full = full

    def send_first(self):
        links, full = self.links, self.full
        return [links.flip(full, bit) for bit in links.bits[:2]] + [links.swap(full)]

    def take_first(self, got):
        self.low, self.high, self.full_over = got
        self.sent = halves(self.low, self.high)

    def send_second(self):
        links = self.links
        low, high = links.bits[0], links.bits[1]
        ends = [links.flip(self.sent[0], high), links.flip(self.sent[1], low)]
        return ends + [links.swap(self.low), links.swap(self.high)]

    def take_second(self, got):
        self.ends, self.over = got[:2], got[2:]

    def send_third(self):
        return [self.links.swap(e) for e in self.ends]

    def take_third(self, got):
        links = self.links
        own = [self.full, self.low, self.high] + self.ends
        over = [self.full_over] + self.over + got
        for bit in links.bits[2:]:
            own = own + [links.flip(p, bit) for p in own]
            over = over + [links.flip(p, bit) for p in over]
        self.pieces = [(p, p.shape[0], 0) for p in own + over]


class PlaneFirst:
    def __init__(self, links, part):
        self.links, self.part = links, part

    def send_first(self):
        return [self.links.flip(self.part, bit) for bit in self.links.bits[:2]]

    def take_first(self, got):
        self.low, self.high = got
        half = self.part.shape[0] // 2
        self.sent = [self.low[:half], self.high[half:]]

    def send_second(self):
        low, high = self.links.bits[0], self.links.bits[1]
        return [self.links.flip(self.sent[0], high), self.links.flip(self.sent[1], low)]

    def take_second(self, got):
        self.end = jnp.concatenate(got)

    def take_lines(self, own):
        for bit in self.links.bits[2:]:
            own = own + [self.links.flip(p, bit) for p in own]
        self.own = own

    def send_over(self, which):
        return [self.links.swap(self.own[number]) for number in which]

    def take_over(self, got):
        self.pieces = [(p, p.shape[0], 0) for p in self.own + got]


def piece_rows(links, own_rows):
    height = links.narrow * own_rows
    low, high = links.bits[0], links.bits[1]
    marks = [(0, 0), (low, 0), (high, 0), (low | high, 0), (low | high, height // 2)]
    for bit in links.bits[2:]:
        marks = marks + [(mask | bit, extra) for mask, extra in marks]
    return jnp.stack(
        [
            ((links.outer ^ mask) * 2 + (links.core ^ over)) * height + extra
            for over in range(2)
            for mask, extra in marks
        ]
    ).astype(i32)


def part_rows(links, own_rows):
    height = links.narrow * own_rows
    return jnp.stack(
        [
            ((links.outer ^ mask) * 2 + (links.core ^ over)) * height
            for over in range(2)
            for mask in range(links.wide // 2)
        ]
    ).astype(i32)


def total(*terms):
    out = terms[0].astype(f32)
    for term in terms[1:]:
        out = out + term.astype(f32)
    return out


class Scatter:
    def __init__(self, links, own, other):
        self.links, self.own, self.other = links, own, other

    def send_over(self):
        return [self.links.swap(part) for part in self.other]

    def take_over(self, got):
        links, own = self.links, self.own
        for bit in links.bits[:1:-1]:
            height = own[0].shape[0] // 2
            sums = [total(a, b).astype(bf16) for a, b in zip(own, got)]
            own = [s[:height] for s in sums]
            got = [links.flip(s[height:], bit) for s in sums]
        self.near, self.got = own, got

    def end(self):
        return end_sums(self.near, self.got)

    def send_first(self):
        low, high = self.links.bits[0], self.links.bits[1]
        return [self.links.flip(self.sums[0], low), self.links.flip(self.sums[1], high)]

    def take_first(self, got):
        self.sums = middle_sums(self.near, self.got, list(got))

    def send_second(self):
        low, high = self.links.bits[0], self.links.bits[1]
        return [self.links.flip(self.sums[0], low), self.links.flip(self.sums[1], high)]

    def take_second(self, got):
        links = self.links
        place = links.place.astype(i32).reshape(1)
        self.mine, self.sums = line_sums(place, links.narrow, self.near, self.got, list(got))

    def send_along(self, which=None):
        which = range(1, self.links.narrow) if which is None else which
        return [self.links.shift(self.sums[by - 1], by) for by in which]

    def take_along(self, got):
        self.result = total(self.mine, *got)


def on_device(
    wide, narrow, inputs, segment_ids, routes, attention_gain, qkv_weight, output_weight,
    mixture_gain, router_train, router_frozen, expert_in, expert_out, frozen_in, frozen_out,
    cotangent,
):
    links = Links(wide, narrow)
    length, width = inputs.shape
    own_rows = qkv_weight.shape[0]
    train_count = expert_in.shape[1]
    experts = train_count + frozen_in.shape[1]
    groups = expert_in.shape[2] // width
    docs = segment_ids[0]
    small = jnp.concatenate(
        [attention_gain[:, None], mixture_gain[:, None], router_train, router_frozen], axis=1
    )
    small = jnp.pad(small, ((0, 0), (0, LANES - small.shape[1])))
    dense = Gather(links, jnp.concatenate([qkv_weight, output_weight, small], axis=1))
    rows, order = piece_rows(links, own_rows), part_rows(links, own_rows)

    def packed(inner, outer):
        inner = inner.reshape(own_rows, width, groups).transpose(0, 2, 1).reshape(own_rows, -1)
        return jnp.concatenate([inner, outer.reshape(own_rows, -1)], axis=1)

    def part_of(e):
        if e < train_count:
            return packed(expert_in[:, e], expert_out[:, e])
        return packed(frozen_in[:, e - train_count], frozen_out[:, e - train_count])

    last = experts - 1
    weights = [Gather(links, part_of(e)) for e in range(last)] + [PlaneFirst(links, part_of(last))]
    always = segment_ids[0, 0] >= 0
    chosen = (routes[:, :, None] == jnp.arange(experts, dtype=i32)).astype(i32)
    per_block = jnp.sum(chosen.reshape(length // BLOCK, 2 * BLOCK, experts), axis=1)
    counts = jnp.concatenate([jnp.zeros((1, experts), i32), jnp.cumsum(per_block, axis=0)])
    counts = counts.reshape(-1)
    place, place_t = route_places(routes)

    def pick(expert, normed, gates):
        return dispatch(
            expert, experts, expert < train_count, order, counts, place_t, gates, normed, cotangent
        )

    def run(expert, picked):
        return expert_pass(
            expert, length // BLOCK * experts + expert, expert < train_count,
            order if expert == last else rows, order, counts, picked, weights[expert].pieces,
        )

    shifts = list(range(1, narrow))

    def line(part, *deps):
        part = after(part, *deps) if deps else part
        return lax.all_gather(part, "narrow", axis=0, tiled=True)

    w0, w1, w2, w3 = weights
    w0.part = after(w0.part, dense.part)
    got = dense.send_along()
    dense.take_along(after(got, [w.part for w in weights]))
    w0.full = line(w0.part, dense.full)
    dense.take_first(together(always, dense.send_first))
    w1.full = line(w1.part, dense.low)
    dense.take_second(together(always, dense.send_second))
    w2.full = line(w2.part, dense.ends)
    dense.take_third(dense.send_third())

    def step():
        qkv, full, gains = project(rows, inputs, dense.pieces)
        attended, logs = attend(docs, qkv)
        return w0.send_first(), w3.send_first(), (qkv, full, gains, attended, logs)

    got, ahead, (qkv, dense, gains, attended, logs) = together(always, step)
    w0.take_first(got)
    w3.take_first(ahead)
    w3.own = [line(shard, qkv) for shard in (w3.part, w3.low, w3.high)]
    def step():
        made = middle(inputs, attended, place, dense)
        return w0.send_second(), made, pick(0, *made[1:])

    got, (hidden, normed, gates), picked = together(always, step)
    w0.take_second(got)
    w0.take_third(w0.send_third())
    got, ahead, one = together(
        always, lambda: (w1.send_first(), w3.send_second(), run(0, picked))
    )
    w1.take_first(got)
    w3.take_second(ahead)
    got, picked = together(
        always,
        lambda: (w1.send_second(), [pick(e, normed, gates) for e in range(1, experts)]),
    )
    w1.take_second(got)
    w1.take_third(w1.send_third())
    end = line(w3.end, w1.ends)
    term0 = Scatter(links, [one[2], one[4]], [one[3], one[5]])
    w2.full = after(w2.full, one[0])
    got, more, two = together(
        always, lambda: (w2.send_first(), term0.send_over(), run(1, picked[0]))
    )
    w2.take_first(got)

    term0.take_over(more)
    got, ahead, term0.sums = together(
        always, lambda: (w2.send_second(), w3.send_over([0]), term0.end())
    )
    w2.take_second(got)
    w2.take_third(w2.send_third())
    w3.take_lines(w3.own + [end])
    term1 = Scatter(links, [two[2], two[4]], [two[3], two[5]])
    count = len(w3.own)
    got, more, three = together(
        always, lambda: (w3.send_over(range(1, count - 1)), term1.send_over(), run(2, picked[1]))
    )
    w3.own = w3.own[:-1] + [after(w3.own[-1], three[0])]
    w3.take_over(ahead + got + w3.send_over([count - 1]))
    term1.take_over(more)
    term1.sums = term1.end()
    got, more, four = together(
        always, lambda: (term0.send_first(), term1.send_first(), run(3, picked[2]))
    )
    term0.take_first(got)
    results, backs = [[m[i] for m in (one, two, three, four)] for i in range(2)]

    def step():
        made = combine(
            experts, order, counts, place, gates, hidden, normed, cotangent, attended, dense,
            results, backs,
        )
        term1.take_first(more)
        return term0.send_second(), term1.sums, made

    got, term1.sums, (block_output, grad_hidden, grad_heads, *made) = together(always, step)
    term0.take_second(got)
    out_term = Scatter(links, *[[m] for m in made])
    got, more, (dq, dk, dv) = together(
        always,
        lambda: (
            term1.send_second(), term0.send_along(), attend_back(docs, qkv, grad_heads, attended, logs)
        ),
    )
    term1.take_second(got)
    over, one, made = together(
        always,
        lambda: (
            out_term.send_over(), term1.send_along(shifts[:1]),
            weigh(order, inputs, gains, dq, dk, dv),
        ),
    )
    out_term.take_over(over)
    out_term.sums = out_term.end()
    qkv_term = Scatter(links, *[[m] for m in made])
    over, got, last, input_grad = together(
        always,
        lambda: (
            qkv_term.send_over(), out_term.send_first(), term1.send_along(shifts[2:]),
            finish(inputs, gains, dq, dk, dv, grad_hidden, dense),
        ),
    )
    qkv_term.take_over(over)
    qkv_term.sums = qkv_term.end()
    out_term.take_first(got)

    def unpacked(parts):
        full = total(*parts)
        inner = groups * width
        inner, outer = full[:, :inner], full[:, inner:]
        inner = inner.reshape(own_rows, groups, width).transpose(0, 2, 1).reshape(own_rows, -1)
        return inner, outer.reshape(own_rows * groups, width)

    got, two, middle_part, first = together(
        always,
        lambda: (
            qkv_term.send_first(), out_term.send_second(), term1.send_along(shifts[1:2]),
            unpacked([term0.mine] + more),
        ),
    )
    qkv_term.take_first(got)
    out_term.take_second(two)

    def step():
        second = unpacked([term1.mine] + one + middle_part + last)
        in_grad, down_grad = [jnp.stack(pair, axis=1) for pair in zip(first, second)]
        return qkv_term.send_second(), out_term.send_along(), in_grad, down_grad

    got, two, in_grad, down_grad = together(always, step)
    qkv_term.take_second(got)

    def step():
        out_term.take_along(two)
        out = out_term.result
        return qkv_term.send_along(), (
            out[:, :width], out[:, width + LANES - 1], out[:, width : width + train_count]
        )

    got, outs = together(always, step)
    qkv_term.take_along(got)
    qkv_grad = qkv_term.result
    gain_grad = jnp.sum(qkv_weight.astype(f32) * qkv_grad, axis=1) / attention_gain.astype(f32)
    return (
        block_output,
        input_grad,
        gain_grad,
        qkv_grad,
        *outs,
        in_grad,
        down_grad,
    )


def solution(mesh):
    wide, narrow = mesh.shape["wide"], mesh.shape["narrow"]
    mesh = Mesh(mesh.devices.reshape(wide // 2, 2, narrow), AXES)
    rows = P(AXES)
    return jax.shard_map(
        functools.partial(on_device, wide, narrow),
        mesh=mesh,
        in_specs=(rows,) * 14,
        out_specs=(rows,) * 9,
        check_vma=False,
    )
```
